32 devices in a mesh: wide: 8 (over z, x), narrow: 4 (over y, core).
Axes of the slice: x: 2, y: 2, z: 4, core: 2. Of those that a mesh axis runs over, the one named last changes fastest.
Arguments:
- cells_in: bfloat16 [32, 2048, 256], P(('wide', 'narrow')), may hold values from -6 to 6
- lengths: int32 [32], P(('wide', 'narrow')), may hold values from 300 to 2048, as said below
- cotangent: bfloat16 [32, 2048, 256], P(('wide', 'narrow')), may hold values from -6 to 6
- query_weight: bfloat16 [2, 256, 256], P(None, None, ('wide', 'narrow')), may hold values from -0.375 to 0.375
- query_bias: bfloat16 [2, 256], P(None, ('wide', 'narrow')), may hold values from -3 to 3
- key_weight: bfloat16 [2, 256, 256], P(None, None, ('wide', 'narrow')), may hold values from -0.375 to 0.375
- value_weight: bfloat16 [2, 256, 256], P(None, None, ('wide', 'narrow')), may hold values from -0.375 to 0.375
- value_bias: bfloat16 [2, 256], P(None, ('wide', 'narrow')), may hold values from -3 to 3
- out_weight: bfloat16 [2, 256, 256], P(None, None, ('wide', 'narrow')), may hold values from -4 to 4
- out_bias: bfloat16 [2, 256], P(None, ('wide', 'narrow')), may hold values from -3 to 3
- first_gain: bfloat16 [2, 256], P(None, ('wide', 'narrow')), may hold values from 0.5 to 1.5
- first_shift: bfloat16 [2, 256], P(None, ('wide', 'narrow')), may hold values from -2 to 2
- up_weight: bfloat16 [2, 256, 512], P(None, None, ('wide', 'narrow')), may hold values from -0.375 to 0.375
- up_bias: bfloat16 [2, 512], P(None, ('wide', 'narrow')), may hold values from -3 to 3
- down_weight: bfloat16 [2, 512, 256], P(None, None, ('wide', 'narrow')), may hold values from -0.25 to 0.25
- down_bias: bfloat16 [2, 256], P(None, ('wide', 'narrow')), may hold values from -3 to 3
- second_gain: bfloat16 [2, 256], P(None, ('wide', 'narrow')), may hold values from 0.5 to 1.5
- second_shift: bfloat16 [2, 256], P(None, ('wide', 'narrow')), may hold values from -2 to 2
Outputs:
- cells_out: bfloat16 [32, 2048, 256], P(('wide', 'narrow'))
- grad_input: float32 [32, 2048, 256], P(('wide', 'narrow'))
- query_weight_grad: float32 [2, 256, 256], P(None, None, ('wide', 'narrow'))
- query_bias_grad: float32 [2, 256], P(None, ('wide', 'narrow'))
- key_weight_grad: float32 [2, 256, 256], P(None, None, ('wide', 'narrow'))
- value_weight_grad: float32 [2, 256, 256], P(None, None, ('wide', 'narrow'))
- value_bias_grad: float32 [2, 256], P(None, ('wide', 'narrow'))
- out_weight_grad: float32 [2, 256, 256], P(None, None, ('wide', 'narrow'))
- out_bias_grad: float32 [2, 256], P(None, ('wide', 'narrow'))
- first_gain_grad: float32 [2, 256], P(None, ('wide', 'narrow'))
- first_shift_grad: float32 [2, 256], P(None, ('wide', 'narrow'))
- up_weight_grad: float32 [2, 256, 512], P(None, None, ('wide', 'narrow'))
- up_bias_grad: float32 [2, 512], P(None, ('wide', 'narrow'))
- down_weight_grad: float32 [2, 512, 256], P(None, None, ('wide', 'narrow'))
- down_bias_grad: float32 [2, 256], P(None, ('wide', 'narrow'))
- second_gain_grad: float32 [2, 256], P(None, ('wide', 'narrow'))
- second_shift_grad: float32 [2, 256], P(None, ('wide', 'narrow'))
The draws below stay inside these ranges and needn't reach their ends.
Inputs may be any that keep to these rules, and one draw needn't show every extreme that they name: `lengths`: exactly one cell of all has all 2048 genes; the others have at least 300.
All inputs are finite; a program needn't handle non-finite values.
Results may differ from the reference program's by a relative error of at most 0.02.
The reference program's roundings to bfloat16 on the way count: a program that leaves them out, or rounds other values in their place, can miss the bound.
Values may be sent and summed in bfloat16 or wider, within the bound.
A program may use at most 192 MiB of HBM per device.

```python
import math
import jax
import jax.numpy as jnp
from jax import lax

D = 256
HEAD = 64
FF = 512
SEQ = 2048
SHORT = 300
LAYERS = 2
CELLS = 32
TOKENS = 65536


def draw_lengths(key, part):
    key = jax.random.fold_in(key, 7)
    keys = jax.random.split(key, 4)
    span = SEQ - SHORT + 1
    first = jax.random.randint(keys[0], (CELLS,), 0, span)
    second = jax.random.randint(keys[1], (CELLS,), 0, span)
    third = jax.random.randint(keys[2], (CELLS,), 0, span)
    shortest = jnp.minimum(jnp.minimum(first, second), third)
    chosen = jax.random.randint(keys[3], (), 0, CELLS)
    result = jnp.where(jnp.arange(CELLS) == chosen, SEQ, SHORT + shortest)
    return result.astype(jnp.int32)


def raised(array, key, source, target, shards_of, factor):
    owner, partner = [(jnp.arange(array.shape[axis_at]) // (array.shape[axis_at] // shards_of)).reshape([-1 if axis == axis_at else 1 for axis in range(array.ndim)]) for axis_at in (source, target)]
    chosen = jax.random.permutation(key, shards_of)[partner]
    strong = (owner == chosen) | (owner == (partner + shards_of // 2) % shards_of)
    return jnp.where(strong, factor * array, array)


def block_scale(rng, dims, pieces, least, high):
    loudness = 1.0
    for axis_at, parts in pieces:
        steps = jax.random.uniform(jax.random.fold_in(jax.random.fold_in(rng, 6), axis_at), (parts,), jnp.float32, least / len(pieces), high / len(pieces))
        loudness = loudness * jnp.repeat(jnp.exp(steps), dims[axis_at] // parts).reshape((-1,) + (1,) * (len(dims) - 1 - axis_at))
    return loudness


def noise(stream_key, dims, scale, most, cuts=(), held_as=jnp.bfloat16):
    factor_of = block_scale(stream_key, dims, cuts, -0.22, 0.18) if cuts else 1.0
    values = jax.random.normal(stream_key, dims, jnp.float32) * scale * factor_of
    return jnp.minimum(jnp.maximum(values, -most), most).astype(held_as)


def noise_with(rng, shape, scale, bound, cuts, heavy, kind=jnp.bfloat16):
    values = scale * jax.random.normal(rng, shape, jnp.float32)
    if cuts:
        values = values * block_scale(rng, shape, cuts, -0.22, 0.18)
    return jnp.clip(raised(values, jax.random.fold_in(rng, 3), *heavy), -bound, bound).astype(kind)


def setup_inputs(seed: int = 0) -> dict:
    arg_keys = jax.random.split(jax.random.key(seed), 19)
    return {
        "cells_in": noise(arg_keys[0], (CELLS, SEQ, D), 1.0, 6.0, ((0, 32),)),
        "lengths": draw_lengths(jax.random.fold_in(arg_keys[18], 71), 0),
        "cotangent": noise_with(arg_keys[2], (CELLS, SEQ, D), 1.0, 6.0, ((0, 32),), (0, 2, 32, 2.75)),
        "query_weight": noise(arg_keys[3], (LAYERS, D, D), D ** -0.5, 0.375, ((2, 32),)),
        "query_bias": noise(arg_keys[4], (LAYERS, D), 0.5, 3.0, ((1, 32),)),
        "key_weight": noise(arg_keys[5], (LAYERS, D, D), D ** -0.5, 0.375, ((2, 32),)),
        "value_weight": noise(arg_keys[6], (LAYERS, D, D), D ** -0.5, 0.375, ((2, 32),)),
        "value_bias": noise(arg_keys[7], (LAYERS, D), 0.5, 3.0, ((1, 32),)),
        "out_weight": noise(arg_keys[8], (LAYERS, D, D), 2 ** -0.5, 4.0, ((2, 32),)),
        "out_bias": noise(arg_keys[9], (LAYERS, D), 0.5, 3.0, ((1, 32),)),
        "first_gain": jnp.clip(1.0 + 0.1 * jax.random.normal(arg_keys[10], (LAYERS, D), jnp.float32), 0.5, 1.5).astype(jnp.bfloat16),
        "first_shift": noise(arg_keys[11], (LAYERS, D), 0.3, 2.0, ((1, 32),)),
        "up_weight": noise(arg_keys[12], (LAYERS, D, FF), D ** -0.5, 0.375, ((2, 32),)),
        "up_bias": noise(arg_keys[13], (LAYERS, FF), 0.5, 3.0, ((1, 32),)),
        "down_weight": noise(arg_keys[14], (LAYERS, FF, D), FF ** -0.5, 0.25, ((2, 32),)),
        "down_bias": noise(arg_keys[15], (LAYERS, D), 0.5, 3.0, ((1, 32),)),
        "second_gain": jnp.clip(1.0 + 0.1 * jax.random.normal(arg_keys[16], (LAYERS, D), jnp.float32), 0.5, 1.5).astype(jnp.bfloat16),
        "second_shift": noise(arg_keys[17], (LAYERS, D), 0.3, 2.0, ((1, 32),)),
    }


neg_fill = -1000000000.0
norm_eps = 1e-06

@jax.custom_vjp
def low(v):
    return lax.optimization_barrier(v.astype(jnp.bfloat16)).astype(jnp.float32)

@jax.custom_vjp
def low_back(v):
    return v

def low_keep(v):
    return (low(v), None)

def low_pass(kept, grad):
    return (grad,)

def back_keep(v):
    return (v, None)

def back_low(kept, grad):
    return (low(grad),)
low.defvjp(low_keep, low_pass)
low_back.defvjp(back_keep, back_low)

def dense(left, weight):
    return jnp.dot(left, weight, precision=lax.Precision.HIGHEST)

def layer_norm(resid, gain, shift):
    center = lax.optimization_barrier(jnp.mean(resid, axis=-1, keepdims=True))
    offset = resid - center
    spread = lax.optimization_barrier(jnp.mean(offset * offset, axis=-1, keepdims=True))
    return offset * lax.rsqrt(spread + norm_eps) * gain + shift

def attention(query, keys, values, valid):
    length, heads, size = query.shape
    block = min(length, 512)
    scale = 1.0 / math.sqrt(size)
    blocks = query.reshape(length // block, block, heads, size)

    def one_block(rows):
        scores = jnp.einsum('bhe,khe->hbk', rows, keys, precision=lax.Precision.HIGHEST) * scale
        scores = low_back(jnp.where(valid[None, None, :], scores, neg_fill))
        probs = low(jax.nn.softmax(scores, axis=-1))
        return jnp.einsum('hbk,khe->bhe', probs, values, precision=lax.Precision.HIGHEST)
    context = lax.map(jax.checkpoint(one_block), blocks)
    return context.reshape(length, heads * size)

def encoder_layer(weights, inputs, valid):
    query_weight, query_bias, key_weight, value_weight, value_bias, out_weight, out_bias, first_gain, first_shift, up_weight, up_bias, down_weight, down_bias, second_gain, second_shift = weights
    length, width = inputs.shape
    heads = width // HEAD
    low_in = low(inputs)
    query = low_back(low(dense(low_in, query_weight) + query_bias))
    keys = low_back(low(dense(low_in, key_weight)))
    values = low_back(low(dense(low_in, value_weight) + value_bias))
    shape = (length, heads, HEAD)
    context = low_back(low(attention(query.reshape(shape), keys.reshape(shape), values.reshape(shape), valid)))
    attn = low_back(dense(context, out_weight) + out_bias)
    middle = layer_norm(inputs + attn, first_gain, first_shift)
    hidden = low_back(dense(low(middle), up_weight) + up_bias)
    active = low(jax.nn.gelu(hidden))
    branch = low_back(dense(active, down_weight) + down_bias)
    return layer_norm(middle + branch, second_gain, second_shift)

def reference(cells_in, lengths, cotangent, query_weight, query_bias, key_weight, value_weight, value_bias, out_weight, out_bias, first_gain, first_shift, up_weight, up_bias, down_weight, down_bias, second_gain, second_shift):
    params = (query_weight, query_bias, key_weight, value_weight, value_bias, out_weight, out_bias, first_gain, first_shift, up_weight, up_bias, down_weight, down_bias, second_gain, second_shift)
    params = tuple((part.astype(jnp.float32) for part in params))
    positions = jnp.arange(SEQ, dtype=jnp.int32)

    def forward(weights, inputs, valid):
        current = inputs
        for layer in range(LAYERS):
            current = encoder_layer(tuple((part[layer] for part in weights)), current, valid)
        return current

    def per_cell(totals, item):
        inputs, length, grad_out = item
        valid = positions < length
        result, back = jax.vjp(lambda weights, rows: forward(weights, rows, valid), params, inputs.astype(jnp.float32))
        weight_grads, input_grad = back(grad_out.astype(jnp.float32) * valid[:, None].astype(jnp.float32))
        totals = jax.tree.map(jnp.add, totals, weight_grads)
        return (totals, (result.astype(jnp.bfloat16), input_grad))
    zeros = tuple((jnp.zeros_like(part) for part in params))
    totals, (outputs, input_grads) = lax.scan(per_cell, zeros, (cells_in, lengths, cotangent))
    factor = 1.0 / jnp.sqrt(jnp.float32(TOKENS))
    return (outputs, input_grads, totals[0] * factor, totals[1] * factor, totals[2] * factor, totals[3] * factor, totals[4] * factor, totals[5] * factor, totals[6] * factor, totals[7] * factor, totals[8] * factor, totals[9] * factor, totals[10] * factor, totals[11] * factor, totals[12] * factor, totals[13] * factor, totals[14] * factor)
```

```python
import functools
import math

import jax
import jax.numpy as jnp
from jax import lax
from jax.experimental import pallas as pl
from jax.experimental.pallas import tpu as pltpu
from jax.sharding import PartitionSpec as P

HEAD = 64
NEG = -1000000000.0
EPS = 1e-06
AXES = ("wide", "narrow")
MESH = pl.DeviceIdType.MESH
BF = jnp.bfloat16
F32 = jnp.float32
EXT = 16
GUARD = 3600.0
KEY_SIZES = (512, 768, 1024, 1280, 1536, 2048)
ROWS = 64
VMEM_SPEC = pl.BlockSpec(memory_space=pltpu.VMEM)
SMEM_SPEC = pl.BlockSpec(memory_space=pltpu.SMEM)
ANY_SPEC = pl.BlockSpec(memory_space=pl.ANY)
QB, VB, OB, G1, S1, DB, G2, S2, UB = range(9)


def dot(a, b, ca, cb):
    return lax.dot_general(a, b, (((ca,), (cb,)), ((), ())), preferred_element_type=F32)


def params(collective_id=None, limit=56):
    if collective_id is None:
        return pltpu.CompilerParams(vmem_limit_bytes=limit << 20)
    return pltpu.CompilerParams(
        vmem_limit_bytes=limit << 20, collective_id=collective_id, has_side_effects=True
    )


def shape_of(shape, dtype):
    return jax.ShapeDtypeStruct(shape, dtype)


def pair_of():
    narrow = lax.axis_index("narrow")
    core = lax.rem(narrow, 2)
    return core, (lax.axis_index("wide"), narrow + 1 - 2 * core)


def greet(peer):
    barrier = pltpu.get_barrier_semaphore()
    pl.semaphore_signal(barrier, inc=1, device_id=peer, device_id_type=MESH)
    pl.semaphore_wait(barrier, 1)


def to_peer(src, dst, send, recv, peer):
    return pltpu.make_async_remote_copy(
        src_ref=src, dst_ref=dst, send_sem=send, recv_sem=recv, device_id=peer, device_id_type=MESH
    )


def half_rows(ref, lead, base, half):
    return ref[lead, pl.ds(pl.multiple_of(base + half * 128, 128), 128)]


def tile_lanes(column, count):
    return jnp.concatenate([column] * (count // 128), axis=1)


def spread(vec_ref, cols_ref):
    vec = vec_ref[...]
    width = vec.shape[0]
    for i in range(8):
        cols_ref[pl.ds(i * width, width)] = jnp.broadcast_to(vec[:, i : i + 1], (width, 128))
    low = jnp.broadcast_to(vec[:, 8:9], (width, 128)).reshape(width // 8, 8, 128)
    high = jnp.broadcast_to(vec[:, 9:10], (width, 128)).reshape(width // 8, 8, 128)
    cols_ref[pl.ds(8 * width, 2 * width)] = jnp.concatenate([low, high], axis=1).reshape(
        2 * width, 128
    )


def column(cols_ref, i, count):
    rows = 512 if i == UB else 256
    return tile_lanes(cols_ref[pl.ds(i * 256, rows)], count)


def fold_lanes(x):
    total = x[:, :128]
    for start in range(128, x.shape[1], 128):
        total = total + x[:, start : start + 128]
    return total


def norm(resid):
    offset = resid - jnp.mean(resid, axis=0, keepdims=True)
    scale = lax.rsqrt(jnp.mean(offset * offset, axis=0, keepdims=True) + EPS)
    return offset * scale, scale


def norm_back(grad, gain, unit, scale):
    q = grad * gain
    return (
        q - jnp.mean(q, axis=0, keepdims=True) - unit * jnp.mean(q * unit, axis=0, keepdims=True)
    ) * scale


GELU_C = 0.7978845608028654
GELU_A = 0.044715


def gelu_tanh(u):
    return jnp.tanh(GELU_C * (u + GELU_A * (u * u * u)))


def project(xb, contract, w_ref, cols_ref, half):
    parts = []
    for i in range(3):
        y = dot(half_rows(w_ref, 0, i * 256, half), xb, 1, contract)
        if i != 1:
            bias = cols_ref[
                pl.ds(pl.multiple_of((QB if i == 0 else VB) * 256 + half * 128, 128), 128)
            ]
            y = y + tile_lanes(bias, y.shape[1])
        y = y.astype(BF)
        parts.append(y * jnp.asarray(0.125, BF) if i == 0 else y)
    return jnp.concatenate(parts, axis=0)


def join(core, own, peer):
    return jnp.concatenate(
        [jnp.where(core == 0, own, peer), jnp.where(core == 0, peer, own)], axis=0
    )


def forward_block(context, x, wo, wup, wdn, cols_ref):
    count = x.shape[1]
    unit1, scale1 = norm(x + dot(wo, context, 1, 0) + column(cols_ref, OB, count))
    middle = unit1 * column(cols_ref, G1, count) + column(cols_ref, S1, count)
    hidden = dot(wup, middle.astype(BF), 1, 0) + column(cols_ref, UB, count)
    active = (0.5 * hidden * (1.0 + gelu_tanh(hidden))).astype(BF)
    unit2, scale2 = norm(middle + dot(wdn, active, 1, 0) + column(cols_ref, DB, count))
    x_next = unit2 * column(cols_ref, G2, count) + column(cols_ref, S2, count)
    return unit1, scale1, hidden, unit2, scale2, x_next


def backward_block(grad, context, saved, weights, cols_ref, sums, dwo, dwup, dwdn):
    unit1, scale1, hidden, unit2, scale2 = saved
    wo, wup, wdn = weights
    count = grad.shape[1]

    def add(i, x):
        rows = x.shape[0]
        sums[pl.ds(i * 256, rows)] += fold_lanes(x)

    add(S2, grad)
    add(G2, grad * unit2)
    d_second = norm_back(grad, column(cols_ref, G2, count), unit2, scale2)
    branch = d_second.astype(BF)
    add(DB, branch.astype(F32))
    t = gelu_tanh(hidden)
    active = (0.5 * hidden * (1.0 + t)).astype(BF)
    slope = 0.5 * (1.0 + t) + (0.5 * GELU_C) * hidden * (1.0 - t * t) * (
        1.0 + (3.0 * GELU_A) * (hidden * hidden)
    )
    dwdn[...] += dot(branch, active, 1, 1)
    d_hidden = (dot(wdn, branch, 0, 0) * slope).astype(BF)
    add(UB, d_hidden.astype(F32))
    middle = unit1 * column(cols_ref, G1, count) + column(cols_ref, S1, count)
    dwup[...] += dot(d_hidden, middle.astype(BF), 1, 1)
    d_middle = d_second + dot(wup, d_hidden, 0, 0)
    add(S1, d_middle)
    add(G1, d_middle * unit1)
    d_first = norm_back(d_middle, column(cols_ref, G1, count), unit1, scale1)
    attn = d_first.astype(BF)
    add(OB, attn.astype(F32))
    dwo[...] += dot(attn, context, 1, 1)
    return d_first, dot(wo, attn, 0, 0).astype(BF)


def place_vectors(sums):
    lane = lax.broadcasted_iota(jnp.int32, (256, 128), 1)
    out = jnp.zeros((256, 128), F32)
    for i in range(8):
        total = jnp.sum(sums[pl.ds(i * 256, 256)], axis=1, keepdims=True)
        out = jnp.where(lane == i, total, out)
    up = jnp.sum(sums[pl.ds(2048, 512)], axis=1, keepdims=True)
    up = jnp.broadcast_to(up, (512, 128)).reshape(32, 16, 128)
    out = jnp.where(lane == 8, up[:, :8].reshape(256, 128), out)
    return jnp.where(lane == 9, up[:, 8:].reshape(256, 128), out)


def pack_own(weights, vectors, pack, flat):
    qw, kw, vw, ow, uw, dw = weights
    for layer in range(2):
        rows = [jnp.transpose(w[layer].astype(F32)) for w in (qw, kw, vw, ow, uw)]
        down = jnp.transpose(dw[layer].astype(F32))
        rows += [down[:, :256], down[:, 256:]]
        pack[pl.ds(layer * ROWS, ROWS)] = jnp.concatenate(rows, axis=0).astype(BF)
    flat[...] = jnp.zeros_like(flat)
    for i, v in enumerate(vectors):
        flat[pl.ds(2 * i, 2), 0:8] = v[:, 0:8].astype(F32)
        if v.shape[1] == 16:
            flat[pl.ds(2 * i + 2, 2), 0:8] = v[:, 8:16].astype(F32)
    columns = jnp.transpose(flat[...])[0:8]
    block = jnp.concatenate([columns, jnp.zeros_like(columns)], axis=1)
    pack[pl.ds(2 * ROWS, 16)] = jnp.concatenate([block, jnp.zeros_like(block)], axis=0).astype(BF)


def gather_kernel(devices, narrow, *refs):
    weights, vectors = refs[:6], refs[6:15]
    wqkv, wo, wup, wdn, vec = refs[15:20]
    pack, flat, landed, send, recv = refs[20:]
    me = lax.axis_index("wide") * narrow + lax.axis_index("narrow")

    def place(i):
        return (i // narrow, lax.rem(i, narrow))

    barrier = pltpu.get_barrier_semaphore()

    @pl.loop(1, devices)
    def _(step):
        pl.semaphore_signal(
            barrier,
            inc=1,
            device_id=place(lax.rem(me + step, devices)),
            device_id_type=MESH,
        )

    pack_own(weights, vectors, pack, flat)
    pl.semaphore_wait(barrier, devices - 1)

    def copy(step):
        return pltpu.make_async_remote_copy(
            src_ref=pack,
            dst_ref=landed.at[me],
            send_sem=send.at[step],
            recv_sem=recv.at[step],
            device_id=place(lax.rem(me + step, devices)),
            device_id_type=MESH,
        )

    @pl.loop(1, devices)
    def _(step):
        copy(step).start()

    landed[me] = pack[...]

    @pl.loop(1, devices)
    def _(step):
        copy(step).wait()

    unpack(landed, wqkv, wo, wup, wdn, vec)


def unpack(landed, wqkv, wo, wup, wdn, vec):
    for layer in range(2):
        base = layer * ROWS
        pair = landed[:, base : base + 16, :].astype(F32)
        wqkv[layer, 0:256] = pair[:, :8].reshape(256, 256).astype(BF)
        wqkv[layer, 256:512] = pair[:, 8:].reshape(256, 256).astype(BF)
        pair = landed[:, base + 16 : base + 32, :].astype(F32)
        wqkv[layer, 512:768] = pair[:, :8].reshape(256, 256).astype(BF)
        wo[layer] = pair[:, 8:].reshape(256, 256).astype(BF)
        wup[layer] = landed[:, base + 32 : base + 48, :].reshape(512, 256)
        pair = landed[:, base + 48 : base + 64, :].astype(F32)
        wdn[layer, :, 0:256] = pair[:, :8].reshape(256, 256).astype(BF)
        wdn[layer, :, 256:512] = pair[:, 8:].reshape(256, 256).astype(BF)
    both = landed[:, 2 * ROWS : 2 * ROWS + 16, :].astype(F32)[:, :8, :128].reshape(256, 128)
    lane = lax.broadcasted_iota(jnp.int32, (256, 128), 1)
    for layer in range(2):
        out = jnp.zeros((256, 128), F32)
        for i in range(10):
            out = jnp.where(lane == i, both[:, 2 * i + layer : 2 * i + layer + 1], out)
        vec[layer] = out


def gather_weights(devices, narrow, weights, vectors):
    shapes = (
        shape_of((2, 768, 256), BF),
        shape_of((2, 256, 256), BF),
        shape_of((2, 512, 256), BF),
        shape_of((2, 256, 512), BF),
        shape_of((2, 256, 128), F32),
    )
    rows = 2 * ROWS + 16
    return pl.pallas_call(
        functools.partial(gather_kernel, devices, narrow),
        name="gather_weights",
        out_shape=shapes,
        in_specs=[VMEM_SPEC] * 15,
        out_specs=[VMEM_SPEC] * 5,
        scratch_shapes=[
            pltpu.VMEM((rows, 256), BF),
            pltpu.VMEM((128, 128), F32),
            pltpu.VMEM((devices, rows, 256), BF),
            pltpu.SemaphoreType.DMA((devices,)),
            pltpu.SemaphoreType.DMA((devices,)),
        ],
        compiler_params=params(1),
    )(*weights, *vectors)


def start_kernel(len_ref, x_ref, w_ref, vec_ref, lens, qkv, cols, out, own_len, send, recv):
    core, peer = pair_of()
    spread(vec_ref.at[0], cols)
    own_len[...] = jnp.full(own_len.shape, len_ref[0], jnp.int32)
    greet(peer)
    len_copy = to_peer(own_len, lens.at[1], send.at[0], recv.at[0], peer)
    len_copy.start()
    lens[0] = own_len[...]
    block = 512
    count = x_ref.shape[1] // block

    def copy(i):
        ds = pl.ds(pl.multiple_of(i * block, block), block)
        return to_peer(out.at[:, ds], qkv.at[1, :, ds], send.at[1 + i], recv.at[1 + i], peer)

    @pl.loop(0, count)
    def _(i):
        ds = pl.ds(pl.multiple_of(i * block, block), block)
        out[:, ds] = project(x_ref[0, ds], 1, w_ref, cols, 1 - core)
        copy(i).start()

    @pl.loop(0, count)
    def _(i):
        ds = pl.ds(pl.multiple_of(i * block, block), block)
        qkv[0, :, ds] = project(x_ref[0, ds], 1, w_ref, cols, core)

    len_copy.wait()

    @pl.loop(0, count)
    def _(i):
        copy(i).wait()


def start(lengths, cells, wqkv, vec):
    length = cells.shape[1]
    count = length // 512
    return pl.pallas_call(
        start_kernel,
        name="project_first",
        out_shape=(shape_of((2, 8, 128), jnp.int32), shape_of((2, 384, length), BF)),
        in_specs=[SMEM_SPEC] + [VMEM_SPEC] * 3,
        out_specs=[VMEM_SPEC] * 2,
        scratch_shapes=[
            pltpu.VMEM((2560, 128), F32),
            pltpu.VMEM((384, length), BF),
            pltpu.VMEM((8, 128), jnp.int32),
            pltpu.SemaphoreType.DMA((count + 1,)),
            pltpu.SemaphoreType.DMA((count + 1,)),
        ],
        compiler_params=params(2),
    )(lengths, cells, wqkv, vec)


def key_sizes(length):
    return [size for size in KEY_SIZES if size < length] + [length]


def extended(x, extra):
    return jnp.concatenate([x, extra], axis=0)


def one_head(x, head):
    row = lax.broadcasted_iota(jnp.int32, x.shape, 0)
    return jnp.where((row // HEAD) == head, x, jnp.zeros_like(x))


def attend_kernel(lens, qkv, ctx, ctx32, logs, kx, scores, total, acc):
    length = qkv.shape[2]
    wide = 512
    count = length // wide
    row = lax.broadcasted_iota(jnp.int32, (EXT, wide), 0)
    ones = jnp.where(row == 0, 1.0, 0.0).astype(BF)

    def query_of(cell, i, head):
        q = qkv[cell, 0:128, pl.ds(pl.multiple_of(i * wide, wide), wide)]
        return extended(one_head(q, head), ones)

    def finish(cell, i, head, high, sums, out):
        ds = pl.ds(pl.multiple_of(i * wide, wide), wide)
        sums = jnp.sum(sums, axis=0, keepdims=True)
        out = out * (1.0 / sums)
        rows = slice(HEAD * head, HEAD * head + HEAD)
        ctx[cell, rows, ds] = out.astype(BF)
        ctx32[cell, rows, ds] = out
        logs[cell, head : head + 1, ds] = jnp.log(sums) + high

    def largest(x):
        x = x.astype(F32)
        square = x * x
        return [
            jnp.max(jnp.sum(square[HEAD * h : HEAD * h + HEAD], axis=0, keepdims=True))
            for h in range(2)
        ]

    @pl.loop(0, 2)
    def _(cell):
        valid = lens[cell, 0, 0]
        q_most = largest(qkv[cell, 0:128])
        k_most = largest(qkv[cell, 128:256])
        plain = jnp.maximum(q_most[0] * k_most[0], q_most[1] * k_most[1]) <= GUARD

        @pl.loop(0, pl.cdiv(valid, 256))
        def _(i):
            ds = pl.ds(pl.multiple_of(i * 256, 256), 256)
            where = lax.broadcasted_iota(jnp.int32, (EXT, 256), 1) + i * 256
            first = lax.broadcasted_iota(jnp.int32, (EXT, 256), 0) == 0
            extra = jnp.where(first & (where >= valid), NEG, 0.0).astype(BF)
            kx[ds] = jnp.transpose(extended(qkv[cell, 128:256, ds], extra))

        sizes = key_sizes(length)
        for low, size in zip([0] + sizes[:-1], sizes):
            @pl.when(plain & (valid > low) & (valid <= size))
            def _(size=size):
                @pl.loop(pl.cdiv(valid, 256), size // 256)
                def _(i):
                    lane = lax.broadcasted_iota(jnp.int32, (256, 128 + EXT), 1)
                    kx[pl.ds(pl.multiple_of(i * 256, 256), 256)] = jnp.where(
                        lane == 128, NEG, 0.0
                    ).astype(BF)

                @pl.loop(0, count)
                def _(i):
                    for head in range(2):
                        s = dot(kx[0:size], query_of(cell, i, head), 1, 0)
                        e = jnp.exp(s)
                        sums = jnp.sum(e.reshape(size // 8, 8, wide), axis=0)
                        v = qkv[cell, 256 + HEAD * head : 320 + HEAD * head, 0:size]
                        finish(cell, i, head, 0.0, sums, dot(v, e.astype(BF), 1, 0))

        @pl.when(jnp.logical_not(plain))
        def _():
            chunks = pl.cdiv(valid, 256)

            @pl.loop(0, count)
            def _(i):
                for head in range(2):
                    query = query_of(cell, i, head)

                    def score(j, high):
                        s = dot(kx[pl.ds(pl.multiple_of(j * 256, 256), 256)], query, 1, 0)
                        scores[j] = s
                        return jnp.maximum(high, jnp.max(s.reshape(32, 8, wide), axis=0))

                    high = lax.fori_loop(0, chunks, score, jnp.full((8, wide), NEG * 2, F32))
                    high = jnp.max(high, axis=0, keepdims=True)
                    acc[...] = jnp.zeros_like(acc)
                    total[...] = jnp.zeros_like(total)

                    @pl.loop(0, chunks)
                    def _(j):
                        e = jnp.exp(scores[j] - high)
                        total[...] += jnp.sum(e.reshape(32, 8, wide), axis=0)
                        v = qkv[
                            cell,
                            256 + HEAD * head : 320 + HEAD * head,
                            pl.ds(pl.multiple_of(j * 256, 256), 256),
                        ]
                        acc[...] += dot(v, e.astype(BF), 1, 0)

                    finish(cell, i, head, high, total[...], acc[...])


def attend(lens, qkv):
    length = qkv.shape[2]
    return pl.pallas_call(
        attend_kernel,
        name="attend",
        out_shape=(
            shape_of((2, 128, length), BF),
            shape_of((2, 128, length), F32),
            shape_of((2, 2, length), F32),
        ),
        in_specs=[SMEM_SPEC, VMEM_SPEC],
        out_specs=[VMEM_SPEC] * 3,
        scratch_shapes=[
            pltpu.VMEM((length, 128 + EXT), BF),
            pltpu.VMEM((length // 256, 256, 512), F32),
            pltpu.VMEM((8, 512), F32),
            pltpu.VMEM((HEAD, 512), F32),
        ],
        compiler_params=params(),
    )(lens, qkv)


def in_three(x):
    high = x.astype(BF)
    rest = x - high.astype(F32)
    middle = rest.astype(BF)
    return high, middle, (rest - middle.astype(F32)).astype(BF)


def attend_back_kernel(lens, qkv, grad, ctx32, logs, out, right_s, right_d, keys, sum_k, sum_v):
    length = qkv.shape[2]
    wide = 256
    row = lax.broadcasted_iota(jnp.int32, (EXT, wide), 0)

    def left(x, head, value, last):
        a, b, c = in_three(value)
        zero = jnp.zeros((EXT, wide), BF)
        extra = jnp.where(row == 0, a, jnp.where(row == 1, b, jnp.where(row == 2, c, zero)))
        if last:
            extra = jnp.where(row == 3, jnp.ones_like(zero), extra)
        return jnp.transpose(extended(one_head(x, head), extra))

    @pl.loop(0, 2)
    def _(cell):
        valid = lens[cell, 0, 0]
        out[cell] = jnp.zeros_like(out[cell])
        sizes = key_sizes(length)
        for low, size in zip([0] + sizes[:-1], sizes):

            @pl.when((valid > low) & (valid <= size))
            def _(size=size):
                where = lax.broadcasted_iota(jnp.int32, (EXT, size), 1)
                rows = lax.broadcasted_iota(jnp.int32, (EXT, size), 0)
                extra = jnp.where(
                    rows < 3, 1.0, jnp.where((rows == 3) & (where >= valid), NEG, 0.0)
                ).astype(BF)
                right_s[0:128, 0:size] = qkv[cell, 128:256, 0:size]
                right_s[128:, 0:size] = extra
                right_d[0:128, 0:size] = qkv[cell, 256:384, 0:size]
                right_d[128:, 0:size] = extra
                keys[0:size] = jnp.transpose(qkv[cell, 128:256, 0:size])
                sum_k[:, 0:size] = jnp.zeros((128, size), F32)
                sum_v[:, 0:size] = jnp.zeros((128, size), F32)

                @pl.loop(0, pl.cdiv(valid, wide))
                def _(i):
                    ds = pl.ds(pl.multiple_of(i * wide, wide), wide)
                    q = qkv[cell, 0:128, ds]
                    d = grad[cell, :, ds]
                    inner = d.astype(F32) * ctx32[cell, :, ds]
                    for head in range(2):
                        at = slice(HEAD * head, HEAD * head + HEAD)
                        delta = jnp.sum(inner[at], axis=0, keepdims=True)
                        s = dot(
                            left(q, head, -logs[cell, head : head + 1, ds], True),
                            right_s[:, 0:size],
                            1,
                            0,
                        )
                        p = jnp.exp(s)
                        dp = dot(left(d, head, -delta, False), right_d[:, 0:size], 1, 0)
                        ds_low = (p * dp).astype(BF)
                        sum_v[at, 0:size] += dot(d[at], p.astype(BF), 1, 0)
                        sum_k[at, 0:size] += dot(q[at], ds_low, 1, 0)
                        dq = dot(qkv[cell, 128 + HEAD * head : 192 + HEAD * head, 0:size], ds_low, 1, 1)
                        out[cell, at, ds] = (dq * 0.125).astype(BF)

                out[cell, 128:256, 0:size] = sum_k[:, 0:size].astype(BF)
                out[cell, 256:384, 0:size] = sum_v[:, 0:size].astype(BF)


def attend_back(lens, qkv, grad, ctx32, logs):
    length = qkv.shape[2]
    return pl.pallas_call(
        attend_back_kernel,
        name="attend_back",
        out_shape=shape_of((2, 384, length), BF),
        in_specs=[SMEM_SPEC] + [VMEM_SPEC] * 4,
        out_specs=VMEM_SPEC,
        scratch_shapes=[
            pltpu.VMEM((128 + EXT, length), BF),
            pltpu.VMEM((128 + EXT, length), BF),
            pltpu.VMEM((length, 128), BF),
            pltpu.VMEM((128, length), F32),
            pltpu.VMEM((128, length), F32),
        ],
        compiler_params=params(),
    )(lens, qkv, grad, ctx32, logs)


def between_kernel(
    ctx_any, ctx, x_ref, w_next, wo, wup, wdn, vec, vec_next,
    x_out, ctx_out, unit1, hidden, unit2, scales, qkv_own, qkv_peer,
    landed, cols, cols_next, out, send, recv,
):
    i, count = pl.program_id(0), pl.num_programs(0)
    block = x_out.shape[1]
    core, peer = pair_of()
    ctx_copy = to_peer(ctx_any.at[1], landed, send.at[0], recv.at[0], peer)

    def copy(step):
        ds = pl.ds(pl.multiple_of(step * block, block), block)
        return to_peer(out.at[:, ds], qkv_peer.at[:, ds], send.at[1 + step], recv.at[1 + step], peer)

    @pl.when(i == 0)
    def _():
        greet(peer)
        ctx_copy.start()
        spread(vec.at[0], cols)
        spread(vec_next.at[0], cols_next)
        ctx_copy.wait()

    ds = pl.ds(pl.multiple_of(i * block, block), block)
    context = join(core, ctx[0], landed[:, ds])
    ctx_out[...] = context
    x = jnp.transpose(x_ref[0].astype(F32))
    unit1[...], scale1, hidden[...], unit2[...], scale2, x_next = forward_block(
        context, x, wo[0], wup[0], wdn[0], cols
    )
    scales[0:1] = scale1
    scales[1:2] = scale2
    x_out[...] = x_next
    low = x_next.astype(BF)
    out[:, ds] = project(low, 0, w_next, cols_next, 1 - core)
    copy(i).start()
    qkv_own[...] = project(low, 0, w_next, cols_next, core)

    @pl.when(i == count - 1)
    def _():
        @pl.loop(0, count)
        def _(step):
            copy(step).wait()


def between(ctx, cells, wqkv, wo, wup, wdn, vec):
    length, block = ctx.shape[2], 512
    count = length // block

    def layer(full, at):
        return pl.BlockSpec((1,) + full.shape[1:], lambda i: (at, 0, 0))

    def tokens(rows):
        return pl.BlockSpec((rows, block), lambda i: (0, i))

    return pl.pallas_call(
        between_kernel,
        name="between_layers",
        grid=(count,),
        out_shape=(
            shape_of((256, length), F32),
            shape_of((256, length), BF),
            shape_of((256, length), F32),
            shape_of((512, length), F32),
            shape_of((256, length), F32),
            shape_of((8, length), F32),
            shape_of((384, length), BF),
            shape_of((384, length), BF),
        ),
        in_specs=[
            ANY_SPEC,
            pl.BlockSpec((1, 128, block), lambda i: (0, 0, i)),
            pl.BlockSpec((1, block, 256), lambda i: (0, i, 0)),
            layer(wqkv, 1),
            layer(wo, 0),
            layer(wup, 0),
            layer(wdn, 0),
            layer(vec, 0),
            layer(vec, 1),
        ],
        out_specs=[
            tokens(256), tokens(256), tokens(256), tokens(512), tokens(256), tokens(8), tokens(384), ANY_SPEC,
        ],
        scratch_shapes=[
            pltpu.VMEM((128, length), BF),
            pltpu.VMEM((2560, 128), F32),
            pltpu.VMEM((2560, 128), F32),
            pltpu.VMEM((384, length), BF),
            pltpu.SemaphoreType.DMA((count + 1,)),
            pltpu.SemaphoreType.DMA((count + 1,)),
        ],
        compiler_params=params(3),
    )(ctx, ctx, cells, wqkv, wo, wup, wdn, vec, vec)


def turn_kernel(
    len_ref, ctx_any, ctx, x_ref, cot, wo, wup, wdn, vec,
    cells_out, d_first, dctx_own, dctx_peer, dwo, dwup, dwdn, dvec,
    landed, cols, sums, out, send, recv,
):
    i, count = pl.program_id(0), pl.num_programs(0)
    block = x_ref.shape[1]
    core, peer = pair_of()
    ctx_copy = to_peer(ctx_any.at[1], landed, send.at[0], recv.at[0], peer)

    def copy(step):
        ds = pl.ds(pl.multiple_of(step * block, block), block)
        return to_peer(out.at[:, ds], dctx_peer.at[:, ds], send.at[1 + step], recv.at[1 + step], peer)

    @pl.when(i == 0)
    def _():
        greet(peer)
        ctx_copy.start()
        spread(vec.at[0], cols)
        for ref in (sums, dwo, dwup, dwdn):
            ref[...] = jnp.zeros_like(ref)
        ctx_copy.wait()

    ds = pl.ds(pl.multiple_of(i * block, block), block)
    context = join(core, ctx[0], landed[:, ds])
    weights = (wo[0], wup[0], wdn[0])
    *saved, x_next = forward_block(context, x_ref[...], *weights, cols)
    cells_out[0] = jnp.transpose(x_next).astype(BF)
    where = lax.broadcasted_iota(jnp.int32, (256, block), 1) + i * block
    grad = jnp.where(where < len_ref[0], jnp.transpose(cot[0].astype(F32)), 0.0)
    d_first[...], d_context = backward_block(
        grad, context, saved, weights, cols, sums, dwo, dwup, dwdn
    )
    low, high = d_context[:128], d_context[128:]
    dctx_own[...] = jnp.where(core == 0, low, high)
    out[:, ds] = jnp.where(core == 0, high, low)
    copy(i).start()

    @pl.when(i == count - 1)
    def _():
        dvec[...] = place_vectors(sums)

        @pl.loop(0, count)
        def _(step):
            copy(step).wait()


GRAD_SHAPES = ((256, 256), (512, 256), (256, 512), (256, 128))


def whole(shape):
    return pl.BlockSpec(shape, lambda i: (0,) * len(shape))


def turn(lengths, ctx, x, cot, wo, wup, wdn, vec):
    length, block = ctx.shape[2], 512
    count = length // block

    def layer(full):
        return pl.BlockSpec((1,) + full.shape[1:], lambda i: (1, 0, 0))

    def tokens(rows):
        return pl.BlockSpec((rows, block), lambda i: (0, i))

    by_cell = pl.BlockSpec((1, block, 256), lambda i: (0, i, 0))
    return pl.pallas_call(
        turn_kernel,
        name="turn",
        grid=(count,),
        out_shape=(
            shape_of((1, length, 256), BF),
            shape_of((256, length), F32),
            shape_of((128, length), BF),
            shape_of((128, length), BF),
        )
        + tuple(shape_of(s, F32) for s in GRAD_SHAPES),
        in_specs=[
            SMEM_SPEC,
            ANY_SPEC,
            pl.BlockSpec((1, 128, block), lambda i: (0, 0, i)),
            tokens(256),
            by_cell,
            layer(wo),
            layer(wup),
            layer(wdn),
            layer(vec),
        ],
        out_specs=[by_cell, tokens(256), tokens(128), ANY_SPEC] + [whole(s) for s in GRAD_SHAPES],
        scratch_shapes=[
            pltpu.VMEM((128, length), BF),
            pltpu.VMEM((2560, 128), F32),
            pltpu.VMEM((2560, 128), F32),
            pltpu.VMEM((128, length), BF),
            pltpu.SemaphoreType.DMA((count + 1,)),
            pltpu.SemaphoreType.DMA((count + 1,)),
        ],
        compiler_params=params(4),
    )(lengths, ctx, ctx, x, cot, wo, wup, wdn, vec)


def input_block(core, own, peer, d_first, xb, contract, w_ref, sums, dwqkv):
    grad = d_first
    for half, part in ((core, own), (1 - core, peer)):
        rows = jnp.concatenate([half_rows(w_ref, 0, 256 * j, half) for j in range(3)], axis=0)
        grad = grad + dot(rows, part, 0, 0)
        dw = dot(part, xb, 1, contract)
        for j in range(3):
            at = pl.ds(pl.multiple_of(256 * j + half * 128, 128), 128)
            dwqkv[at] += dw[128 * j : 128 * j + 128]
        for j, name in ((0, QB), (2, VB)):
            at = pl.ds(pl.multiple_of(256 * name + half * 128, 128), 128)
            sums[at] += fold_lanes(part[128 * j : 128 * j + 128].astype(F32))
    return grad


def middle_kernel(
    dqkv_any, dqkv, d_first_in, x_ref, w_last, ctx, unit1, hidden, unit2, scales, wo, wup, wdn, vec,
    d_first, dctx_own, dctx_peer, dwqkv, dvec_last, dwo, dwup, dwdn, dvec,
    landed, cols, sums_last, sums, out, send, recv,
):
    i, count = pl.program_id(0), pl.num_programs(0)
    block = x_ref.shape[1]
    core, peer = pair_of()
    d_copy = to_peer(dqkv_any.at[1], landed, send.at[0], recv.at[0], peer)

    def copy(step):
        ds = pl.ds(pl.multiple_of(step * block, block), block)
        return to_peer(out.at[:, ds], dctx_peer.at[:, ds], send.at[1 + step], recv.at[1 + step], peer)

    @pl.when(i == 0)
    def _():
        greet(peer)
        d_copy.start()
        spread(vec.at[0], cols)
        for ref in (sums_last, sums, dwqkv, dwo, dwup, dwdn):
            ref[...] = jnp.zeros_like(ref)
        d_copy.wait()

    ds = pl.ds(pl.multiple_of(i * block, block), block)
    grad = input_block(
        core, dqkv[0], landed[:, ds], d_first_in[...], x_ref[...].astype(BF), 1, w_last, sums_last, dwqkv
    )
    saved = (unit1[...], scales[0:1], hidden[...], unit2[...], scales[1:2])
    d_first[...], d_context = backward_block(
        grad, ctx[...], saved, (wo[0], wup[0], wdn[0]), cols, sums, dwo, dwup, dwdn
    )
    low, high = d_context[:128], d_context[128:]
    dctx_own[...] = jnp.where(core == 0, low, high)
    out[:, ds] = jnp.where(core == 0, high, low)
    copy(i).start()

    @pl.when(i == count - 1)
    def _():
        dvec_last[...] = place_vectors(sums_last)
        dvec[...] = place_vectors(sums)

        @pl.loop(0, count)
        def _(step):
            copy(step).wait()


def middle(dqkv, d_first, x, wqkv, ctx, unit1, hidden, unit2, scales, wo, wup, wdn, vec):
    length, block = x.shape[1], 512
    count = length // block

    def layer(full, at):
        return pl.BlockSpec((1,) + full.shape[1:], lambda i: (at, 0, 0))

    def tokens(rows):
        return pl.BlockSpec((rows, block), lambda i: (0, i))

    shapes = ((768, 256), (256, 128)) + GRAD_SHAPES
    return pl.pallas_call(
        middle_kernel,
        name="back_between",
        grid=(count,),
        out_shape=(
            shape_of((256, length), F32),
            shape_of((128, length), BF),
            shape_of((128, length), BF),
        )
        + tuple(shape_of(s, F32) for s in shapes),
        in_specs=[
            ANY_SPEC,
            pl.BlockSpec((1, 384, block), lambda i: (0, 0, i)),
            tokens(256),
            tokens(256),
            layer(wqkv, 1),
            tokens(256),
            tokens(256),
            tokens(512),
            tokens(256),
            tokens(8),
            layer(wo, 0),
            layer(wup, 0),
            layer(wdn, 0),
            layer(vec, 0),
        ],
        out_specs=[tokens(256), tokens(128), ANY_SPEC] + [whole(s) for s in shapes],
        scratch_shapes=[
            pltpu.VMEM((384, length), BF),
            pltpu.VMEM((2560, 128), F32),
            pltpu.VMEM((2560, 128), F32),
            pltpu.VMEM((2560, 128), F32),
            pltpu.VMEM((128, length), BF),
            pltpu.SemaphoreType.DMA((count + 1,)),
            pltpu.SemaphoreType.DMA((count + 1,)),
        ],
        compiler_params=params(5),
    )(dqkv, dqkv, d_first, x, wqkv, ctx, unit1, hidden, unit2, scales, wo, wup, wdn, vec)


def last_kernel(
    dqkv_any, dqkv, d_first_in, x_ref, w_ref,
    grad_out, dwqkv, dvec,
    landed, sums, send, recv,
):
    i, count = pl.program_id(0), pl.num_programs(0)
    block = x_ref.shape[1]
    core, peer = pair_of()
    d_copy = to_peer(dqkv_any.at[1], landed, send, recv, peer)

    @pl.when(i == 0)
    def _():
        greet(peer)
        d_copy.start()
        for ref in (sums, dwqkv):
            ref[...] = jnp.zeros_like(ref)
        d_copy.wait()

    ds = pl.ds(pl.multiple_of(i * block, block), block)
    grad_out[...] = input_block(
        core, dqkv[0], landed[:, ds], d_first_in[...], x_ref[0], 0, w_ref, sums, dwqkv
    )

    @pl.when(i == count - 1)
    def _():
        dvec[...] = place_vectors(sums)


def last(dqkv, d_first, cells, wqkv):
    length, block = cells.shape[1], 512
    count = length // block

    def tokens(rows):
        return pl.BlockSpec((rows, block), lambda i: (0, i))

    shapes = ((768, 256), (256, 128))
    return pl.pallas_call(
        last_kernel,
        name="back_input",
        grid=(count,),
        out_shape=(shape_of((256, length), F32),) + tuple(shape_of(s, F32) for s in shapes),
        in_specs=[
            ANY_SPEC,
            pl.BlockSpec((1, 384, block), lambda i: (0, 0, i)),
            tokens(256),
            pl.BlockSpec((1, block, 256), lambda i: (0, i, 0)),
            pl.BlockSpec((1,) + wqkv.shape[1:], lambda i: (0, 0, 0)),
        ],
        out_specs=[tokens(256)] + [whole(s) for s in shapes],
        scratch_shapes=[
            pltpu.VMEM((384, length), BF),
            pltpu.VMEM((2560, 128), F32),
            pltpu.SemaphoreType.DMA,
            pltpu.SemaphoreType.DMA,
        ],
        compiler_params=params(6),
    )(dqkv, dqkv, d_first, cells, wqkv)


def sent_rows(ref, devices):
    return ref.reshape(devices, ref.shape[0] // devices, 256)


def exchange_kernel(devices, narrow, *refs):
    layers = (refs[0:6], refs[6:12])
    landed, out, send, recv = refs[12:]
    me = lax.axis_index("wide") * narrow + lax.axis_index("narrow")

    def place(i):
        return (i // narrow, lax.rem(i, narrow))

    barrier = pltpu.get_barrier_semaphore()

    @pl.loop(1, devices)
    def _(step):
        pl.semaphore_signal(
            barrier,
            inc=1,
            device_id=place(lax.rem(me + step, devices)),
            device_id_type=MESH,
        )

    for layer, (dwqkv, dvec_qkv, dwo, dwup, dwdn, dvec) in enumerate(layers):
        base = layer * (ROWS + 16)
        parts = [sent_rows(dwqkv[256 * j : 256 * j + 256], devices) for j in range(3)]
        parts += [sent_rows(dwo[...], devices), sent_rows(dwup[...], devices)]
        parts += [sent_rows(dwdn[:, 0:256], devices), sent_rows(dwdn[:, 256:512], devices)]
        vec = dvec_qkv[...] + dvec[...]
        high = vec.astype(BF).astype(F32)
        both = sent_rows(jnp.concatenate([high, vec - high], axis=1), devices)
        parts += [both, jnp.zeros_like(both)]
        out[:, base : base + ROWS + 16] = jnp.concatenate(parts, axis=1).astype(BF)

    pl.semaphore_wait(barrier, devices - 1)

    def copy(step):
        other = lax.rem(me + step, devices)
        return pltpu.make_async_remote_copy(
            src_ref=out.at[other],
            dst_ref=landed.at[me],
            send_sem=send.at[step],
            recv_sem=recv.at[step],
            device_id=place(other),
            device_id_type=MESH,
        )

    @pl.loop(1, devices)
    def _(step):
        copy(step).start()

    landed[me] = out[me]

    @pl.loop(1, devices)
    def _(step):
        copy(step).wait()


def exchange(devices, narrow, grads):
    block = (devices, 2 * (ROWS + 16), 256)
    return pl.pallas_call(
        functools.partial(exchange_kernel, devices, narrow),
        name="exchange_grads",
        out_shape=shape_of(block, BF),
        in_specs=[VMEM_SPEC] * 12,
        out_specs=VMEM_SPEC,
        scratch_shapes=[
            pltpu.VMEM(block, BF),
            pltpu.SemaphoreType.DMA((devices,)),
            pltpu.SemaphoreType.DMA((devices,)),
        ],
        compiler_params=params(7),
    )(*grads)


def finish_kernel(factor, landed, grad, grad_out, *refs):
    qw, qb, kw, vw, vb, ow, ob, g1, s1, uw, ub, dw, db, g2, s2 = refs
    length = grad.shape[1]
    total = jnp.sum(landed[...].astype(F32), axis=0) * factor
    for layer in range(2):
        rows = total[layer * (ROWS + 16) : (layer + 1) * (ROWS + 16)]
        for ref, at in ((qw, 0), (kw, 8), (vw, 16), (ow, 24)):
            ref[layer] = jnp.transpose(rows[at : at + 8])
        uw[layer] = jnp.transpose(rows[32:48])
        dw[layer, 0:256] = jnp.transpose(rows[48:56])
        dw[layer, 256:512] = jnp.transpose(rows[56:64])
        vec = jnp.transpose(rows[64:72, 0:128] + rows[64:72, 128:256])
        for i, ref in enumerate((qb, vb, ob, g1, s1, db, g2, s2)):
            ref[layer : layer + 1] = vec[i : i + 1]
        ub[layer : layer + 1, 0:8] = vec[8:9]
        ub[layer : layer + 1, 8:16] = vec[9:10]

    @pl.loop(0, length // 256)
    def _(i):
        ds = pl.ds(pl.multiple_of(i * 256, 256), 256)
        grad_out[0, ds] = jnp.transpose(grad[:, ds])


def finish(factor, landed, grad, like):
    return pl.pallas_call(
        functools.partial(finish_kernel, factor),
        name="finish",
        out_shape=(shape_of((1, grad.shape[1], 256), F32),)
        + tuple(shape_of(a.shape, F32) for a in like),
        in_specs=[VMEM_SPEC] * 2,
        out_specs=[VMEM_SPEC] * (1 + len(like)),
        compiler_params=params(),
    )(landed, grad)


def gather_by_collectives(weights, vectors):
    def whole_of(w):
        return lax.all_gather(jnp.swapaxes(w, 1, 2), AXES, axis=1, tiled=True)

    qw, kw, vw, ow, uw, dw = (whole_of(w) for w in weights)
    columns = [lax.all_gather(v, AXES, axis=1, tiled=True).astype(F32) for v in vectors]
    up = columns.pop().reshape(2, 32, 2, 8)
    columns += [up[:, :, 0].reshape(2, 256), up[:, :, 1].reshape(2, 256)]
    vec = jnp.pad(jnp.stack(columns, axis=2), ((0, 0), (0, 0), (0, 118)))
    return jnp.concatenate([qw, kw, vw], axis=1), ow, uw, dw, vec


def sum_by_collectives(factor, layers):
    def share(x):
        return lax.psum_scatter(x, AXES, scatter_dimension=0, tiled=True) * factor

    found = []
    for dwqkv, dvec_qkv, dwo, dwup, dwdn, dvec in layers:
        vec = dvec_qkv + dvec
        qb, vb, ob, g1, s1, db, g2, s2 = (share(vec[:, i]) for i in range(8))
        up = jnp.stack([vec[:, 8].reshape(32, 8), vec[:, 9].reshape(32, 8)], axis=1)
        qw, kw, vw = (share(dwqkv[256 * i : 256 * i + 256]).T for i in range(3))
        ow, uw, dw = share(dwo).T, share(dwup).T, share(dwdn).T
        ub = share(up.reshape(512))
        found.append((qw, qb, kw, vw, vb, ow, ob, g1, s1, uw, ub, dw, db, g2, s2))
    return [jnp.stack(pair) for pair in zip(*found)]


def on_device(devices, narrow, cells_in, lengths, cotangent, *weights):
    qw, qb, kw, vw, vb, ow, ob, g1, s1, uw, ub, dw, db, g2, s2 = weights
    direct = qw.shape[2] == 8
    gathered = (qw, kw, vw, ow, uw, dw), (qb, vb, ob, g1, s1, db, g2, s2, ub)
    if direct:
        wqkv, wo, wup, wdn, vec = gather_weights(devices, narrow, *gathered)
    else:
        wqkv, wo, wup, wdn, vec = gather_by_collectives(*gathered)
    lens, qkv0 = start(lengths, cells_in, wqkv, vec)
    ctx_pair, ctx32_0, logs0 = attend(lens, qkv0)
    x1, ctx0, unit1, hidden, unit2, scales, own, other = between(
        ctx_pair, cells_in, wqkv, wo, wup, wdn, vec
    )
    qkv1 = jnp.stack([own, other])
    ctx_pair, ctx32_1, logs1 = attend(lens, qkv1)
    cells_out, d_first, own, other, dwo1, dwup1, dwdn1, dvec1 = turn(
        lengths, ctx_pair, x1, cotangent, wo, wup, wdn, vec
    )
    dqkv = attend_back(lens, qkv1, jnp.stack([own, other]), ctx32_1, logs1)
    d_first, own, other, dwqkv1, dvecq1, dwo0, dwup0, dwdn0, dvec0 = middle(
        dqkv, d_first, x1, wqkv, ctx0, unit1, hidden, unit2, scales, wo, wup, wdn, vec
    )
    dqkv = attend_back(lens, qkv0, jnp.stack([own, other]), ctx32_0, logs0)
    grad, dwqkv0, dvecq0 = last(dqkv, d_first, cells_in, wqkv)
    layers = (
        (dwqkv0, dvecq0, dwo0, dwup0, dwdn0, dvec0),
        (dwqkv1, dvecq1, dwo1, dwup1, dwdn1, dvec1),
    )
    factor = 1.0 / math.sqrt(devices * cells_in.shape[0] * cells_in.shape[1])
    if not direct:
        grads = sum_by_collectives(factor, layers)
        return (cells_out, jnp.transpose(grad)[None], *grads)
    landed = exchange(devices, narrow, layers[0] + layers[1])
    grad_in, *grads = finish(factor, landed, grad, weights)
    return (cells_out, grad_in, *grads)


def solution(mesh):
    devices, narrow = mesh.size, mesh.shape["narrow"]
    cell, vector, matrix = P(AXES, None, None), P(None, AXES), P(None, None, AXES)
    placed = (
        matrix, vector, matrix, matrix, vector, matrix, vector, vector, vector,
        matrix, vector, matrix, vector, vector, vector,
    )
    return jax.shard_map(
        functools.partial(on_device, devices, narrow),
        mesh=mesh,
        in_specs=(cell, P(AXES), cell) + placed,
        out_specs=(cell, cell) + placed,
        check_vma=False,
    )
```

```python
import functools
import math

import jax
import jax.numpy as jnp
from jax import lax
from jax.experimental import pallas as pl
from jax.experimental.pallas import tpu as pltpu
from jax.sharding import PartitionSpec as P

HEAD = 64
NEG = -1000000000.0
EPS = 1e-06
AXES = ("wide", "narrow")
MESH = pl.DeviceIdType.MESH
BF = jnp.bfloat16
F32 = jnp.float32
EXT = 16
GUARD = 3600.0
KEY_SIZES = (512, 768, 1024, 1280, 1536, 2048)
ROWS = 64
VMEM_SPEC = pl.BlockSpec(memory_space=pltpu.VMEM)
SMEM_SPEC = pl.BlockSpec(memory_space=pltpu.SMEM)
ANY_SPEC = pl.BlockSpec(memory_space=pl.ANY)
QB, VB, OB, G1, S1, DB, G2, S2, UB = range(9)


def dot(a, b, ca, cb):
    return lax.dot_general(a, b, (((ca,), (cb,)), ((), ())), preferred_element_type=F32)


def params(collective_id=None, limit=56):
    if collective_id is None:
        return pltpu.CompilerParams(vmem_limit_bytes=limit << 20)
    return pltpu.CompilerParams(
        vmem_limit_bytes=limit << 20, collective_id=collective_id, has_side_effects=True
    )


def shape_of(shape, dtype):
    return jax.ShapeDtypeStruct(shape, dtype)


def pair_of():
    narrow = lax.axis_index("narrow")
    core = lax.rem(narrow, 2)
    return core, (lax.axis_index("wide"), narrow + 1 - 2 * core)


def greet(peer):
    barrier = pltpu.get_barrier_semaphore()
    pl.semaphore_signal(barrier, inc=1, device_id=peer, device_id_type=MESH)
    pl.semaphore_wait(barrier, 1)


def to_peer(src, dst, send, recv, peer):
    return pltpu.make_async_remote_copy(
        src_ref=src, dst_ref=dst, send_sem=send, recv_sem=recv, device_id=peer, device_id_type=MESH
    )


def half_rows(ref, lead, base, half):
    return ref[lead, pl.ds(pl.multiple_of(base + half * 128, 128), 128)]


def tile_lanes(column, count):
    return jnp.concatenate([column] * (count // 128), axis=1)


def spread(vec_ref, cols_ref):
    vec = vec_ref[...]
    width = vec.shape[0]
    for i in range(8):
        cols_ref[pl.ds(i * width, width)] = jnp.broadcast_to(vec[:, i : i + 1], (width, 128))
    low = jnp.broadcast_to(vec[:, 8:9], (width, 128)).reshape(width // 8, 8, 128)
    high = jnp.broadcast_to(vec[:, 9:10], (width, 128)).reshape(width // 8, 8, 128)
    cols_ref[pl.ds(8 * width, 2 * width)] = jnp.concatenate([low, high], axis=1).reshape(
        2 * width, 128
    )


def column(cols_ref, i, count):
    rows = 512 if i == UB else 256
    return tile_lanes(cols_ref[pl.ds(i * 256, rows)], count)


def fold_lanes(x):
    total = x[:, :128]
    for start in range(128, x.shape[1], 128):
        total = total + x[:, start : start + 128]
    return total


def norm(resid):
    offset = resid - jnp.mean(resid, axis=0, keepdims=True)
    scale = lax.rsqrt(jnp.mean(offset * offset, axis=0, keepdims=True) + EPS)
    return offset * scale, scale


def norm_back(grad, gain, unit, scale):
    q = grad * gain
    return (
        q - jnp.mean(q, axis=0, keepdims=True) - unit * jnp.mean(q * unit, axis=0, keepdims=True)
    ) * scale


GELU_C = 0.7978845608028654
GELU_A = 0.044715


def gelu_tanh(u):
    return jnp.tanh(GELU_C * (u + GELU_A * (u * u * u)))


def project(xb, contract, w_ref, cols_ref, half):
    parts = []
    for i in range(3):
        y = dot(half_rows(w_ref, 0, i * 256, half), xb, 1, contract)
        if i != 1:
            bias = cols_ref[
                pl.ds(pl.multiple_of((QB if i == 0 else VB) * 256 + half * 128, 128), 128)
            ]
            y = y + tile_lanes(bias, y.shape[1])
        y = y.astype(BF)
        parts.append(y * jnp.asarray(0.125, BF) if i == 0 else y)
    return jnp.concatenate(parts, axis=0)


def join(core, own, peer):
    return jnp.concatenate(
        [jnp.where(core == 0, own, peer), jnp.where(core == 0, peer, own)], axis=0
    )


def forward_block(context, x, wo, wup, wdn, cols_ref):
    count = x.shape[1]
    unit1, scale1 = norm(x + dot(wo, context, 1, 0) + column(cols_ref, OB, count))
    middle = unit1 * column(cols_ref, G1, count) + column(cols_ref, S1, count)
    hidden = dot(wup, middle.astype(BF), 1, 0) + column(cols_ref, UB, count)
    active = (0.5 * hidden * (1.0 + gelu_tanh(hidden))).astype(BF)
    unit2, scale2 = norm(middle + dot(wdn, active, 1, 0) + column(cols_ref, DB, count))
    x_next = unit2 * column(cols_ref, G2, count) + column(cols_ref, S2, count)
    return unit1, scale1, hidden, unit2, scale2, x_next


def backward_block(grad, context, saved, weights, cols_ref, sums, dwo, dwup, dwdn):
    unit1, scale1, hidden, unit2, scale2 = saved
    wo, wup, wdn = weights
    count = grad.shape[1]

    def add(i, x):
        rows = x.shape[0]
        sums[pl.ds(i * 256, rows)] += fold_lanes(x)

    add(S2, grad)
    add(G2, grad * unit2)
    d_second = norm_back(grad, column(cols_ref, G2, count), unit2, scale2)
    branch = d_second.astype(BF)
    add(DB, branch.astype(F32))
    t = gelu_tanh(hidden)
    active = (0.5 * hidden * (1.0 + t)).astype(BF)
    slope = 0.5 * (1.0 + t) + (0.5 * GELU_C) * hidden * (1.0 - t * t) * (
        1.0 + (3.0 * GELU_A) * (hidden * hidden)
    )
    dwdn[...] += dot(branch, active, 1, 1)
    d_hidden = (dot(wdn, branch, 0, 0) * slope).astype(BF)
    add(UB, d_hidden.astype(F32))
    middle = unit1 * column(cols_ref, G1, count) + column(cols_ref, S1, count)
    dwup[...] += dot(d_hidden, middle.astype(BF), 1, 1)
    d_middle = d_second + dot(wup, d_hidden, 0, 0)
    add(S1, d_middle)
    add(G1, d_middle * unit1)
    d_first = norm_back(d_middle, column(cols_ref, G1, count), unit1, scale1)
    attn = d_first.astype(BF)
    add(OB, attn.astype(F32))
    dwo[...] += dot(attn, context, 1, 1)
    return d_first, dot(wo, attn, 0, 0).astype(BF)


def place_vectors(sums):
    lane = lax.broadcasted_iota(jnp.int32, (256, 128), 1)
    out = jnp.zeros((256, 128), F32)
    for i in range(8):
        total = jnp.sum(sums[pl.ds(i * 256, 256)], axis=1, keepdims=True)
        out = jnp.where(lane == i, total, out)
    up = jnp.sum(sums[pl.ds(2048, 512)], axis=1, keepdims=True)
    up = jnp.broadcast_to(up, (512, 128)).reshape(32, 16, 128)
    out = jnp.where(lane == 8, up[:, :8].reshape(256, 128), out)
    return jnp.where(lane == 9, up[:, 8:].reshape(256, 128), out)


def coordinates():
    wide, narrow = lax.axis_index("wide"), lax.axis_index("narrow")
    return wide // 2, lax.rem(wide, 2), narrow // 2, lax.rem(narrow, 2)


def device_at(z, x, y, core):
    return (2 * z + x, 2 * y + core)


def plane_mates():
    z, x, y, core = coordinates()
    return [
        (device_at(z, a, b, core), 2 * a + b) for a, b in ((x, 1 - y), (1 - x, y), (1 - x, 1 - y))
    ]


def line_mates():
    z, x, y, core = coordinates()
    there = [lax.rem(z + j, 4) for j in (1, 2, 3)]
    return [(device_at(a, x, y, core), a) for a in there]


def sibling():
    z, x, y, core = coordinates()
    return device_at(z, x, y, 1 - core)


def greet_all():
    barrier = pltpu.get_barrier_semaphore()
    mates = [sibling()] + [d for d, _ in plane_mates()] + [d for d, _ in line_mates()]
    for mate in mates:
        pl.semaphore_signal(barrier, inc=1, device_id=mate, device_id_type=MESH)
    pl.semaphore_wait(barrier, len(mates))


FIRST, REST = 48, 96


def eight(x):
    return x.astype(F32)


def pack_own(weights, vectors, first, rest, flat):
    qw, kw, vw, ow, uw, dw = weights

    def four(layer):
        return [eight(w[layer]) for w in (qw, kw, vw, ow)]

    def two(layer):
        down = eight(dw[layer])
        return [eight(uw[layer]), down[:, :256], down[:, 256:]]

    flat[...] = jnp.zeros_like(flat)
    for i, v in enumerate(vectors):
        flat[pl.ds(2 * i, 2), 0:8] = v[:, 0:8].astype(F32)
        if v.shape[1] == 16:
            flat[pl.ds(2 * i + 2, 2), 0:8] = v[:, 8:16].astype(F32)
    columns = jnp.transpose(flat[...])[0:8]
    block = jnp.concatenate([columns, jnp.zeros_like(columns)], axis=1)
    first[...] = jnp.concatenate(four(0) + [block, jnp.zeros_like(block)], axis=0).astype(BF)
    rest[...] = jnp.concatenate(two(0) + four(1) + two(1), axis=0).astype(BF)


def ordered(landed, at, rows):
    pieces = [
        landed[core, plane, z, at : at + rows]
        for z in range(4)
        for plane in range(4)
        for core in range(2)
    ]
    return jnp.stack(pieces)


def two_matrices(landed, at):
    pair = ordered(landed, at, 16).astype(F32)
    return (
        pair[:, :8].reshape(256, 256).astype(BF),
        pair[:, 8:].reshape(256, 256).astype(BF),
    )


def unpack_first(landed, wqkv, wo, vec):
    wqkv[0, 0:256], wqkv[0, 256:512] = two_matrices(landed, 0)
    wqkv[0, 512:768], wo[0] = two_matrices(landed, 16)
    both = ordered(landed, 32, 16).astype(F32)[:, :8, :128].reshape(256, 128)
    lane = lax.broadcasted_iota(jnp.int32, (256, 128), 1)
    for layer in range(2):
        out = jnp.zeros((256, 128), F32)
        for i in range(10):
            out = jnp.where(lane == i, both[:, 2 * i + layer : 2 * i + layer + 1], out)
        vec[layer] = out


def unpack_rest(landed, wqkv, wo, wup, wdn):
    wqkv[1, 0:256], wqkv[1, 256:512] = two_matrices(landed, 32)
    wqkv[1, 512:768], wo[1] = two_matrices(landed, 48)
    for layer, at in ((0, 0), (1, 64)):
        wup[layer] = ordered(landed, at, 16).reshape(512, 256)
        wdn[layer, :, 0:256], wdn[layer, :, 256:512] = two_matrices(landed, at + 16)


class Gather:
    def __init__(self, own, landed, send, recv, part):
        z, x, y, core = coordinates()
        plane = 2 * x + y

        def copy(src, dst, i, device):
            return pltpu.make_async_remote_copy(
                src_ref=src,
                dst_ref=dst,
                send_sem=send.at[part, i],
                recv_sem=recv.at[part, i],
                device_id=device,
                device_id_type=MESH,
            )

        def column(i):
            return landed.at[core, i]

        self.keep = lambda: landed.at[core, plane, z].__setitem__(Ellipsis, own[...])
        self.line = [
            copy(own, landed.at[core, plane, z], i, device)
            for i, (device, _) in enumerate(line_mates())
        ]
        self.plane = [
            copy(column(plane), column(plane), 3 + i, device)
            for i, (device, _) in enumerate(plane_mates())
        ]
        columns = [plane] + [number for _, number in plane_mates()]
        self.cores = [
            copy(column(number), column(number), 6 + i, sibling())
            for i, number in enumerate(columns)
        ]


def start_kernel(*refs):
    len_ref, x_ref = refs[:2]
    weights, vectors = refs[2:8], refs[8:17]
    lens, qkv, wqkv, wo, wup, wdn, vec = refs[17:24]
    first, rest, flat, landed_first, landed_rest, cols, out, own_len = refs[24:32]
    send, recv, pair_send, pair_recv = refs[32:]
    core, peer = pair_of()
    pack_own(weights, vectors, first, rest, flat)
    a = Gather(first, landed_first, send, recv, 0)
    b = Gather(rest, landed_rest, send, recv, 1)
    greet_all()
    for c in a.line + b.line:
        c.start()
    own_len[...] = jnp.full(own_len.shape, len_ref[0], jnp.int32)
    len_copy = to_peer(own_len, lens.at[1], pair_send.at[0], pair_recv.at[0], peer)
    len_copy.start()
    lens[0] = own_len[...]
    a.keep()
    b.keep()
    for part in (a, b):
        for c in part.line:
            c.wait()
        for c in part.plane + part.cores[:1]:
            c.start()
    for i in range(3):
        a.plane[i].wait()
        a.cores[1 + i].start()
    for c in a.cores:
        c.wait()
    unpack_first(landed_first, wqkv, wo, vec)
    spread(vec.at[0], cols)
    block = 512
    count = x_ref.shape[1] // block

    def copy(i):
        ds = pl.ds(pl.multiple_of(i * block, block), block)
        return to_peer(
            out.at[:, ds], qkv.at[1, :, ds], pair_send.at[1 + i], pair_recv.at[1 + i], peer
        )

    @pl.loop(0, count)
    def _(i):
        ds = pl.ds(pl.multiple_of(i * block, block), block)
        out[:, ds] = project(x_ref[0, ds], 1, wqkv, cols, 1 - core)
        copy(i).start()

    @pl.loop(0, count)
    def _(i):
        ds = pl.ds(pl.multiple_of(i * block, block), block)
        qkv[0, :, ds] = project(x_ref[0, ds], 1, wqkv, cols, core)

    for i in range(3):
        b.plane[i].wait()
        b.cores[1 + i].start()
    for c in b.cores:
        c.wait()
    unpack_rest(landed_rest, wqkv, wo, wup, wdn)
    len_copy.wait()

    @pl.loop(0, count)
    def _(i):
        copy(i).wait()


def start(lengths, cells, weights, vectors):
    length = cells.shape[1]
    count = length // 512
    return pl.pallas_call(
        start_kernel,
        name="gather_and_project",
        out_shape=(
            shape_of((2, 8, 128), jnp.int32),
            shape_of((2, 384, length), BF),
            shape_of((2, 768, 256), BF),
            shape_of((2, 256, 256), BF),
            shape_of((2, 512, 256), BF),
            shape_of((2, 256, 512), BF),
            shape_of((2, 256, 128), F32),
        ),
        in_specs=[SMEM_SPEC] + [VMEM_SPEC] * 16,
        out_specs=[VMEM_SPEC] * 7,
        scratch_shapes=[
            pltpu.VMEM((FIRST, 256), BF),
            pltpu.VMEM((REST, 256), BF),
            pltpu.VMEM((128, 128), F32),
            pltpu.VMEM((2, 4, 4, FIRST, 256), BF),
            pltpu.VMEM((2, 4, 4, REST, 256), BF),
            pltpu.VMEM((2560, 128), F32),
            pltpu.VMEM((384, length), BF),
            pltpu.VMEM((8, 128), jnp.int32),
            pltpu.SemaphoreType.DMA((2, 10)),
            pltpu.SemaphoreType.DMA((2, 10)),
            pltpu.SemaphoreType.DMA((count + 1,)),
            pltpu.SemaphoreType.DMA((count + 1,)),
        ],
        compiler_params=params(1),
    )(lengths, cells, *weights, *vectors)


def project_kernel(len_ref, x_ref, w_ref, vec_ref, lens, qkv, cols, out, own_len, send, recv):
    core, peer = pair_of()
    spread(vec_ref.at[0], cols)
    own_len[...] = jnp.full(own_len.shape, len_ref[0], jnp.int32)
    greet(peer)
    len_copy = to_peer(own_len, lens.at[1], send.at[0], recv.at[0], peer)
    len_copy.start()
    lens[0] = own_len[...]
    out[...] = project(x_ref[0], 1, w_ref, cols, 1 - core)
    qkv_copy = to_peer(out, qkv.at[1], send.at[1], recv.at[1], peer)
    qkv_copy.start()
    qkv[0] = project(x_ref[0], 1, w_ref, cols, core)
    len_copy.wait()
    qkv_copy.wait()


def project_first(lengths, cells, wqkv, vec):
    length = cells.shape[1]
    return pl.pallas_call(
        project_kernel,
        name="project_first",
        out_shape=(shape_of((2, 8, 128), jnp.int32), shape_of((2, 384, length), BF)),
        in_specs=[SMEM_SPEC] + [VMEM_SPEC] * 3,
        out_specs=[VMEM_SPEC] * 2,
        scratch_shapes=[
            pltpu.VMEM((2560, 128), F32),
            pltpu.VMEM((384, length), BF),
            pltpu.VMEM((8, 128), jnp.int32),
            pltpu.SemaphoreType.DMA((2,)),
            pltpu.SemaphoreType.DMA((2,)),
        ],
        compiler_params=params(2),
    )(lengths, cells, wqkv, vec)


def key_sizes(length):
    return [size for size in KEY_SIZES if size < length] + [length]


def extended(x, extra):
    return jnp.concatenate([x, extra], axis=0)


def one_head(x, head):
    row = lax.broadcasted_iota(jnp.int32, x.shape, 0)
    return jnp.where((row // HEAD) == head, x, jnp.zeros_like(x))


def attend_kernel(lens, qkv, ctx, ctx32, logs, kx, scores, total, acc):
    length = qkv.shape[2]
    wide = 512
    count = length // wide
    row = lax.broadcasted_iota(jnp.int32, (EXT, wide), 0)
    ones = jnp.where(row == 0, 1.0, 0.0).astype(BF)

    def query_of(cell, i, head):
        q = qkv[cell, 0:128, pl.ds(pl.multiple_of(i * wide, wide), wide)]
        return extended(one_head(q, head), ones)

    def finish(cell, i, head, high, sums, out):
        ds = pl.ds(pl.multiple_of(i * wide, wide), wide)
        sums = jnp.sum(sums, axis=0, keepdims=True)
        out = out * (1.0 / sums)
        rows = slice(HEAD * head, HEAD * head + HEAD)
        ctx[cell, rows, ds] = out.astype(BF)
        ctx32[cell, rows, ds] = out
        logs[cell, head : head + 1, ds] = jnp.log(sums) + high

    def largest(x):
        x = x.astype(F32)
        square = x * x
        return [
            jnp.max(jnp.sum(square[HEAD * h : HEAD * h + HEAD], axis=0, keepdims=True))
            for h in range(2)
        ]

    @pl.loop(0, 2)
    def _(cell):
        valid = lens[cell, 0, 0]
        q_most = largest(qkv[cell, 0:128])
        k_most = largest(qkv[cell, 128:256])
        plain = jnp.maximum(q_most[0] * k_most[0], q_most[1] * k_most[1]) <= GUARD

        @pl.loop(0, pl.cdiv(valid, 256))
        def _(i):
            ds = pl.ds(pl.multiple_of(i * 256, 256), 256)
            where = lax.broadcasted_iota(jnp.int32, (EXT, 256), 1) + i * 256
            first = lax.broadcasted_iota(jnp.int32, (EXT, 256), 0) == 0
            extra = jnp.where(first & (where >= valid), NEG, 0.0).astype(BF)
            kx[ds] = jnp.transpose(extended(qkv[cell, 128:256, ds], extra))

        sizes = key_sizes(length)
        for low, size in zip([0] + sizes[:-1], sizes):
            @pl.when(plain & (valid > low) & (valid <= size))
            def _(size=size):
                @pl.loop(pl.cdiv(valid, 256), size // 256)
                def _(i):
                    lane = lax.broadcasted_iota(jnp.int32, (256, 128 + EXT), 1)
                    kx[pl.ds(pl.multiple_of(i * 256, 256), 256)] = jnp.where(
                        lane == 128, NEG, 0.0
                    ).astype(BF)

                @pl.loop(0, count)
                def _(i):
                    for head in range(2):
                        s = dot(kx[0:size], query_of(cell, i, head), 1, 0)
                        e = jnp.exp(s)
                        sums = jnp.sum(e.reshape(size // 8, 8, wide), axis=0)
                        v = qkv[cell, 256 + HEAD * head : 320 + HEAD * head, 0:size]
                        finish(cell, i, head, 0.0, sums, dot(v, e.astype(BF), 1, 0))

        @pl.when(jnp.logical_not(plain))
        def _():
            chunks = pl.cdiv(valid, 256)

            @pl.loop(0, count)
            def _(i):
                for head in range(2):
                    query = query_of(cell, i, head)

                    def score(j, high):
                        s = dot(kx[pl.ds(pl.multiple_of(j * 256, 256), 256)], query, 1, 0)
                        scores[j] = s
                        return jnp.maximum(high, jnp.max(s.reshape(32, 8, wide), axis=0))

                    high = lax.fori_loop(0, chunks, score, jnp.full((8, wide), NEG * 2, F32))
                    high = jnp.max(high, axis=0, keepdims=True)
                    acc[...] = jnp.zeros_like(acc)
                    total[...] = jnp.zeros_like(total)

                    @pl.loop(0, chunks)
                    def _(j):
                        e = jnp.exp(scores[j] - high)
                        total[...] += jnp.sum(e.reshape(32, 8, wide), axis=0)
                        v = qkv[
                            cell,
                            256 + HEAD * head : 320 + HEAD * head,
                            pl.ds(pl.multiple_of(j * 256, 256), 256),
                        ]
                        acc[...] += dot(v, e.astype(BF), 1, 0)

                    finish(cell, i, head, high, total[...], acc[...])


def attend(lens, qkv):
    length = qkv.shape[2]
    return pl.pallas_call(
        attend_kernel,
        name="attend",
        out_shape=(
            shape_of((2, 128, length), BF),
            shape_of((2, 128, length), F32),
            shape_of((2, 2, length), F32),
        ),
        in_specs=[SMEM_SPEC, VMEM_SPEC],
        out_specs=[VMEM_SPEC] * 3,
        scratch_shapes=[
            pltpu.VMEM((length, 128 + EXT), BF),
            pltpu.VMEM((length // 256, 256, 512), F32),
            pltpu.VMEM((8, 512), F32),
            pltpu.VMEM((HEAD, 512), F32),
        ],
        compiler_params=params(),
    )(lens, qkv)


def in_three(x):
    high = x.astype(BF)
    rest = x - high.astype(F32)
    middle = rest.astype(BF)
    return high, middle, (rest - middle.astype(F32)).astype(BF)


def attend_back_kernel(lens, qkv, grad, ctx32, logs, out, right_s, right_d, keys, sum_k, sum_v):
    length = qkv.shape[2]
    wide = 256
    row = lax.broadcasted_iota(jnp.int32, (EXT, wide), 0)

    def left(x, head, value, last):
        a, b, c = in_three(value)
        zero = jnp.zeros((EXT, wide), BF)
        extra = jnp.where(row == 0, a, jnp.where(row == 1, b, jnp.where(row == 2, c, zero)))
        if last:
            extra = jnp.where(row == 3, jnp.ones_like(zero), extra)
        return jnp.transpose(extended(one_head(x, head), extra))

    @pl.loop(0, 2)
    def _(cell):
        valid = lens[cell, 0, 0]
        out[cell] = jnp.zeros_like(out[cell])
        sizes = key_sizes(length)
        for low, size in zip([0] + sizes[:-1], sizes):

            @pl.when((valid > low) & (valid <= size))
            def _(size=size):
                where = lax.broadcasted_iota(jnp.int32, (EXT, size), 1)
                rows = lax.broadcasted_iota(jnp.int32, (EXT, size), 0)
                extra = jnp.where(
                    rows < 3, 1.0, jnp.where((rows == 3) & (where >= valid), NEG, 0.0)
                ).astype(BF)
                right_s[0:128, 0:size] = qkv[cell, 128:256, 0:size]
                right_s[128:, 0:size] = extra
                right_d[0:128, 0:size] = qkv[cell, 256:384, 0:size]
                right_d[128:, 0:size] = extra
                keys[0:size] = jnp.transpose(qkv[cell, 128:256, 0:size])
                sum_k[:, 0:size] = jnp.zeros((128, size), F32)
                sum_v[:, 0:size] = jnp.zeros((128, size), F32)

                @pl.loop(0, pl.cdiv(valid, wide))
                def _(i):
                    ds = pl.ds(pl.multiple_of(i * wide, wide), wide)
                    q = qkv[cell, 0:128, ds]
                    d = grad[cell, :, ds]
                    inner = d.astype(F32) * ctx32[cell, :, ds]
                    for head in range(2):
                        at = slice(HEAD * head, HEAD * head + HEAD)
                        delta = jnp.sum(inner[at], axis=0, keepdims=True)
                        s = dot(
                            left(q, head, -logs[cell, head : head + 1, ds], True),
                            right_s[:, 0:size],
                            1,
                            0,
                        )
                        p = jnp.exp(s)
                        dp = dot(left(d, head, -delta, False), right_d[:, 0:size], 1, 0)
                        ds_low = (p * dp).astype(BF)
                        sum_v[at, 0:size] += dot(d[at], p.astype(BF), 1, 0)
                        sum_k[at, 0:size] += dot(q[at], ds_low, 1, 0)
                        dq = dot(qkv[cell, 128 + HEAD * head : 192 + HEAD * head, 0:size], ds_low, 1, 1)
                        out[cell, at, ds] = (dq * 0.125).astype(BF)

                out[cell, 128:256, 0:size] = sum_k[:, 0:size].astype(BF)
                out[cell, 256:384, 0:size] = sum_v[:, 0:size].astype(BF)


def attend_back(lens, qkv, grad, ctx32, logs):
    length = qkv.shape[2]
    return pl.pallas_call(
        attend_back_kernel,
        name="attend_back",
        out_shape=shape_of((2, 384, length), BF),
        in_specs=[SMEM_SPEC] + [VMEM_SPEC] * 4,
        out_specs=VMEM_SPEC,
        scratch_shapes=[
            pltpu.VMEM((128 + EXT, length), BF),
            pltpu.VMEM((128 + EXT, length), BF),
            pltpu.VMEM((length, 128), BF),
            pltpu.VMEM((128, length), F32),
            pltpu.VMEM((128, length), F32),
        ],
        compiler_params=params(),
    )(lens, qkv, grad, ctx32, logs)


def between_kernel(
    ctx_any, ctx, x_ref, w_next, wo, wup, wdn, vec, vec_next,
    x_out, ctx_out, unit1, hidden, unit2, scales, qkv,
    landed, cols, cols_next, kept, out, send, recv, local,
):
    i, count = pl.program_id(0), pl.num_programs(0)
    block = x_out.shape[1]
    core, peer = pair_of()
    ctx_copy = to_peer(ctx_any.at[1], landed, send.at[0], recv.at[0], peer)

    def copy(step):
        ds = pl.ds(pl.multiple_of(step * block, block), block)
        return to_peer(out.at[:, ds], qkv.at[1, :, ds], send.at[1 + step], recv.at[1 + step], peer)

    def keep(step):
        ds = pl.ds(pl.multiple_of(step * block, block), block)
        return pltpu.make_async_copy(kept.at[:, ds], qkv.at[0, :, ds], local.at[step])

    @pl.when(i == 0)
    def _():
        greet(peer)
        ctx_copy.start()
        spread(vec.at[0], cols)
        spread(vec_next.at[0], cols_next)
        ctx_copy.wait()

    ds = pl.ds(pl.multiple_of(i * block, block), block)
    context = join(core, ctx[0], landed[:, ds])
    ctx_out[...] = context
    x = jnp.transpose(x_ref[0].astype(F32))
    unit1[...], scale1, hidden[...], unit2[...], scale2, x_next = forward_block(
        context, x, wo[0], wup[0], wdn[0], cols
    )
    scales[0:1] = scale1
    scales[1:2] = scale2
    x_out[...] = x_next
    low = x_next.astype(BF)
    out[:, ds] = project(low, 0, w_next, cols_next, 1 - core)
    copy(i).start()
    kept[:, ds] = project(low, 0, w_next, cols_next, core)
    keep(i).start()

    @pl.when(i == count - 1)
    def _():
        @pl.loop(0, count)
        def _(step):
            copy(step).wait()
            keep(step).wait()


def between(ctx, cells, wqkv, wo, wup, wdn, vec):
    length, block = ctx.shape[2], 512
    count = length // block

    def layer(full, at):
        return pl.BlockSpec((1,) + full.shape[1:], lambda i: (at, 0, 0))

    def tokens(rows):
        return pl.BlockSpec((rows, block), lambda i: (0, i))

    return pl.pallas_call(
        between_kernel,
        name="between_layers",
        grid=(count,),
        out_shape=(
            shape_of((256, length), F32),
            shape_of((256, length), BF),
            shape_of((256, length), F32),
            shape_of((512, length), F32),
            shape_of((256, length), F32),
            shape_of((8, length), F32),
            shape_of((2, 384, length), BF),
        ),
        in_specs=[
            ANY_SPEC,
            pl.BlockSpec((1, 128, block), lambda i: (0, 0, i)),
            pl.BlockSpec((1, block, 256), lambda i: (0, i, 0)),
            layer(wqkv, 1),
            layer(wo, 0),
            layer(wup, 0),
            layer(wdn, 0),
            layer(vec, 0),
            layer(vec, 1),
        ],
        out_specs=[
            tokens(256), tokens(256), tokens(256), tokens(512), tokens(256), tokens(8), ANY_SPEC,
        ],
        scratch_shapes=[
            pltpu.VMEM((128, length), BF),
            pltpu.VMEM((2560, 128), F32),
            pltpu.VMEM((2560, 128), F32),
            pltpu.VMEM((384, length), BF),
            pltpu.VMEM((384, length), BF),
            pltpu.SemaphoreType.DMA((count + 1,)),
            pltpu.SemaphoreType.DMA((count + 1,)),
            pltpu.SemaphoreType.DMA((count,)),
        ],
        compiler_params=params(3),
    )(ctx, ctx, cells, wqkv, wo, wup, wdn, vec, vec)


def turn_kernel(
    len_ref, ctx_any, ctx, x_ref, cot, wo, wup, wdn, vec,
    cells_out, d_first, dctx, dwo, dwup, dwdn, dvec,
    landed, cols, sums, kept, out, send, recv, local,
):
    i, count = pl.program_id(0), pl.num_programs(0)
    block = x_ref.shape[1]
    core, peer = pair_of()
    ctx_copy = to_peer(ctx_any.at[1], landed, send.at[0], recv.at[0], peer)

    def copy(step):
        ds = pl.ds(pl.multiple_of(step * block, block), block)
        return to_peer(out.at[:, ds], dctx.at[1, :, ds], send.at[1 + step], recv.at[1 + step], peer)

    def keep(step):
        ds = pl.ds(pl.multiple_of(step * block, block), block)
        return pltpu.make_async_copy(kept.at[:, ds], dctx.at[0, :, ds], local.at[step])

    @pl.when(i == 0)
    def _():
        greet(peer)
        ctx_copy.start()
        spread(vec.at[0], cols)
        for ref in (sums, dwo, dwup, dwdn):
            ref[...] = jnp.zeros_like(ref)
        ctx_copy.wait()

    ds = pl.ds(pl.multiple_of(i * block, block), block)
    context = join(core, ctx[0], landed[:, ds])
    weights = (wo[0], wup[0], wdn[0])
    *saved, x_next = forward_block(context, x_ref[...], *weights, cols)
    cells_out[0] = jnp.transpose(x_next).astype(BF)
    where = lax.broadcasted_iota(jnp.int32, (256, block), 1) + i * block
    grad = jnp.where(where < len_ref[0], jnp.transpose(cot[0].astype(F32)), 0.0)
    d_first[...], d_context = backward_block(
        grad, context, saved, weights, cols, sums, dwo, dwup, dwdn
    )
    low, high = d_context[:128], d_context[128:]
    out[:, ds] = jnp.where(core == 0, high, low)
    copy(i).start()
    kept[:, ds] = jnp.where(core == 0, low, high)
    keep(i).start()

    @pl.when(i == count - 1)
    def _():
        dvec[...] = place_vectors(sums)

        @pl.loop(0, count)
        def _(step):
            copy(step).wait()
            keep(step).wait()


GRAD_SHAPES = ((256, 256), (512, 256), (256, 512), (256, 128))


def whole(shape):
    return pl.BlockSpec(shape, lambda i: (0,) * len(shape))


def turn(lengths, ctx, x, cot, wo, wup, wdn, vec):
    length, block = ctx.shape[2], 512
    count = length // block

    def layer(full):
        return pl.BlockSpec((1,) + full.shape[1:], lambda i: (1, 0, 0))

    def tokens(rows):
        return pl.BlockSpec((rows, block), lambda i: (0, i))

    by_cell = pl.BlockSpec((1, block, 256), lambda i: (0, i, 0))
    return pl.pallas_call(
        turn_kernel,
        name="turn",
        grid=(count,),
        out_shape=(
            shape_of((1, length, 256), BF),
            shape_of((256, length), F32),
            shape_of((2, 128, length), BF),
        )
        + tuple(shape_of(s, F32) for s in GRAD_SHAPES),
        in_specs=[
            SMEM_SPEC,
            ANY_SPEC,
            pl.BlockSpec((1, 128, block), lambda i: (0, 0, i)),
            tokens(256),
            by_cell,
            layer(wo),
            layer(wup),
            layer(wdn),
            layer(vec),
        ],
        out_specs=[by_cell, tokens(256), ANY_SPEC] + [whole(s) for s in GRAD_SHAPES],
        scratch_shapes=[
            pltpu.VMEM((128, length), BF),
            pltpu.VMEM((2560, 128), F32),
            pltpu.VMEM((2560, 128), F32),
            pltpu.VMEM((128, length), BF),
            pltpu.VMEM((128, length), BF),
            pltpu.SemaphoreType.DMA((count + 1,)),
            pltpu.SemaphoreType.DMA((count + 1,)),
            pltpu.SemaphoreType.DMA((count,)),
        ],
        compiler_params=params(4),
    )(lengths, ctx, ctx, x, cot, wo, wup, wdn, vec)


OUTER, INNER = 48, 32


def shares(x):
    return x.reshape(32, x.shape[0] // 32, 256)


def vector_shares(vec):
    high = vec.astype(BF).astype(F32)
    return shares(jnp.concatenate([high, vec - high], axis=1))


def outer_shares(dwo, dwup, dwdn, dvec):
    return [
        shares(dwo[...]),
        shares(dwdn[:, 0:256]),
        shares(dwdn[:, 256:512]),
        vector_shares(dvec[...]),
        shares(dwup[...]),
    ]


def inner_shares(dwqkv, dvec):
    return [shares(dwqkv[256 * j : 256 * j + 256]) for j in range(3)] + [vector_shares(dvec[...])]


def reduce_scratch(rows):
    return [
        pltpu.VMEM((2, 4, 4, rows, 256), BF),
        pltpu.VMEM((4, 4, rows, 256), BF),
        pltpu.VMEM((4, 4, rows, 256), BF),
        pltpu.VMEM((3, 4, rows, 256), BF),
        pltpu.VMEM((4, rows, 256), BF),
        pltpu.VMEM((3, rows, 256), BF),
        pltpu.SemaphoreType.DMA((7,)),
        pltpu.SemaphoreType.DMA((7,)),
    ]


REDUCE_REFS = 8


class Reduce:
    def __init__(self, own, from_core, by_plane, from_plane, by_line, from_line, send, recv):
        self.refs = own, from_core, by_plane, from_plane, by_line, from_line
        z, x, y, core = coordinates()
        self.z, self.number, self.core = z, 2 * x + y, core

        def copy(src, dst, i, device):
            return pltpu.make_async_remote_copy(
                src_ref=src,
                dst_ref=dst,
                send_sem=send.at[i],
                recv_sem=recv.at[i],
                device_id=device,
                device_id_type=MESH,
            )

        self.cores = [copy(own.at[1 - core], from_core, 0, sibling())]
        self.plane = [
            copy(by_plane.at[number], from_plane.at[i], 1 + i, device)
            for i, (device, number) in enumerate(plane_mates())
        ]
        self.line = [
            copy(by_line.at[there], from_line.at[i], 4 + i, device)
            for i, (device, there) in enumerate(line_mates())
        ]

    def fill(self, pieces):
        own = self.refs[0]
        rows = own.shape[3]
        terms = jnp.concatenate(pieces, axis=1).astype(BF).reshape(4, 4, 2, rows, 256)
        for core in range(2):
            for plane in range(4):
                own[core, plane] = terms[:, plane, core]

    def first(self):
        for c in self.cores:
            c.start()

    def second(self):
        own, from_core, by_plane = self.refs[:3]
        for c in self.cores:
            c.wait()
        by_plane[...] = (own[self.core].astype(F32) + from_core[...].astype(F32)).astype(BF)
        for c in self.plane:
            c.start()

    def third(self):
        by_plane, from_plane, by_line = self.refs[2:5]
        for c in self.plane:
            c.wait()
        total = by_plane[self.number].astype(F32)
        for i in range(3):
            total = total + from_plane[i].astype(F32)
        by_line[...] = total.astype(BF)
        for c in self.line:
            c.start()

    def result(self):
        by_line, from_line = self.refs[4:6]
        for c in self.line:
            c.wait()
        total = by_line[self.z].astype(F32)
        for i in range(3):
            total = total + from_line[i].astype(F32)
        return total


def input_block(core, own, peer, d_first, xb, contract, w_ref, sums, dwqkv):
    grad = d_first
    for half, part in ((core, own), (1 - core, peer)):
        rows = jnp.concatenate([half_rows(w_ref, 0, 256 * j, half) for j in range(3)], axis=0)
        grad = grad + dot(rows, part, 0, 0)
        dw = dot(part, xb, 1, contract)
        for j in range(3):
            at = pl.ds(pl.multiple_of(256 * j + half * 128, 128), 128)
            dwqkv[at] += dw[128 * j : 128 * j + 128]
        for j, name in ((0, QB), (2, VB)):
            at = pl.ds(pl.multiple_of(256 * name + half * 128, 128), 128)
            sums[at] += fold_lanes(part[128 * j : 128 * j + 128].astype(F32))
    return grad


def middle_kernel(direct, *refs):
    dqkv_any, dqkv, d_first_in, x_ref, w_last, ctx = refs[:6]
    unit1, hidden, unit2, scales, wo, wup, wdn, vec = refs[6:14]
    refs = refs[14:]
    if direct:
        outer, refs = refs[:4], refs[4:]
    d_first, dctx, dwqkv, dvec_last, dwo, dwup, dwdn, dvec = refs[:8]
    refs = refs[8:]
    if direct:
        summed, refs = refs[0], refs[1:]
    landed, cols, sums_last, sums, kept, out, send, recv, local = refs[:9]
    i, count = pl.program_id(0), pl.num_programs(0)
    block = x_ref.shape[1]
    core, peer = pair_of()
    d_copy = to_peer(dqkv_any.at[1], landed, send.at[0], recv.at[0], peer)
    if direct:
        reduction = Reduce(*refs[9:])

    def copy(step):
        ds = pl.ds(pl.multiple_of(step * block, block), block)
        return to_peer(out.at[:, ds], dctx.at[1, :, ds], send.at[1 + step], recv.at[1 + step], peer)

    def keep(step):
        ds = pl.ds(pl.multiple_of(step * block, block), block)
        return pltpu.make_async_copy(kept.at[:, ds], dctx.at[0, :, ds], local.at[step])

    @pl.when(i == 0)
    def _():
        if direct:
            greet_all()
        else:
            greet(peer)
        d_copy.start()
        if direct:
            reduction.fill(outer_shares(*outer))
            reduction.first()
        spread(vec.at[0], cols)
        for ref in (sums_last, sums, dwqkv, dwo, dwup, dwdn):
            ref[...] = jnp.zeros_like(ref)
        d_copy.wait()

    if direct:
        pl.when(i == 1)(reduction.second)
        pl.when(i == 2)(reduction.third)

    ds = pl.ds(pl.multiple_of(i * block, block), block)
    grad = input_block(
        core, dqkv[0], landed[:, ds], d_first_in[...], x_ref[...].astype(BF), 1, w_last, sums_last, dwqkv
    )
    saved = (unit1[...], scales[0:1], hidden[...], unit2[...], scales[1:2])
    d_first[...], d_context = backward_block(
        grad, ctx[...], saved, (wo[0], wup[0], wdn[0]), cols, sums, dwo, dwup, dwdn
    )
    low, high = d_context[:128], d_context[128:]
    out[:, ds] = jnp.where(core == 0, high, low)
    copy(i).start()
    kept[:, ds] = jnp.where(core == 0, low, high)
    keep(i).start()

    @pl.when(i == count - 1)
    def _():
        dvec_last[...] = place_vectors(sums_last)
        dvec[...] = place_vectors(sums)
        if direct:
            summed[...] = reduction.result()

        @pl.loop(0, count)
        def _(step):
            copy(step).wait()
            keep(step).wait()


def middle(direct, dqkv, d_first, x, wqkv, ctx, unit1, hidden, unit2, scales, wo, wup, wdn, vec, outer):
    length, block = x.shape[1], 512
    count = length // block
    outer = outer if direct else ()

    def layer(full, at):
        return pl.BlockSpec((1,) + full.shape[1:], lambda i: (at, 0, 0))

    def tokens(rows):
        return pl.BlockSpec((rows, block), lambda i: (0, i))

    shapes = ((768, 256), (256, 128)) + GRAD_SHAPES
    shapes += ((OUTER, 256),) if direct else ()
    return pl.pallas_call(
        functools.partial(middle_kernel, direct),
        name="back_between",
        grid=(count,),
        out_shape=(
            shape_of((256, length), F32),
            shape_of((2, 128, length), BF),
        )
        + tuple(shape_of(s, F32) for s in shapes),
        in_specs=[
            ANY_SPEC,
            pl.BlockSpec((1, 384, block), lambda i: (0, 0, i)),
            tokens(256),
            tokens(256),
            layer(wqkv, 1),
            tokens(256),
            tokens(256),
            tokens(512),
            tokens(256),
            tokens(8),
            layer(wo, 0),
            layer(wup, 0),
            layer(wdn, 0),
            layer(vec, 0),
        ]
        + [whole(a.shape) for a in outer],
        out_specs=[tokens(256), ANY_SPEC] + [whole(s) for s in shapes],
        scratch_shapes=[
            pltpu.VMEM((384, length), BF),
            pltpu.VMEM((2560, 128), F32),
            pltpu.VMEM((2560, 128), F32),
            pltpu.VMEM((2560, 128), F32),
            pltpu.VMEM((128, length), BF),
            pltpu.VMEM((128, length), BF),
            pltpu.SemaphoreType.DMA((count + 1,)),
            pltpu.SemaphoreType.DMA((count + 1,)),
            pltpu.SemaphoreType.DMA((count,)),
        ]
        + (reduce_scratch(OUTER) if direct else []),
        compiler_params=params(5),
    )(dqkv, dqkv, d_first, x, wqkv, ctx, unit1, hidden, unit2, scales, wo, wup, wdn, vec, *outer)


def last_kernel(direct, *refs):
    dqkv_any, dqkv, d_first_in, x_ref, w_ref = refs[:5]
    refs = refs[5:]
    if direct:
        inner, outer, refs = refs[:2], refs[2:6], refs[6:]
        grad_out, sums_one, sums_two, dwqkv, dvec = refs[:5]
        refs = refs[5:]
    else:
        grad_out, dwqkv, dvec = refs[:3]
        refs = refs[3:]
    landed, sums, send, recv = refs[:4]
    i, count = pl.program_id(0), pl.num_programs(0)
    block = x_ref.shape[1]
    core, peer = pair_of()
    d_copy = to_peer(dqkv_any.at[1], landed, send, recv, peer)
    if direct:
        one = Reduce(*refs[4 : 4 + REDUCE_REFS])
        two = Reduce(*refs[4 + REDUCE_REFS :])

    @pl.when(i == 0)
    def _():
        if direct:
            greet_all()
        else:
            greet(peer)
        d_copy.start()
        if direct:
            one.fill(inner_shares(*inner) + outer_shares(*outer))
            one.first()
        for ref in (sums, dwqkv):
            ref[...] = jnp.zeros_like(ref)
        d_copy.wait()

    if direct:
        pl.when(i == 1)(one.second)
        pl.when(i == 3)(one.third)

    ds = pl.ds(pl.multiple_of(i * block, block), block)
    grad = input_block(
        core, dqkv[0], landed[:, ds], d_first_in[...], x_ref[0], 0, w_ref, sums, dwqkv
    )
    grad_out[0] = jnp.transpose(grad)

    @pl.when(i == count - 1)
    def _():
        dvec[...] = place_vectors(sums)
        if direct:
            two.fill(inner_shares(dwqkv, dvec))
            two.first()
            two.second()
            sums_one[...] = one.result()
            two.third()
            sums_two[...] = two.result()


def last(direct, dqkv, d_first, cells, wqkv, inner, outer):
    length, block = cells.shape[1], 512
    count = length // block
    terms = tuple(inner) + tuple(outer) if direct else ()

    def tokens(rows):
        return pl.BlockSpec((rows, block), lambda i: (0, i))

    grads = ((768, 256), (256, 128))
    shapes = ((INNER + OUTER, 256), (INNER, 256)) if direct else grads
    by_cell = pl.BlockSpec((1, block, 256), lambda i: (0, i, 0))
    scratch = [pltpu.VMEM(s, F32) for s in grads] if direct else []
    scratch += [
        pltpu.VMEM((384, length), BF),
        pltpu.VMEM((2560, 128), F32),
        pltpu.SemaphoreType.DMA,
        pltpu.SemaphoreType.DMA,
    ]
    if direct:
        scratch += reduce_scratch(INNER + OUTER) + reduce_scratch(INNER)
    return pl.pallas_call(
        functools.partial(last_kernel, direct),
        name="back_input",
        grid=(count,),
        out_shape=(shape_of((1, length, 256), F32),) + tuple(shape_of(s, F32) for s in shapes),
        in_specs=[
            ANY_SPEC,
            pl.BlockSpec((1, 384, block), lambda i: (0, 0, i)),
            tokens(256),
            by_cell,
            pl.BlockSpec((1,) + wqkv.shape[1:], lambda i: (0, 0, 0)),
        ]
        + [whole(a.shape) for a in terms],
        out_specs=[by_cell] + [whole(s) for s in shapes],
        scratch_shapes=scratch,
        compiler_params=params(6),
    )(dqkv, dqkv, d_first, cells, wqkv, *terms)


def finish_kernel(factor, one, two, three, *refs):
    qw, qb, kw, vw, vb, ow, ob, g1, s1, uw, ub, dw, db, g2, s2 = refs
    layers = (
        (three[...] * factor, two[INNER:] * factor),
        (two[0:INNER] * factor, one[...] * factor),
    )
    for layer, (inner, outer) in enumerate(layers):
        qw[layer], kw[layer], vw[layer] = inner[0:8], inner[8:16], inner[16:24]
        ow[layer] = outer[0:8]
        dw[layer, :, 0:256], dw[layer, :, 256:512] = outer[8:16], outer[16:24]
        uw[layer] = outer[32:48]
        vec = inner[24:32] + outer[24:32]
        vec = jnp.transpose(vec[:, 0:128] + vec[:, 128:256])
        for i, ref in enumerate((qb, vb, ob, g1, s1, db, g2, s2)):
            ref[layer : layer + 1] = vec[i : i + 1]
        ub[layer : layer + 1, 0:8] = vec[8:9]
        ub[layer : layer + 1, 8:16] = vec[9:10]


def finish(factor, sums, like):
    found = pl.pallas_call(
        functools.partial(finish_kernel, factor),
        name="finish",
        out_shape=tuple(shape_of(a.shape, F32) for a in like),
        in_specs=[VMEM_SPEC] * 3,
        out_specs=[VMEM_SPEC] * len(like),
        compiler_params=params(),
    )(*sums)
    return [jnp.swapaxes(a, 1, 2) if a.ndim == 3 else a for a in found]


def gather_by_collectives(weights, vectors):
    def whole_of(w):
        return lax.all_gather(w, AXES, axis=1, tiled=True)

    qw, kw, vw, ow, uw, dw = (whole_of(w) for w in weights)
    columns = [lax.all_gather(v, AXES, axis=1, tiled=True).astype(F32) for v in vectors]
    up = columns.pop().reshape(2, 32, 2, 8)
    columns += [up[:, :, 0].reshape(2, 256), up[:, :, 1].reshape(2, 256)]
    vec = jnp.pad(jnp.stack(columns, axis=2), ((0, 0), (0, 0), (0, 118)))
    return jnp.concatenate([qw, kw, vw], axis=1), ow, uw, dw, vec


def sum_by_collectives(factor, layers):
    def share(x):
        return lax.psum_scatter(x, AXES, scatter_dimension=0, tiled=True) * factor

    found = []
    for dwqkv, dvec_qkv, dwo, dwup, dwdn, dvec in layers:
        vec = dvec_qkv + dvec
        qb, vb, ob, g1, s1, db, g2, s2 = (share(vec[:, i]) for i in range(8))
        up = jnp.stack([vec[:, 8].reshape(32, 8), vec[:, 9].reshape(32, 8)], axis=1)
        qw, kw, vw = (share(dwqkv[256 * i : 256 * i + 256]).T for i in range(3))
        ow, uw, dw = share(dwo).T, share(dwup).T, share(dwdn).T
        ub = share(up.reshape(512))
        found.append((qw, qb, kw, vw, vb, ow, ob, g1, s1, uw, ub, dw, db, g2, s2))
    return [jnp.stack(pair) for pair in zip(*found)]


def on_device(devices, direct, cells_in, lengths, cotangent, *weights):
    qw, qb, kw, vw, vb, ow, ob, g1, s1, uw, ub, dw, db, g2, s2 = weights
    matrices, vectors = (qw, kw, vw, ow, uw, dw), (qb, vb, ob, g1, s1, db, g2, s2, ub)
    turned = [jnp.swapaxes(w, 1, 2) for w in matrices]
    if direct:
        lens, qkv0, wqkv, wo, wup, wdn, vec = start(lengths, cells_in, turned, vectors)
    else:
        wqkv, wo, wup, wdn, vec = gather_by_collectives(turned, vectors)
        lens, qkv0 = project_first(lengths, cells_in, wqkv, vec)
    ctx_pair, ctx32_0, logs0 = attend(lens, qkv0)
    x1, ctx0, unit1, hidden, unit2, scales, qkv1 = between(
        ctx_pair, cells_in, wqkv, wo, wup, wdn, vec
    )
    ctx_pair, ctx32_1, logs1 = attend(lens, qkv1)
    cells_out, d_first, dctx, *outer1 = turn(
        lengths, ctx_pair, x1, cotangent, wo, wup, wdn, vec
    )
    dqkv = attend_back(lens, qkv1, dctx, ctx32_1, logs1)
    d_first, dctx, *found = middle(
        direct, dqkv, d_first, x1, wqkv, ctx0, unit1, hidden, unit2, scales, wo, wup, wdn, vec, outer1
    )
    inner1, outer0, rest = found[:2], found[2:6], found[6:]
    dqkv = attend_back(lens, qkv0, dctx, ctx32_0, logs0)
    grad_in, *found = last(direct, dqkv, d_first, cells_in, wqkv, inner1, outer0)
    factor = 1.0 / math.sqrt(devices * cells_in.shape[0] * cells_in.shape[1])
    if direct:
        like = [shape_of(a.shape[:1] + a.shape[:0:-1], F32) for a in weights]
        grads = finish(factor, (*rest, *found), like)
    else:
        grads = sum_by_collectives(factor, ((*found, *outer0), (*inner1, *outer1)))
    return (cells_out, grad_in, *grads)


def solution(mesh):
    devices = mesh.size
    direct = (mesh.shape["wide"], mesh.shape["narrow"]) == (8, 4)
    cell, vector, matrix = P(AXES, None, None), P(None, AXES), P(None, None, AXES)
    placed = (
        matrix, vector, matrix, matrix, vector, matrix, vector, vector, vector,
        matrix, vector, matrix, vector, vector, vector,
    )
    return jax.shard_map(
        functools.partial(on_device, devices, direct),
        mesh=mesh,
        in_specs=(cell, P(AXES), cell) + placed,
        out_specs=(cell, cell) + placed,
        check_vma=False,
    )
```

```python
import functools
import math

import jax
import jax.numpy as jnp
from jax import lax
from jax.experimental import pallas as pl
from jax.experimental.pallas import tpu as pltpu
from jax.sharding import PartitionSpec as P

HEAD = 64
NEG = -1000000000.0
EPS = 1e-06
AXES = ("wide", "narrow")
MESH = pl.DeviceIdType.MESH
BF = jnp.bfloat16
F32 = jnp.float32
EXT = 16
GUARD = 3600.0
KEY_SIZES = (384, 512, 640, 768, 1024, 1280, 1536, 2048)
ROWS = 64
VMEM_SPEC = pl.BlockSpec(memory_space=pltpu.VMEM)
SMEM_SPEC = pl.BlockSpec(memory_space=pltpu.SMEM)
QB, VB, OB, G1, S1, DB, G2, S2, UB = range(9)


def dot(a, b, ca, cb):
    return lax.dot_general(a, b, (((ca,), (cb,)), ((), ())), preferred_element_type=F32)


def params(collective_id=None, limit=16):
    if collective_id is None:
        return pltpu.CompilerParams(vmem_limit_bytes=limit << 20)
    return pltpu.CompilerParams(
        vmem_limit_bytes=limit << 20, collective_id=collective_id, has_side_effects=True
    )


def shape_of(shape, dtype):
    return jax.ShapeDtypeStruct(shape, dtype)


def pair_of():
    narrow = lax.axis_index("narrow")
    core = lax.rem(narrow, 2)
    return core, (lax.axis_index("wide"), narrow + 1 - 2 * core)


def greet(peer):
    barrier = pltpu.get_barrier_semaphore()
    pl.semaphore_signal(barrier, inc=1, device_id=peer, device_id_type=MESH)
    pl.semaphore_wait(barrier, 1)


def to_peer(src, dst, send, recv, peer):
    return pltpu.make_async_remote_copy(
        src_ref=src, dst_ref=dst, send_sem=send, recv_sem=recv, device_id=peer, device_id_type=MESH
    )


def half_rows(ref, layer, base, half):
    return ref[layer, pl.ds(pl.multiple_of(base + half * 128, 128), 128)]


def tile_lanes(column, count):
    return jnp.concatenate([column] * (count // 128), axis=1)


def spread(vec_ref, cols_ref):
    vec = vec_ref[...]
    width = vec.shape[0]
    for i in range(8):
        cols_ref[pl.ds(i * width, width)] = jnp.broadcast_to(vec[:, i : i + 1], (width, 128))
    low = jnp.broadcast_to(vec[:, 8:9], (width, 128)).reshape(width // 8, 8, 128)
    high = jnp.broadcast_to(vec[:, 9:10], (width, 128)).reshape(width // 8, 8, 128)
    cols_ref[pl.ds(8 * width, 2 * width)] = jnp.concatenate([low, high], axis=1).reshape(
        2 * width, 128
    )


def columns_kernel(vec, cols):
    for layer in range(2):
        spread(vec.at[layer], cols.at[layer])


def columns(vec):
    return pl.pallas_call(
        columns_kernel,
        name="columns",
        out_shape=shape_of((2, 2560, 128), F32),
        in_specs=[VMEM_SPEC],
        out_specs=VMEM_SPEC,
        compiler_params=params(),
    )(vec)


def column(cols_ref, i, count):
    rows = 512 if i == UB else 256
    return tile_lanes(cols_ref[pl.ds(i * 256, rows)], count)


def fold_lanes(x):
    total = x[:, :128]
    for start in range(128, x.shape[1], 128):
        total = total + x[:, start : start + 128]
    return total


def norm(resid):
    offset = resid - jnp.mean(resid, axis=0, keepdims=True)
    scale = lax.rsqrt(jnp.mean(offset * offset, axis=0, keepdims=True) + EPS)
    return offset * scale, scale


def norm_back(grad, gain, unit, scale):
    q = grad * gain
    return (
        q - jnp.mean(q, axis=0, keepdims=True) - unit * jnp.mean(q * unit, axis=0, keepdims=True)
    ) * scale


GELU_C = 0.7978845608028654
GELU_A = 0.044715


def gelu_tanh(u):
    return jnp.tanh(GELU_C * (u + GELU_A * (u * u * u)))


def project(xb, contract, w_ref, cols_ref, half, layer=0):
    parts = []
    for i in range(3):
        y = dot(half_rows(w_ref, layer, i * 256, half), xb, 1, contract)
        if i != 1:
            bias = cols_ref[
                pl.ds(pl.multiple_of((QB if i == 0 else VB) * 256 + half * 128, 128), 128)
            ]
            y = y + tile_lanes(bias, y.shape[1])
        y = y.astype(BF)
        parts.append(y * jnp.asarray(0.125, BF) if i == 0 else y)
    return jnp.concatenate(parts, axis=0)


def join(core, own, peer):
    return jnp.concatenate(
        [jnp.where(core == 0, own, peer), jnp.where(core == 0, peer, own)], axis=0
    )


def forward_block(context, x, wo, wup, wdn, cols_ref):
    count = x.shape[1]
    unit1, scale1 = norm(x + dot(wo, context, 1, 0) + column(cols_ref, OB, count))
    middle = unit1 * column(cols_ref, G1, count) + column(cols_ref, S1, count)
    hidden = dot(wup, middle.astype(BF), 1, 0) + column(cols_ref, UB, count)
    active = (0.5 * hidden * (1.0 + gelu_tanh(hidden))).astype(BF)
    unit2, scale2 = norm(middle + dot(wdn, active, 1, 0) + column(cols_ref, DB, count))
    x_next = unit2 * column(cols_ref, G2, count) + column(cols_ref, S2, count)
    return unit1, scale1, hidden, unit2, scale2, x_next


def backward_block(grad, context, saved, weights, cols_ref, sums, dwo, dwup, dwdn):
    unit1, scale1, hidden, unit2, scale2 = saved
    wo, wup, wdn = weights
    count = grad.shape[1]

    def add(i, x):
        rows = x.shape[0]
        sums[pl.ds(i * 256, rows)] += fold_lanes(x)

    add(S2, grad)
    add(G2, grad * unit2)
    d_second = norm_back(grad, column(cols_ref, G2, count), unit2, scale2)
    branch = d_second.astype(BF)
    add(DB, branch.astype(F32))
    t = gelu_tanh(hidden)
    active = (0.5 * hidden * (1.0 + t)).astype(BF)
    slope = 0.5 * (1.0 + t) + (0.5 * GELU_C) * hidden * (1.0 - t * t) * (
        1.0 + (3.0 * GELU_A) * (hidden * hidden)
    )
    dwdn[...] += dot(branch, active, 1, 1)
    d_hidden = (dot(wdn, branch, 0, 0) * slope).astype(BF)
    add(UB, d_hidden.astype(F32))
    middle = unit1 * column(cols_ref, G1, count) + column(cols_ref, S1, count)
    dwup[...] += dot(d_hidden, middle.astype(BF), 1, 1)
    d_middle = d_second + dot(wup, d_hidden, 0, 0)
    add(S1, d_middle)
    add(G1, d_middle * unit1)
    d_first = norm_back(d_middle, column(cols_ref, G1, count), unit1, scale1)
    attn = d_first.astype(BF)
    add(OB, attn.astype(F32))
    dwo[...] += dot(attn, context, 1, 1)
    return d_first, dot(wo, attn, 0, 0).astype(BF)


def place_vectors(sums):
    lane = lax.broadcasted_iota(jnp.int32, (256, 128), 1)
    out = jnp.zeros((256, 128), F32)
    for i in range(8):
        total = jnp.sum(sums[pl.ds(i * 256, 256)], axis=1, keepdims=True)
        out = jnp.where(lane == i, total, out)
    up = jnp.sum(sums[pl.ds(2048, 512)], axis=1, keepdims=True)
    up = jnp.broadcast_to(up, (512, 128)).reshape(32, 16, 128)
    out = jnp.where(lane == 8, up[:, :8].reshape(256, 128), out)
    return jnp.where(lane == 9, up[:, 8:].reshape(256, 128), out)


def coordinates():
    wide, narrow = lax.axis_index("wide"), lax.axis_index("narrow")
    return wide // 2, lax.rem(wide, 2), narrow // 2, lax.rem(narrow, 2)


def device_at(z, x, y, core):
    return (2 * z + x, 2 * y + core)


def plane_mates():
    z, x, y, core = coordinates()
    return [
        (device_at(z, a, b, core), 2 * a + b) for a, b in ((x, 1 - y), (1 - x, y), (1 - x, 1 - y))
    ]


def line_mates():
    z, x, y, core = coordinates()
    there = [lax.rem(z + j, 4) for j in (1, 2, 3)]
    return [(device_at(a, x, y, core), a) for a in there]


def sibling():
    z, x, y, core = coordinates()
    return device_at(z, x, y, 1 - core)


def greet_all():
    barrier = pltpu.get_barrier_semaphore()
    z, x, y, core = coordinates()
    mates = [sibling()] + [d for d, _ in plane_mates()] + [d for d, _ in line_mates()]
    mates += [device_at(there, x, y, 1 - core) for _, there in line_mates()]
    for mate in mates:
        pl.semaphore_signal(barrier, inc=1, device_id=mate, device_id_type=MESH)
    pl.semaphore_wait(barrier, len(mates))


FIRST, REST, END = 48, 64, 32


SHARE = 80


def share_kernel(length, qw, kw, vw, ow, uw, dw, *refs):
    vectors, (share, end) = refs[:-2], refs[-2:]
    end[0:16] = uw[1]
    end[16:24] = dw[1, :, 0:256]
    end[24:32] = dw[1, :, 256:512]
    for layer in range(2):
        for i, w in enumerate((qw, kw, vw, ow)):
            share[layer, 8 * i : 8 * i + 8] = w[layer]
        share[layer, 32:48] = uw[layer]
        share[layer, 48:56] = dw[layer, :, 0:256]
        share[layer, 56:64] = dw[layer, :, 256:512]
        share[layer, 64:80] = jnp.zeros((16, 256), BF)
        at = 0
        for v in vectors:
            share[layer, 64:65, at : at + v.shape[1]] = v[layer : layer + 1]
            at += v.shape[1]
        share[layer, 64:65, at : at + 1] = (length[...] // 256).astype(F32).astype(BF)
        share[layer, 64:65, at + 1 : at + 2] = (length[...] % 256).astype(F32).astype(BF)


def own_share(lengths, weights, vectors):
    return pl.pallas_call(
        share_kernel,
        name="own_share",
        out_shape=(shape_of((2, SHARE, 256), BF), shape_of((END, 256), BF)),
        in_specs=[VMEM_SPEC] * 16,
        out_specs=[VMEM_SPEC] * 2,
        compiler_params=params(limit=60),
    )(lengths[:, None], *weights, *vectors)


def pack_own(share, first, rest, flat):
    flat[...] = jnp.zeros_like(flat)
    for layer in range(2):
        row = share[layer, 64:80].astype(F32)[0:1]
        for i in range(10):
            at = 2 * i + layer
            flat[at : at + 1, 0:8] = row[:, 8 * i : 8 * i + 8]
    columns = jnp.transpose(flat[...])[0:8]
    block = jnp.concatenate([columns, jnp.zeros_like(columns)], axis=1)
    first[0:32] = share[0, 0:32]
    first[32:48] = jnp.concatenate([block, jnp.zeros_like(block)], axis=0).astype(BF)
    rest[0:32] = share[0, 32:64]
    rest[32:64] = share[1, 0:32]


def ordered(landed, at, rows):
    pieces = [
        landed[core, plane, z, at : at + rows]
        for z in range(4)
        for plane in range(4)
        for core in range(2)
    ]
    return jnp.stack(pieces)


def two_matrices(landed, at):
    pair = ordered(landed, at, 16).astype(F32)
    return (
        pair[:, :8].reshape(256, 256).astype(BF),
        pair[:, 8:].reshape(256, 256).astype(BF),
    )


def unpack_first(landed, wqkv, wo, vec):
    wqkv[0, 0:256], wqkv[0, 256:512] = two_matrices(landed, 0)
    wqkv[0, 512:768], wo[0] = two_matrices(landed, 16)
    both = ordered(landed, 32, 16).astype(F32)[:, :8, :128].reshape(256, 128)
    lane = lax.broadcasted_iota(jnp.int32, (256, 128), 1)
    for layer in range(2):
        out = jnp.zeros((256, 128), F32)
        for i in range(10):
            out = jnp.where(lane == i, both[:, 2 * i + layer : 2 * i + layer + 1], out)
        vec[layer] = out


def unpack_feed_forward(landed, at, up, down):
    up[...] = ordered(landed, at, 16).reshape(512, 256)
    down[:, 0:256], down[:, 256:512] = two_matrices(landed, at + 16)


def unpack_rest(landed, wqkv, wo, up, down):
    unpack_feed_forward(landed, 0, up, down)
    wqkv[1, 0:256], wqkv[1, 256:512] = two_matrices(landed, 32)
    wqkv[1, 512:768], wo[1] = two_matrices(landed, 48)


class Gather:
    def __init__(self, own, landed, send, recv, part):
        z, x, y, core = coordinates()
        plane = 2 * x + y

        def copy(src, dst, i, device):
            return pltpu.make_async_remote_copy(
                src_ref=src,
                dst_ref=dst,
                send_sem=send.at[part, i],
                recv_sem=recv.at[part, i],
                device_id=device,
                device_id_type=MESH,
            )

        def column(i):
            return landed.at[core, i]

        self.keep = lambda: landed.at[core, plane, z].__setitem__(Ellipsis, own[...])
        self.line = [
            copy(own, landed.at[core, plane, z], i, device)
            for i, (device, _) in enumerate(line_mates())
        ]
        self.plane = [
            copy(column(plane), column(plane), 3 + i, device)
            for i, (device, _) in enumerate(plane_mates())
        ]
        columns = [plane] + [number for _, number in plane_mates()]
        self.cores = [
            copy(column(number), column(number), 6 + i, sibling())
            for i, number in enumerate(columns)
        ]


def start_kernel(
    share, x_ref,
    lens, qkv, wqkv, wo, wup, wdn, cols, xs,
    first, rest, flat, landed_first, landed_rest, vec, out, own_len, send, recv, pair_send, pair_recv, x_sems,
):
    core, peer = pair_of()
    pack_own(share, first, rest, flat)
    a = Gather(first, landed_first, send, recv, 0)
    b = Gather(rest, landed_rest, send, recv, 1)
    greet_all()
    for c in a.line + b.line:
        c.start()
    number = share[0, 64:80].astype(F32)[0:1]
    number = number[:, 80:81] * 256.0 + number[:, 81:82]
    own_len[...] = jnp.broadcast_to(number, own_len.shape).astype(jnp.int32)
    len_copy = to_peer(own_len, lens.at[1], pair_send.at[0], pair_recv.at[0], peer)
    len_copy.start()
    lens[0] = own_len[...]
    x_copy = to_peer(x_ref.at[0], xs.at[1], x_sems.at[0], x_sems.at[1], peer)
    x_copy.start()
    a.keep()
    b.keep()
    xs[0] = x_ref[0]
    for part in (a, b):
        for c in part.line:
            c.wait()
        for c in part.plane + part.cores[:1]:
            c.start()
    for i in range(3):
        a.plane[i].wait()
        a.cores[1 + i].start()
    for c in a.cores:
        c.wait()
    unpack_first(landed_first, wqkv, wo, vec)
    spread(vec.at[0], cols.at[0])
    block = 1024
    count = x_ref.shape[1] // block

    def copy(i):
        ds = pl.ds(pl.multiple_of(i * block, block), block)
        return to_peer(
            out.at[:, ds], qkv.at[1, :, ds], pair_send.at[1 + i], pair_recv.at[1 + i], peer
        )

    @pl.loop(0, count)
    def _(i):
        ds = pl.ds(pl.multiple_of(i * block, block), block)
        out[:, ds] = project(x_ref[0, ds], 1, wqkv, cols.at[0], 1 - core)
        copy(i).start()

    for i in range(3):
        b.plane[i].wait()
        b.cores[1 + i].start()

    @pl.loop(0, count)
    def _(i):
        ds = pl.ds(pl.multiple_of(i * block, block), block)
        qkv[0, :, ds] = project(x_ref[0, ds], 1, wqkv, cols.at[0], core)

    spread(vec.at[1], cols.at[1])
    for c in b.cores:
        c.wait()
    unpack_rest(landed_rest, wqkv, wo, wup, wdn)
    len_copy.wait()
    x_copy.wait()

    @pl.loop(0, count)
    def _(i):
        copy(i).wait()


def start(share, cells):
    length = cells.shape[1]
    count = length // 1024
    return pl.pallas_call(
        start_kernel,
        name="gather_and_project",
        out_shape=(
            shape_of((2, 8, 128), jnp.int32),
            shape_of((2, 384, length), BF),
            shape_of((2, 768, 256), BF),
            shape_of((2, 256, 256), BF),
            shape_of((512, 256), BF),
            shape_of((256, 512), BF),
            shape_of((2, 2560, 128), F32),
            shape_of((2, length, 256), BF),
        ),
        in_specs=[VMEM_SPEC] * 2,
        out_specs=[VMEM_SPEC] * 8,
        scratch_shapes=[
            pltpu.VMEM((FIRST, 256), BF),
            pltpu.VMEM((REST, 256), BF),
            pltpu.VMEM((128, 128), F32),
            pltpu.VMEM((2, 4, 4, FIRST, 256), BF),
            pltpu.VMEM((2, 4, 4, REST, 256), BF),
            pltpu.VMEM((2, 256, 128), F32),
            pltpu.VMEM((384, length), BF),
            pltpu.VMEM((8, 128), jnp.int32),
            pltpu.SemaphoreType.DMA((2, 10)),
            pltpu.SemaphoreType.DMA((2, 10)),
            pltpu.SemaphoreType.DMA((count + 1,)),
            pltpu.SemaphoreType.DMA((count + 1,)),
            pltpu.SemaphoreType.DMA((2,)),
        ],
        compiler_params=params(1),
    )(share, cells)


def project_kernel(len_ref, x_ref, w_ref, cols_ref, lens, qkv, xs, out, own_len, send, recv):
    core, peer = pair_of()
    cols = cols_ref.at[0]
    own_len[...] = jnp.full(own_len.shape, len_ref[0], jnp.int32)
    greet(peer)
    len_copy = to_peer(own_len, lens.at[1], send.at[0], recv.at[0], peer)
    len_copy.start()
    lens[0] = own_len[...]
    x_copy = to_peer(x_ref.at[0], xs.at[1], send.at[2], recv.at[2], peer)
    x_copy.start()
    xs[0] = x_ref[0]
    out[...] = project(x_ref[0], 1, w_ref, cols, 1 - core)
    qkv_copy = to_peer(out, qkv.at[1], send.at[1], recv.at[1], peer)
    qkv_copy.start()
    qkv[0] = project(x_ref[0], 1, w_ref, cols, core)
    len_copy.wait()
    qkv_copy.wait()
    x_copy.wait()


def project_first(lengths, cells, wqkv, cols):
    length = cells.shape[1]
    return pl.pallas_call(
        project_kernel,
        name="project_first",
        out_shape=(
            shape_of((2, 8, 128), jnp.int32),
            shape_of((2, 384, length), BF),
            shape_of((2, length, 256), BF),
        ),
        in_specs=[SMEM_SPEC] + [VMEM_SPEC] * 3,
        out_specs=[VMEM_SPEC] * 3,
        scratch_shapes=[
            pltpu.VMEM((384, length), BF),
            pltpu.VMEM((8, 128), jnp.int32),
            pltpu.SemaphoreType.DMA((3,)),
            pltpu.SemaphoreType.DMA((3,)),
        ],
        compiler_params=params(2),
    )(lengths, cells, wqkv, cols)


def key_sizes(length):
    return [size for size in KEY_SIZES if size < length] + [length]


def extended(x, extra):
    return jnp.concatenate([x, extra], axis=0)


def one_head(x, head):
    row = lax.broadcasted_iota(jnp.int32, x.shape, 0)
    return jnp.where((row // HEAD) == head, x, jnp.zeros_like(x))


def attend_kernel(lens, qkv, ctx, ctx32, logs, kx, scores, total, acc):
    length = qkv.shape[2]

    def query_of(cell, i, head, wide):
        q = qkv[cell, 0:128, pl.ds(pl.multiple_of(i * wide, wide), wide)]
        row = lax.broadcasted_iota(jnp.int32, (EXT, wide), 0)
        return extended(one_head(q, head), jnp.where(row == 0, 1.0, 0.0).astype(BF))

    def finish(cell, i, head, wide, high, sums, out):
        ds = pl.ds(pl.multiple_of(i * wide, wide), wide)
        sums = jnp.sum(sums, axis=0, keepdims=True)
        out = out * (1.0 / sums)
        rows = slice(HEAD * head, HEAD * head + HEAD)
        ctx[cell, rows, ds] = out.astype(BF)
        ctx32[cell, rows, ds] = out
        logs[cell, head : head + 1, ds] = jnp.log(sums) + high

    def largest(x):
        x = x.astype(F32)
        square = x * x
        return [
            jnp.max(jnp.sum(square[HEAD * h : HEAD * h + HEAD], axis=0, keepdims=True))
            for h in range(2)
        ]

    @pl.loop(0, 2)
    def _(cell):
        valid = lens[cell, 0, 0]
        q_most = largest(qkv[cell, 0:128])
        k_most = largest(qkv[cell, 128:256])
        plain = jnp.maximum(q_most[0] * k_most[0], q_most[1] * k_most[1]) <= GUARD

        @pl.loop(0, jnp.minimum(pl.cdiv(valid, 256) + 1, length // 256))
        def _(i):
            ds = pl.ds(pl.multiple_of(i * 256, 256), 256)
            where = lax.broadcasted_iota(jnp.int32, (EXT, 256), 1) + i * 256
            first = lax.broadcasted_iota(jnp.int32, (EXT, 256), 0) == 0
            extra = jnp.where(first & (where >= valid), NEG, 0.0).astype(BF)
            kx[ds] = jnp.transpose(extended(qkv[cell, 128:256, ds], extra))

        sizes = key_sizes(length)
        for low, size in zip([0] + sizes[:-1], sizes):
            wide = next(w for w in (2048, 1024, 512) if w * size <= 1024 * 1024 or w == 512)
            wide = min(wide, length)

            @pl.when(plain & (valid > low) & (valid <= size))
            def _(size=size, wide=wide):
                @pl.loop(0, length // wide)
                def _(i):
                    for head in range(2):
                        s = dot(kx[0:size], query_of(cell, i, head, wide), 1, 0)
                        e = jnp.exp(s)
                        sums = jnp.sum(e.reshape(size // 8, 8, wide), axis=0)
                        v = qkv[cell, 256 + HEAD * head : 320 + HEAD * head, 0:size]
                        finish(cell, i, head, wide, 0.0, sums, dot(v, e.astype(BF), 1, 0))

        @pl.when(jnp.logical_not(plain))
        def _():
            chunks = pl.cdiv(valid, 256)
            wide = 512

            @pl.loop(0, length // wide)
            def _(i):
                for head in range(2):
                    query = query_of(cell, i, head, wide)

                    def score(j, high):
                        s = dot(kx[pl.ds(pl.multiple_of(j * 256, 256), 256)], query, 1, 0)
                        scores[j] = s
                        return jnp.maximum(high, jnp.max(s.reshape(32, 8, wide), axis=0))

                    high = lax.fori_loop(0, chunks, score, jnp.full((8, wide), NEG * 2, F32))
                    high = jnp.max(high, axis=0, keepdims=True)
                    acc[...] = jnp.zeros_like(acc)
                    total[...] = jnp.zeros_like(total)

                    @pl.loop(0, chunks)
                    def _(j):
                        e = jnp.exp(scores[j] - high)
                        total[...] += jnp.sum(e.reshape(32, 8, wide), axis=0)
                        v = qkv[
                            cell,
                            256 + HEAD * head : 320 + HEAD * head,
                            pl.ds(pl.multiple_of(j * 256, 256), 256),
                        ]
                        acc[...] += dot(v, e.astype(BF), 1, 0)

                    finish(cell, i, head, wide, high, total[...], acc[...])


def attend(lens, qkv):
    length = qkv.shape[2]
    return pl.pallas_call(
        attend_kernel,
        name="attend",
        out_shape=(
            shape_of((2, 128, length), BF),
            shape_of((2, 128, length), F32),
            shape_of((2, 2, length), F32),
        ),
        in_specs=[SMEM_SPEC, VMEM_SPEC],
        out_specs=[VMEM_SPEC] * 3,
        scratch_shapes=[
            pltpu.VMEM((length, 128 + EXT), BF),
            pltpu.VMEM((length // 256, 256, 512), F32),
            pltpu.VMEM((8, 512), F32),
            pltpu.VMEM((HEAD, 512), F32),
        ],
        compiler_params=params(),
    )(lens, qkv)


def in_three(x):
    high = x.astype(BF)
    rest = x - high.astype(F32)
    middle = rest.astype(BF)
    return high, middle, (rest - middle.astype(F32)).astype(BF)


def attend_back_kernel(
    lens, qkv, grad, ctx32, logs, xs, out, dwqkv, dvec, right_s, right_d, sum_k, sum_v, sums
):
    length = qkv.shape[2]
    wide = 512
    row = lax.broadcasted_iota(jnp.int32, (EXT, wide), 0)

    def left(x, head, value, last):
        a, b, c = in_three(value)
        zero = jnp.zeros((EXT, wide), BF)
        extra = jnp.where(row == 0, a, jnp.where(row == 1, b, jnp.where(row == 2, c, zero)))
        if last:
            extra = jnp.where(row == 3, jnp.ones_like(zero), extra)
        return jnp.transpose(extended(one_head(x, head), extra))

    dwqkv[...] = jnp.zeros_like(dwqkv)
    sums[...] = jnp.zeros_like(sums)

    @pl.loop(0, 2)
    def _(cell):
        valid = lens[cell, 0, 0]
        out[cell] = jnp.zeros_like(out[cell])
        sizes = key_sizes(length)
        for low, size in zip([0] + sizes[:-1], sizes):

            @pl.when((valid > low) & (valid <= size))
            def _(size=size):
                where = lax.broadcasted_iota(jnp.int32, (EXT, size), 1)
                rows = lax.broadcasted_iota(jnp.int32, (EXT, size), 0)
                extra = jnp.where(
                    rows < 3, 1.0, jnp.where((rows == 3) & (where >= valid), NEG, 0.0)
                ).astype(BF)
                right_s[0:128, 0:size] = qkv[cell, 128:256, 0:size]
                right_s[128:, 0:size] = extra
                right_d[0:128, 0:size] = qkv[cell, 256:384, 0:size]
                right_d[128:, 0:size] = extra
                sum_k[:, 0:size] = jnp.zeros((128, size), F32)
                sum_v[:, 0:size] = jnp.zeros((128, size), F32)

                @pl.loop(0, pl.cdiv(valid, wide))
                def _(i):
                    ds = pl.ds(pl.multiple_of(i * wide, wide), wide)
                    q = qkv[cell, 0:128, ds]
                    d = grad[cell, :, ds]
                    inner = d.astype(F32) * ctx32[cell, :, ds]
                    for head in range(2):
                        at = slice(HEAD * head, HEAD * head + HEAD)
                        delta = jnp.sum(inner[at], axis=0, keepdims=True)
                        s = dot(
                            left(q, head, -logs[cell, head : head + 1, ds], True),
                            right_s[:, 0:size],
                            1,
                            0,
                        )
                        p = jnp.exp(s)
                        dp = dot(left(d, head, -delta, False), right_d[:, 0:size], 1, 0)
                        ds_low = (p * dp).astype(BF)
                        sum_v[at, 0:size] += dot(d[at], p.astype(BF), 1, 0)
                        sum_k[at, 0:size] += dot(q[at], ds_low, 1, 0)
                        dq = dot(qkv[cell, 128 + HEAD * head : 192 + HEAD * head, 0:size], ds_low, 1, 1)
                        out[cell, at, ds] = (dq * 0.125).astype(BF)

                out[cell, 128:256, 0:size] = sum_k[:, 0:size].astype(BF)
                out[cell, 256:384, 0:size] = sum_v[:, 0:size].astype(BF)
                part = out[cell, :, 0:size]
                dwqkv[...] += dot(part, xs[cell, 0:size], 1, 0)
                sums[0:128] += fold_lanes(part[0:128].astype(F32))
                sums[128:256] += fold_lanes(part[256:384].astype(F32))

    lane = lax.broadcasted_iota(jnp.int32, (128, 128), 1)
    q_sum = jnp.sum(sums[0:128], axis=1, keepdims=True)
    v_sum = jnp.sum(sums[128:256], axis=1, keepdims=True)
    dvec[...] = jnp.where(lane == QB, q_sum, jnp.where(lane == VB, v_sum, 0.0))


def attend_back(lens, qkv, grad, ctx32, logs, xs):
    length = qkv.shape[2]
    return pl.pallas_call(
        attend_back_kernel,
        name="attend_back",
        out_shape=(
            shape_of((2, 384, length), BF),
            shape_of((384, 256), F32),
            shape_of((128, 128), F32),
        ),
        in_specs=[SMEM_SPEC] + [VMEM_SPEC] * 5,
        out_specs=[VMEM_SPEC] * 3,
        scratch_shapes=[
            pltpu.VMEM((128 + EXT, length), BF),
            pltpu.VMEM((128 + EXT, length), BF),
            pltpu.VMEM((128, length), F32),
            pltpu.VMEM((128, length), F32),
            pltpu.VMEM((256, 128), F32),
        ],
        compiler_params=params(),
    )(lens, qkv, grad, ctx32, logs, xs)


BLOCK = 1024


def block_of(i):
    return pl.ds(pl.multiple_of(i * BLOCK, BLOCK), BLOCK)


def pair_semaphores(count):
    return [pltpu.SemaphoreType.DMA((count + 1,)), pltpu.SemaphoreType.DMA((count + 1,))]


def between_kernel(direct, *refs):
    ctx, x_ref, wqkv, wo, wup, wdn, cols_ref = refs[:7]
    refs = refs[7:]
    if direct:
        end, refs = refs[0], refs[1:]
    x_out, ctx_out, unit1, hidden, unit2, scales, qkv, lows = refs[:8]
    refs = refs[8:]
    if direct:
        landed_end, refs = refs[0], refs[1:]
    landed, out, send, recv = refs[:4]
    cols, cols_next = cols_ref.at[0], cols_ref.at[1]
    count = x_out.shape[1] // BLOCK
    core, peer = pair_of()
    ctx_copy = to_peer(ctx.at[1], landed, send.at[2 * count], recv.at[2 * count], peer)
    if direct:
        part = Gather(end, landed_end, *refs[4:], 0)

    def copies(i):
        ds, j = block_of(i), count + i
        return (
            to_peer(out.at[:, ds], qkv.at[1, :, ds], send.at[i], recv.at[i], peer),
            to_peer(lows.at[0, ds], lows.at[1, ds], send.at[j], recv.at[j], peer),
        )

    if direct:
        greet_all()
    else:
        greet(peer)
    ctx_copy.start()
    if direct:
        for c in part.line:
            c.start()
        part.keep()
    ctx_copy.wait()

    @pl.loop(0, count)
    def _(i):
        ds = block_of(i)
        context = join(core, ctx[0, :, ds], landed[:, ds])
        ctx_out[:, ds] = context
        x = jnp.transpose(x_ref[0, ds].astype(F32))
        one, scale1, hid, two, scale2, x_next = forward_block(
            context, x, wo[0], wup[...], wdn[...], cols
        )
        unit1[:, ds], hidden[:, ds], unit2[:, ds] = one, hid, two
        scales[0:1, ds], scales[1:2, ds] = scale1, scale2
        x_out[:, ds] = x_next
        low = x_next.astype(BF)
        lows[0, ds] = jnp.transpose(low)
        if direct:

            @pl.when(i == 0)
            def _():
                for c in part.line:
                    c.wait()
                for c in part.plane + part.cores[:1]:
                    c.start()

            @pl.when(i == 1)
            def _():
                for j in range(3):
                    part.plane[j].wait()
                    part.cores[1 + j].start()

        out[:, ds] = project(low, 0, wqkv, cols_next, 1 - core, 1)
        for c in copies(i):
            c.start()
        qkv[0, :, ds] = project(low, 0, wqkv, cols_next, core, 1)

    if direct:
        for c in part.cores:
            c.wait()

    @pl.loop(0, count)
    def _(i):
        for c in copies(i):
            c.wait()


def between(direct, ctx, cells, wqkv, wo, wup, wdn, cols, end):
    length = ctx.shape[2]
    shapes = (
        shape_of((256, length), F32),
        shape_of((256, length), BF),
        shape_of((256, length), F32),
        shape_of((512, length), F32),
        shape_of((256, length), F32),
        shape_of((8, length), F32),
        shape_of((2, 384, length), BF),
        shape_of((2, length, 256), BF),
    )
    scratch = [
        pltpu.VMEM((128, length), BF),
        pltpu.VMEM((384, length), BF),
    ] + pair_semaphores(2 * length // BLOCK)
    if direct:
        shapes += (shape_of((2, 4, 4, END, 256), BF),)
        scratch += [pltpu.SemaphoreType.DMA((1, 10)), pltpu.SemaphoreType.DMA((1, 10))]
    extra = (end,) if direct else ()
    return pl.pallas_call(
        functools.partial(between_kernel, direct),
        name="between_layers",
        out_shape=shapes,
        in_specs=[VMEM_SPEC] * (7 + len(extra)),
        out_specs=[VMEM_SPEC] * len(shapes),
        scratch_shapes=scratch,
        compiler_params=params(3),
    )(ctx, cells, wqkv, wo, wup, wdn, cols, *extra)


def turn_kernel(direct, lens, ctx, x_ref, cot, wo, cols_ref, *refs):
    if direct:
        end, refs = refs[0], refs[1:]
    else:
        (wup, wdn), refs = refs[:2], refs[2:]
    cells_out, d_first, dctx, dwo, dwup, dwdn, dvec = refs[:7]
    landed, sums, out, send, recv = refs[7:12]
    if direct:
        wup, wdn = refs[12:]
    cols = cols_ref.at[1]
    count = x_ref.shape[1] // BLOCK
    core, peer = pair_of()
    ctx_copy = to_peer(ctx.at[1], landed, send.at[count], recv.at[count], peer)

    def copy(i):
        ds = block_of(i)
        return to_peer(out.at[:, ds], dctx.at[1, :, ds], send.at[i], recv.at[i], peer)

    greet(peer)
    ctx_copy.start()
    for ref in (sums, dwo, dwup, dwdn):
        ref[...] = jnp.zeros_like(ref)
    if direct:
        unpack_feed_forward(end, 0, wup, wdn)
    ctx_copy.wait()

    @pl.loop(0, count)
    def _(i):
        ds = block_of(i)
        context = join(core, ctx[0, :, ds], landed[:, ds])
        weights = (wo[1], wup[...], wdn[...])
        *saved, x_next = forward_block(context, x_ref[:, ds], *weights, cols)
        cells_out[0, ds] = jnp.transpose(x_next).astype(BF)
        where = lax.broadcasted_iota(jnp.int32, (1, BLOCK), 1) + i * BLOCK
        valid = jnp.where(where < tile_lanes(lens[0, 0:1], BLOCK), 1.0, 0.0)
        grad = jnp.transpose(cot[0, ds].astype(F32)) * valid
        d_first[:, ds], d_context = backward_block(
            grad, context, saved, weights, cols, sums, dwo, dwup, dwdn
        )
        low, high = d_context[:128], d_context[128:]
        out[:, ds] = jnp.where(core == 0, high, low)
        copy(i).start()
        dctx[0, :, ds] = jnp.where(core == 0, low, high)

    dvec[...] = place_vectors(sums)

    @pl.loop(0, count)
    def _(i):
        copy(i).wait()


GRAD_SHAPES = ((256, 256), (512, 256), (256, 512), (256, 128))


def turn(direct, lens, ctx, x, cot, wo, cols, feed_forward):
    length = ctx.shape[2]
    shapes = (
        shape_of((1, length, 256), BF),
        shape_of((256, length), F32),
        shape_of((2, 128, length), BF),
    ) + tuple(shape_of(s, F32) for s in GRAD_SHAPES)
    return pl.pallas_call(
        functools.partial(turn_kernel, direct),
        name="turn",
        out_shape=shapes,
        in_specs=[VMEM_SPEC] * (6 + len(feed_forward)),
        out_specs=[VMEM_SPEC] * len(shapes),
        scratch_shapes=[
            pltpu.VMEM((128, length), BF),
            pltpu.VMEM((2560, 128), F32),
            pltpu.VMEM((128, length), BF),
        ]
        + pair_semaphores(length // BLOCK)
        + ([pltpu.VMEM((512, 256), BF), pltpu.VMEM((256, 512), BF)] if direct else []),
        compiler_params=params(4),
    )(lens, ctx, x, cot, wo, cols, *feed_forward)


OUTER, INNER = 48, 32


def shares(x):
    return x.reshape(32, x.shape[0] // 32, 256)


def vector_shares(vec):
    high = vec.astype(BF).astype(F32)
    return shares(jnp.concatenate([high, vec - high], axis=1))


def outer_shares(dwo, dwup, dwdn, dvec):
    return [
        shares(dwo[...]),
        shares(dwdn[:, 0:256]),
        shares(dwdn[:, 256:512]),
        vector_shares(dvec[...]),
        shares(dwup[...]),
    ]


def reduce_scratch(rows):
    return [
        pltpu.VMEM((2, 4, 4, rows, 256), BF),
        pltpu.VMEM((4, 4, rows, 256), BF),
        pltpu.VMEM((4, 4, rows, 256), BF),
        pltpu.VMEM((3, 4, rows, 256), BF),
        pltpu.VMEM((4, rows, 256), BF),
        pltpu.VMEM((3, rows, 256), BF),
        pltpu.SemaphoreType.DMA((7,)),
        pltpu.SemaphoreType.DMA((7,)),
    ]


REDUCE_REFS = 8


class Reduce:
    def __init__(self, own, from_core, by_plane, from_plane, by_line, from_line, send, recv):
        self.refs = own, from_core, by_plane, from_plane, by_line, from_line
        z, x, y, core = coordinates()
        self.z, self.number, self.core = z, 2 * x + y, core

        def copy(src, dst, i, device):
            return pltpu.make_async_remote_copy(
                src_ref=src,
                dst_ref=dst,
                send_sem=send.at[i],
                recv_sem=recv.at[i],
                device_id=device,
                device_id_type=MESH,
            )

        self.cores = [copy(own.at[1 - core], from_core, 0, sibling())]
        self.plane = [
            copy(by_plane.at[number], from_plane.at[i], 1 + i, device)
            for i, (device, number) in enumerate(plane_mates())
        ]
        self.line = [
            copy(by_line.at[there], from_line.at[i], 4 + i, device)
            for i, (device, there) in enumerate(line_mates())
        ]

    def fill(self, pieces):
        own = self.refs[0]
        rows = own.shape[3]
        terms = jnp.concatenate(pieces, axis=1).astype(BF).reshape(4, 4, 2, rows, 256)
        for core in range(2):
            for plane in range(4):
                own[core, plane] = terms[:, plane, core]

    def first(self):
        for c in self.cores:
            c.start()

    def second(self):
        own, from_core, by_plane = self.refs[:3]
        for c in self.cores:
            c.wait()
        by_plane[...] = (own[self.core].astype(F32) + from_core[...].astype(F32)).astype(BF)
        for c in self.plane:
            c.start()

    def third(self):
        by_plane, from_plane, by_line = self.refs[2:5]
        for c in self.plane:
            c.wait()
        total = by_plane[self.number].astype(F32)
        for i in range(3):
            total = total + from_plane[i].astype(F32)
        by_line[...] = total.astype(BF)
        for c in self.line:
            c.start()

    def result(self):
        by_line, from_line = self.refs[4:6]
        for c in self.line:
            c.wait()
        total = by_line[self.z].astype(F32)
        for i in range(3):
            total = total + from_line[i].astype(F32)
        return total


def reduce_half_scratch(rows):
    return [
        pltpu.VMEM((4, 4, rows, 256), BF),
        pltpu.VMEM((3, 4, rows, 256), BF),
        pltpu.VMEM((4, rows, 256), BF),
        pltpu.VMEM((4, rows, 256), BF),
        pltpu.SemaphoreType.DMA((7,)),
        pltpu.SemaphoreType.DMA((7,)),
    ]


HALF_REFS = 6


class ReduceHalf:
    def __init__(self, own, from_plane, by_line, from_line, send, recv):
        self.refs = own, from_plane, by_line, from_line
        z, x, y, core = coordinates()
        self.number = 2 * x + y

        def copy(src, dst, i, j, device):
            return pltpu.make_async_remote_copy(
                src_ref=src,
                dst_ref=dst,
                send_sem=send.at[i],
                recv_sem=recv.at[j],
                device_id=device,
                device_id_type=MESH,
            )

        self.plane = [
            copy(own.at[number], from_plane.at[i], i, i, device)
            for i, (device, number) in enumerate(plane_mates())
        ]
        self.line, self.mine = [], []
        for block in range(4):
            there, owner = 2 * core + block // 2, block % 2
            device = device_at(there, x, y, owner)
            self.line.append(copy(by_line.at[block], from_line.at[z], 3 + block, 3 + z, device))
            self.mine.append((there == z) & (owner == core))
        self.arrivals = []
        for there in range(4):
            arrival = copy(by_line.at[0], from_line.at[there], 3, 3 + there, sibling())
            self.arrivals.append((arrival, (there == z) & (z // 2 == core)))

    def fill(self, dwqkv, dvec):
        own = self.refs[0]
        rows = own.shape[2]

        def pieces(x):
            return x.reshape(16, 8, 256)

        terms = [pieces(dwqkv[128 * j : 128 * j + 128]) for j in range(3)]
        vec = dvec[...]
        high = vec.astype(BF).astype(F32)
        terms.append(pieces(jnp.concatenate([high, vec - high], axis=1)))
        terms = jnp.concatenate(terms, axis=1).astype(BF).reshape(2, 4, 2, rows, 256)
        for plane in range(4):
            own[plane] = terms[:, plane].reshape(4, rows, 256)

    def first(self):
        for c in self.plane:
            c.start()

    def second(self):
        own, from_plane, by_line, from_line = self.refs
        z = lax.axis_index("wide") // 2
        for c in self.plane:
            c.wait()
        total = own[self.number].astype(F32)
        for i in range(3):
            total = total + from_plane[i].astype(F32)
        by_line[...] = total.astype(BF)
        for block in range(4):

            @pl.when(jnp.logical_not(self.mine[block]))
            def _(block=block):
                self.line[block].start()

            @pl.when(self.mine[block])
            def _(block=block):
                from_line[z] = by_line[block]

    def result(self):
        from_line = self.refs[3]
        for arrival, mine in self.arrivals:
            pl.when(jnp.logical_not(mine))(arrival.wait_recv)
        for copy, mine in zip(self.line, self.mine):
            pl.when(jnp.logical_not(mine))(copy.wait_send)
        total = from_line[0].astype(F32)
        for i in range(1, 4):
            total = total + from_line[i].astype(F32)
        return total


def project_back(half, part, w_ref, layer):
    rows = jnp.concatenate([half_rows(w_ref, layer, 256 * j, half) for j in range(3)], axis=0)
    return dot(rows, part, 0, 0)


def middle_kernel(direct, *refs):
    dqkv, d_first_in, wqkv, ctx, unit1, hidden, unit2, scales, wo, wup, wdn, cols_ref = refs[:12]
    cols = cols_ref.at[0]
    refs = refs[12:]
    if direct:
        outer, inner, refs = refs[:4], refs[4:6], refs[6:]
    d_first, dctx, dwo, dwup, dwdn, dvec = refs[:6]
    refs = refs[6:]
    if direct:
        (sums_outer, sums_inner), refs = refs[:2], refs[2:]
    landed, sums, out, send, recv = refs[:5]
    count = d_first.shape[1] // BLOCK
    core, peer = pair_of()
    d_copy = to_peer(dqkv.at[1], landed, send.at[count], recv.at[count], peer)
    if direct:
        two = ReduceHalf(*refs[5 : 5 + HALF_REFS])
        one = Reduce(*refs[5 + HALF_REFS :])

    def copy(i):
        ds = block_of(i)
        return to_peer(out.at[:, ds], dctx.at[1, :, ds], send.at[i], recv.at[i], peer)

    if direct:
        greet_all()
    else:
        greet(peer)
    d_copy.start()
    if direct:
        two.fill(*inner)
        two.first()
        one.fill(outer_shares(*outer))
        one.first()
    for ref in (sums, dwo, dwup, dwdn):
        ref[...] = jnp.zeros_like(ref)
    d_copy.wait()
    if direct:
        one.second()

    @pl.loop(0, count)
    def _(i):
        if direct:

            @pl.when(i == 1)
            def _():
                two.second()
                one.third()

        ds = block_of(i)
        g = d_first_in[:, ds] + project_back(core, dqkv[0, :, ds], wqkv, 1)
        g = g + project_back(1 - core, landed[:, ds], wqkv, 1)
        saved = (unit1[:, ds], scales[0:1, ds], hidden[:, ds], unit2[:, ds], scales[1:2, ds])
        d_first[:, ds], d_context = backward_block(
            g, ctx[:, ds], saved, (wo[0], wup[...], wdn[...]), cols, sums, dwo, dwup, dwdn
        )
        low, high = d_context[:128], d_context[128:]
        out[:, ds] = jnp.where(core == 0, high, low)
        copy(i).start()
        dctx[0, :, ds] = jnp.where(core == 0, low, high)

    dvec[...] = place_vectors(sums)
    if direct:
        sums_inner[...] = two.result()
        sums_outer[...] = one.result()

    @pl.loop(0, count)
    def _(i):
        copy(i).wait()


def middle(direct, dqkv, d_first, wqkv, ctx, unit1, hidden, unit2, scales, wo, wup, wdn, cols, outer, inner):
    length = d_first.shape[1]
    terms = (*outer, *inner) if direct else ()
    shapes = (shape_of((256, length), F32), shape_of((2, 128, length), BF))
    shapes += tuple(shape_of(s, F32) for s in GRAD_SHAPES)
    if direct:
        shapes += (shape_of((OUTER, 256), F32), shape_of((INNER, 256), F32))
    return pl.pallas_call(
        functools.partial(middle_kernel, direct),
        name="back_between",
        out_shape=shapes,
        in_specs=[VMEM_SPEC] * (12 + len(terms)),
        out_specs=[VMEM_SPEC] * len(shapes),
        scratch_shapes=[
            pltpu.VMEM((384, length), BF),
            pltpu.VMEM((2560, 128), F32),
            pltpu.VMEM((128, length), BF),
        ]
        + pair_semaphores(length // BLOCK)
        + (reduce_half_scratch(INNER) + reduce_scratch(OUTER) if direct else []),
        compiler_params=params(5),
    )(dqkv, d_first, wqkv, ctx, unit1, hidden, unit2, scales, wo, wup, wdn, cols, *terms)


def last_kernel(direct, *refs):
    dqkv, d_first, wqkv = refs[:3]
    refs = refs[3:]
    if direct:
        outer, inner, (grad_out, sums_outer, sums_inner) = refs[:4], refs[4:6], refs[6:9]
        refs = refs[9:]
    else:
        grad_out, refs = refs[0], refs[1:]
    landed, grad, send, recv = refs[:4]
    count = d_first.shape[1] // BLOCK
    core, peer = pair_of()
    d_copy = to_peer(dqkv.at[1], landed, send, recv, peer)
    if direct:
        two = ReduceHalf(*refs[4 : 4 + HALF_REFS])
        one = Reduce(*refs[4 + HALF_REFS :])
        greet_all()
        two.fill(*inner)
        two.first()
        one.fill(outer_shares(*outer))
        one.first()
    else:
        greet(peer)
    d_copy.start()
    if direct:
        one.second()

    @pl.loop(0, count)
    def _(i):
        ds = block_of(i)
        grad[:, ds] = d_first[:, ds] + project_back(core, dqkv[0, :, ds], wqkv, 0)

    if direct:
        two.second()
    d_copy.wait()

    @pl.loop(0, count)
    def _(i):
        if direct:
            pl.when(i == 1)(one.third)
        ds = block_of(i)
        grad_out[0, ds] = jnp.transpose(grad[:, ds] + project_back(1 - core, landed[:, ds], wqkv, 0))

    if direct:
        sums_inner[...] = two.result()
        sums_outer[...] = one.result()


def last(direct, dqkv, d_first, wqkv, outer, inner):
    length = d_first.shape[1]
    terms = (*outer, *inner) if direct else ()
    shapes = (shape_of((1, length, 256), F32),)
    if direct:
        shapes += (shape_of((OUTER, 256), F32), shape_of((INNER, 256), F32))
    return pl.pallas_call(
        functools.partial(last_kernel, direct),
        name="back_input",
        out_shape=shapes,
        in_specs=[VMEM_SPEC] * (3 + len(terms)),
        out_specs=[VMEM_SPEC] * len(shapes),
        scratch_shapes=[
            pltpu.VMEM((384, length), BF),
            pltpu.VMEM((256, length), F32),
            pltpu.SemaphoreType.DMA,
            pltpu.SemaphoreType.DMA,
        ]
        + (reduce_half_scratch(INNER) + reduce_scratch(OUTER) if direct else []),
        compiler_params=params(6),
    )(dqkv, d_first, wqkv, *terms)


def finish_kernel(factor, outer1, inner1, outer0, inner0, *refs):
    qw, qb, kw, vw, vb, ow, ob, g1, s1, uw, ub, dw, db, g2, s2 = refs
    layers = (
        (inner0[...] * factor, outer0[...] * factor),
        (inner1[...] * factor, outer1[...] * factor),
    )
    for layer, (inner, outer) in enumerate(layers):
        qw[layer], kw[layer], vw[layer] = inner[0:8], inner[8:16], inner[16:24]
        ow[layer] = outer[0:8]
        dw[layer, :, 0:256], dw[layer, :, 256:512] = outer[8:16], outer[16:24]
        uw[layer] = outer[32:48]
        vec = inner[24:32] + outer[24:32]
        vec = jnp.transpose(vec[:, 0:128] + vec[:, 128:256])
        for i, ref in enumerate((qb, vb, ob, g1, s1, db, g2, s2)):
            ref[layer : layer + 1] = vec[i : i + 1]
        ub[layer : layer + 1, 0:8] = vec[8:9]
        ub[layer : layer + 1, 8:16] = vec[9:10]


def finish(factor, sums, like):
    found = pl.pallas_call(
        functools.partial(finish_kernel, factor),
        name="finish",
        out_shape=tuple(shape_of(a.shape, F32) for a in like),
        in_specs=[VMEM_SPEC] * 4,
        out_specs=[VMEM_SPEC] * len(like),
        compiler_params=params(),
    )(*sums)
    return [jnp.swapaxes(a, 1, 2) if a.ndim == 3 else a for a in found]


def gather_by_collectives(weights, vectors):
    def whole_of(w):
        return lax.all_gather(w, AXES, axis=1, tiled=True)

    qw, kw, vw, ow, uw, dw = (whole_of(w) for w in weights)
    columns = [lax.all_gather(v, AXES, axis=1, tiled=True).astype(F32) for v in vectors]
    up = columns.pop().reshape(2, 32, 2, 8)
    columns += [up[:, :, 0].reshape(2, 256), up[:, :, 1].reshape(2, 256)]
    vec = jnp.pad(jnp.stack(columns, axis=2), ((0, 0), (0, 0), (0, 118)))
    return jnp.concatenate([qw, kw, vw], axis=1), ow, uw, dw, vec


def sum_by_collectives(factor, layers):
    def share(x):
        return lax.psum_scatter(x, AXES, scatter_dimension=0, tiled=True) * factor

    found = []
    core = lax.rem(lax.axis_index("narrow"), 2)

    def widen(x):
        parts = x.reshape(-1, 1, 128, x.shape[1])
        mine = (jnp.arange(2) == core)[None, :, None, None]
        return jnp.where(mine, parts, 0.0).reshape(-1, x.shape[1])

    for dwqkv, dvec_qkv, dwo, dwup, dwdn, dvec in layers:
        dwqkv = widen(dwqkv)
        vec = widen(dvec_qkv) + dvec
        qb, vb, ob, g1, s1, db, g2, s2 = (share(vec[:, i]) for i in range(8))
        up = jnp.stack([vec[:, 8].reshape(32, 8), vec[:, 9].reshape(32, 8)], axis=1)
        qw, kw, vw = (share(dwqkv[256 * i : 256 * i + 256]).T for i in range(3))
        ow, uw, dw = share(dwo).T, share(dwup).T, share(dwdn).T
        ub = share(up.reshape(512))
        found.append((qw, qb, kw, vw, vb, ow, ob, g1, s1, uw, ub, dw, db, g2, s2))
    return [jnp.stack(pair) for pair in zip(*found)]


def on_device(devices, direct, cells_in, lengths, cotangent, *weights):
    qw, qb, kw, vw, vb, ow, ob, g1, s1, uw, ub, dw, db, g2, s2 = weights
    matrices, vectors = (qw, kw, vw, ow, uw, dw), (qb, vb, ob, g1, s1, db, g2, s2, ub)
    turned = [jnp.swapaxes(w, 1, 2) for w in matrices]
    if direct:
        share, end = own_share(lengths, turned, vectors)
        lens, qkv0, wqkv, wo, wup0, wdn0, cols, xs0 = start(share, cells_in)
    else:
        wqkv, wo, wup, wdn, vec = gather_by_collectives(turned, vectors)
        wup0, wdn0, end, feed_forward = wup[0], wdn[0], None, (wup[1], wdn[1])
        cols = columns(vec)
        lens, qkv0, xs0 = project_first(lengths, cells_in, wqkv, cols)
    ctx_pair, ctx32_0, logs0 = attend(lens, qkv0)
    x1, ctx0, unit1, hidden, unit2, scales, qkv1, xs1, *landed = between(
        direct, ctx_pair, cells_in, wqkv, wo, wup0, wdn0, cols, end
    )
    if direct:
        feed_forward = landed
    ctx_pair, ctx32_1, logs1 = attend(lens, qkv1)
    cells_out, d_first, dctx, *outer1 = turn(
        direct, lens, ctx_pair, x1, cotangent, wo, cols, feed_forward
    )
    dqkv, *inner1 = attend_back(lens, qkv1, dctx, ctx32_1, logs1, xs1)
    d_first, dctx, *found = middle(
        direct, dqkv, d_first, wqkv, ctx0, unit1, hidden, unit2, scales, wo, wup0, wdn0, cols, outer1, inner1
    )
    outer0, sums1 = found[:4], found[4:]
    dqkv, *inner0 = attend_back(lens, qkv0, dctx, ctx32_0, logs0, xs0)
    grad_in, *sums0 = last(direct, dqkv, d_first, wqkv, outer0, inner0)
    factor = 1.0 / math.sqrt(devices * cells_in.shape[0] * cells_in.shape[1])
    if direct:
        like = [shape_of(a.shape[:1] + a.shape[:0:-1], F32) for a in weights]
        grads = finish(factor, (*sums1, *sums0), like)
    else:
        grads = sum_by_collectives(factor, ((*inner0, *outer0), (*inner1, *outer1)))
    return (cells_out, grad_in, *grads)


def solution(mesh):
    devices = mesh.size
    direct = (mesh.shape["wide"], mesh.shape["narrow"]) == (8, 4)
    cell, vector, matrix = P(AXES, None, None), P(None, AXES), P(None, None, AXES)
    placed = (
        matrix, vector, matrix, matrix, vector, matrix, vector, vector, vector,
        matrix, vector, matrix, vector, vector, vector,
    )
    return jax.shard_map(
        functools.partial(on_device, devices, direct),
        mesh=mesh,
        in_specs=(cell, P(AXES), cell) + placed,
        out_specs=(cell, cell) + placed,
        check_vma=False,
    )
```

```python
import functools
import math

import jax
import jax.numpy as jnp
from jax import lax
from jax.experimental import pallas as pl
from jax.experimental.pallas import tpu as pltpu
from jax.sharding import PartitionSpec as P

HEAD = 64
NEG = -1000000000.0
EPS = 1e-06
AXES = ("wide", "narrow")
MESH = pl.DeviceIdType.MESH
BF = jnp.bfloat16
F32 = jnp.float32
EXT = 16
GUARD = 3600.0
CHUNK = 1024
RESTS = (384, 512, 640, 768)
ROWS = 64
VMEM_SPEC = pl.BlockSpec(memory_space=pltpu.VMEM)
SMEM_SPEC = pl.BlockSpec(memory_space=pltpu.SMEM)
HBM_SPEC = pl.BlockSpec(memory_space=pltpu.HBM)
QB, VB, OB, G1, S1, DB, G2, S2, UB = range(9)


def dot(a, b, ca, cb):
    return lax.dot_general(a, b, (((ca,), (cb,)), ((), ())), preferred_element_type=F32)


def params(collective_id=None, limit=16):
    if collective_id is None:
        return pltpu.CompilerParams(vmem_limit_bytes=limit << 20)
    return pltpu.CompilerParams(
        vmem_limit_bytes=limit << 20, collective_id=collective_id, has_side_effects=True
    )


def shape_of(shape, dtype):
    return jax.ShapeDtypeStruct(shape, dtype)


def pair_of():
    narrow = lax.axis_index("narrow")
    core = lax.rem(narrow, 2)
    return core, (lax.axis_index("wide"), narrow + 1 - 2 * core)


def greet(peer):
    hail([peer])
    await_hails([peer])


def to_peer(src, dst, send, recv, peer):
    return pltpu.make_async_remote_copy(
        src_ref=src, dst_ref=dst, send_sem=send, recv_sem=recv, device_id=peer, device_id_type=MESH
    )


def half_rows(ref, layer, base, half):
    return ref[layer, pl.ds(pl.multiple_of(base + half * 128, 128), 128)]


def tile_lanes(column, count):
    return jnp.concatenate([column] * (count // 128), axis=1)


def spread(both, layer, cols_ref, names):
    def every_lane(i):
        return jnp.broadcast_to(both[:, 2 * i + layer : 2 * i + layer + 1], (256, 128))

    for i in names:
        if i < UB:
            cols_ref[pl.ds(i * 256, 256)] = every_lane(i)
        else:
            halves = [every_lane(j).reshape(32, 8, 128) for j in (UB, UB + 1)]
            cols_ref[pl.ds(i * 256, 512)] = jnp.concatenate(halves, axis=1).reshape(512, 128)


def columns_kernel(vec, cols):
    for layer in range(2):
        spread(vec[...], layer, cols.at[layer], range(9))


def columns(vec):
    return pl.pallas_call(
        columns_kernel,
        name="columns",
        out_shape=shape_of((2, 2560, 128), F32),
        in_specs=[VMEM_SPEC],
        out_specs=VMEM_SPEC,
        compiler_params=params(),
    )(vec)


def column(cols_ref, i, count):
    rows = 512 if i == UB else 256
    return tile_lanes(cols_ref[pl.ds(i * 256, rows)], count)


def fold_lanes(x):
    total = x[:, :128]
    for start in range(128, x.shape[1], 128):
        total = total + x[:, start : start + 128]
    return total


def norm(resid):
    offset = resid - jnp.mean(resid, axis=0, keepdims=True)
    scale = lax.rsqrt(jnp.mean(offset * offset, axis=0, keepdims=True) + EPS)
    return offset * scale, scale


def norm_back(grad, gain, unit, scale):
    q = grad * gain
    return (
        q - jnp.mean(q, axis=0, keepdims=True) - unit * jnp.mean(q * unit, axis=0, keepdims=True)
    ) * scale


GELU_C = 0.7978845608028654
GELU_A = 0.044715


def project(xb, contract, w_ref, cols_ref, half, layer=0):
    parts = []
    for i in range(3):
        y = dot(half_rows(w_ref, layer, i * 256, half), xb, 1, contract)
        if i != 1:
            bias = cols_ref[
                pl.ds(pl.multiple_of((QB if i == 0 else VB) * 256 + half * 128, 128), 128)
            ]
            y = y + tile_lanes(bias, y.shape[1])
        y = y.astype(BF)
        parts.append(y * jnp.asarray(0.125, BF) if i == 0 else y)
    return jnp.concatenate(parts, axis=0)


def join(core, own, peer):
    return jnp.concatenate(
        [jnp.where(core == 0, own, peer), jnp.where(core == 0, peer, own)], axis=0
    )


def forward_block(context, x, wo, wup, wdn, cols_ref):
    count = x.shape[1]
    unit1, scale1 = norm(x + dot(wo, context, 1, 0) + column(cols_ref, OB, count))
    middle = unit1 * column(cols_ref, G1, count) + column(cols_ref, S1, count)
    hidden = dot(wup, middle.astype(BF), 1, 0) + column(cols_ref, UB, count)
    t = jnp.tanh(hidden * (GELU_C + (GELU_C * GELU_A) * (hidden * hidden)))
    active = (0.5 * hidden * (1.0 + t)).astype(BF)
    unit2, scale2 = norm(middle + dot(wdn, active, 1, 0) + column(cols_ref, DB, count))
    x_next = unit2 * column(cols_ref, G2, count) + column(cols_ref, S2, count)
    return unit1, scale1, hidden, unit2, scale2, x_next


def gelu_parts(hidden):
    square = hidden * hidden
    t = jnp.tanh(hidden * (GELU_C + (GELU_C * GELU_A) * square))
    half, more = 0.5 * hidden, 1.0 + t
    slope = 0.5 * more + half * (1.0 - t * t) * (GELU_C + (3.0 * GELU_C * GELU_A) * square)
    return (half * more).astype(BF), slope


def backward_block(grad, context, saved, weights, cols_ref, sums, dwo, dwup, dwdn):
    unit1, scale1, (active, slope), unit2, scale2 = saved
    wo, wup, wdn = weights
    count = grad.shape[1]

    def add(i, x):
        rows = x.shape[0]
        sums[pl.ds(i * 256, rows)] += fold_lanes(x)

    add(S2, grad)
    add(G2, grad * unit2)
    d_second = norm_back(grad, column(cols_ref, G2, count), unit2, scale2)
    branch = d_second.astype(BF)
    add(DB, branch.astype(F32))
    d_hidden = (dot(wdn, branch, 0, 0) * slope).astype(BF)
    dwdn[...] += dot(branch, active, 1, 1)
    add(UB, d_hidden.astype(F32))
    middle = unit1 * column(cols_ref, G1, count) + column(cols_ref, S1, count)
    dwup[...] += dot(d_hidden, middle.astype(BF), 1, 1)
    d_middle = d_second + dot(wup, d_hidden, 0, 0)
    add(S1, d_middle)
    add(G1, d_middle * unit1)
    d_first = norm_back(d_middle, column(cols_ref, G1, count), unit1, scale1)
    attn = d_first.astype(BF)
    add(OB, attn.astype(F32))
    dwo[...] += dot(attn, context, 1, 1)
    return d_first, dot(wo, attn, 0, 0).astype(BF)


def place_vectors(sums):
    lane = lax.broadcasted_iota(jnp.int32, (256, 128), 1)
    out = jnp.zeros((256, 128), F32)
    for i in range(8):
        total = jnp.sum(sums[pl.ds(i * 256, 256)], axis=1, keepdims=True)
        out = jnp.where(lane == i, total, out)
    up = jnp.sum(sums[pl.ds(2048, 512)], axis=1, keepdims=True)
    up = jnp.broadcast_to(up, (512, 128)).reshape(32, 16, 128)
    out = jnp.where(lane == 8, up[:, :8].reshape(256, 128), out)
    return jnp.where(lane == 9, up[:, 8:].reshape(256, 128), out)


def coordinates():
    wide, narrow = lax.axis_index("wide"), lax.axis_index("narrow")
    return wide // 2, lax.rem(wide, 2), narrow // 2, lax.rem(narrow, 2)


def device_at(z, x, y, core):
    return (2 * z + x, 2 * y + core)


def plane_mates():
    z, x, y, core = coordinates()
    return [
        (device_at(z, a, b, core), 2 * a + b) for a, b in ((x, 1 - y), (1 - x, y), (1 - x, 1 - y))
    ]


def line_mates():
    z, x, y, core = coordinates()
    there = [lax.rem(z + j, 4) for j in (1, 2, 3)]
    return [(device_at(a, x, y, core), a) for a in there]


def sibling():
    z, x, y, core = coordinates()
    return device_at(z, x, y, 1 - core)


def column_mates():
    z, x, y, core = coordinates()
    return [device_at(there, x, y, 1 - core) for _, there in line_mates()]


def hail(mates):
    for mate in mates:
        pl.semaphore_signal(
            pltpu.get_barrier_semaphore(), inc=1, device_id=mate, device_id_type=MESH
        )


def await_hails(mates):
    pl.semaphore_wait(pltpu.get_barrier_semaphore(), len(mates))


def gather_mates():
    return [sibling()] + [d for d, _ in plane_mates()] + [d for d, _ in line_mates()]


FIRST, REST = 48, 96


SHARE = 80


def share_kernel(length, qw, kw, vw, ow, uw, dw, *refs):
    vectors, share = refs[:-1], refs[-1]
    for layer in range(2):
        for i, w in enumerate((qw, kw, vw, ow)):
            share[layer, 8 * i : 8 * i + 8] = w[layer]
        share[layer, 32:48] = uw[layer]
        share[layer, 48:56] = dw[layer, :, 0:256]
        share[layer, 56:64] = dw[layer, :, 256:512]
        share[layer, 64:80] = jnp.zeros((16, 256), BF)
        at = 0
        for v in vectors:
            share[layer, 64:65, at : at + v.shape[1]] = v[layer : layer + 1]
            at += v.shape[1]
        number = length[...].reshape(1, 1)
        share[layer, 64:65, at : at + 1] = (number // 256).astype(F32).astype(BF)
        share[layer, 64:65, at + 1 : at + 2] = (number % 256).astype(F32).astype(BF)


def own_share(lengths, weights, vectors):
    return pl.pallas_call(
        share_kernel,
        name="own_share",
        out_shape=shape_of((2, SHARE, 256), BF),
        in_specs=[VMEM_SPEC] * 16,
        out_specs=VMEM_SPEC,
        compiler_params=params(limit=60),
    )(lengths, *weights, *vectors)


def pack_own(share, first, rest, flat):
    flat[...] = jnp.zeros_like(flat)
    for layer in range(2):
        row = share[layer, 64:80].astype(F32)[0:1]
        for i in range(10):
            at = 2 * i + layer
            flat[at : at + 1, 0:8] = row[:, 8 * i : 8 * i + 8]
    columns = jnp.transpose(flat[...])[0:8]
    block = jnp.concatenate([columns, jnp.zeros_like(columns)], axis=1)
    first[0:32] = share[0, 0:32]
    first[32:48] = jnp.concatenate([block, jnp.zeros_like(block)], axis=0).astype(BF)
    rest[0:32] = share[0, 32:64]
    rest[32:96] = share[1, 0:64]


def ordered(landed, at, rows):
    pieces = [
        landed[core, plane, z, at : at + rows]
        for z in range(4)
        for plane in range(4)
        for core in range(2)
    ]
    return jnp.stack(pieces)


def two_matrices(landed, at):
    pair = ordered(landed, at, 16).astype(F32)
    return (
        pair[:, :8].reshape(256, 256).astype(BF),
        pair[:, 8:].reshape(256, 256).astype(BF),
    )


def unpack_first(landed, wqkv, wo, both):
    wqkv[0, 0:256], wqkv[0, 256:512] = two_matrices(landed, 0)
    wqkv[0, 512:768], wo[0] = two_matrices(landed, 16)
    both[...] = ordered(landed, 32, 16).astype(F32)[:, :8, :128].reshape(256, 128)


def unpack_feed_forward(landed, at, up, down):
    up[...] = ordered(landed, at, 16).reshape(512, 256)
    down[:, 0:256], down[:, 256:512] = two_matrices(landed, at + 16)


def unpack_rest(landed, wqkv, wo, up, down):
    unpack_feed_forward(landed, 0, up, down)
    wqkv[1, 0:256], wqkv[1, 256:512] = two_matrices(landed, 32)
    wqkv[1, 512:768], wo[1] = two_matrices(landed, 48)


class Gather:
    def __init__(self, own, landed, send, recv, part):
        z, x, y, core = coordinates()
        plane = 2 * x + y

        def copy(src, dst, i, device):
            return pltpu.make_async_remote_copy(
                src_ref=src,
                dst_ref=dst,
                send_sem=send.at[part, i],
                recv_sem=recv.at[part, i],
                device_id=device,
                device_id_type=MESH,
            )

        def column(i):
            return landed.at[core, i]

        self.keep = lambda: landed.at[core, plane, z].__setitem__(Ellipsis, own[...])
        self.line = [
            copy(own, landed.at[core, plane, z], i, device)
            for i, (device, _) in enumerate(line_mates())
        ]
        self.plane = [
            copy(column(plane), column(plane), 3 + i, device)
            for i, (device, _) in enumerate(plane_mates())
        ]
        columns = [plane] + [number for _, number in plane_mates()]
        self.cores = [
            copy(column(number), column(number), 6 + i, sibling())
            for i, number in enumerate(columns)
        ]


def start_kernel(
    share, x_ref,
    lens, qkv, wqkv, wo, wup, wdn, cols, xs, landed_rest,
    first, rest, flat, landed_first, both, out, own_len, send, recv, pair_send, pair_recv, x_sems,
):
    core, peer = pair_of()
    mates = gather_mates()
    hail(mates)
    pack_own(share, first, rest, flat)
    number = share[0, 64:80].astype(F32)[0:1]
    number = number[:, 80:81] * 256.0 + number[:, 81:82]
    own_len[...] = jnp.broadcast_to(number, own_len.shape).astype(jnp.int32)
    a = Gather(first, landed_first, send, recv, 0)
    b = Gather(rest, landed_rest, send, recv, 1)
    await_hails(mates)
    for c in a.line + b.line:
        c.start()
    len_copy = to_peer(own_len, lens.at[1], pair_send.at[0], pair_recv.at[0], peer)
    len_copy.start()
    x_copy = to_peer(x_ref.at[0], xs.at[1], x_sems.at[0], x_sems.at[1], peer)
    x_copy.start()
    a.keep()
    b.keep()
    lens[0] = own_len[...]
    xs[0] = x_ref[0]
    for part in (a, b):
        for c in part.line:
            c.wait()
        for c in part.plane + part.cores[:1]:
            c.start()
    for i in range(3):
        a.plane[i].wait()
        a.cores[1 + i].start()
    for c in a.cores:
        c.wait()
    unpack_first(landed_first, wqkv, wo, both)
    spread(both[...], 0, cols.at[0], (QB, VB))
    block = 1024
    count = x_ref.shape[1] // block

    def copy(i):
        ds = pl.ds(pl.multiple_of(i * block, block), block)
        return to_peer(
            out.at[:, ds], qkv.at[1, :, ds], pair_send.at[1 + i], pair_recv.at[1 + i], peer
        )

    @pl.loop(0, count)
    def _(i):
        ds = pl.ds(pl.multiple_of(i * block, block), block)
        out[:, ds] = project(x_ref[0, ds], 1, wqkv, cols.at[0], 1 - core)
        copy(i).start()

    @pl.loop(0, count)
    def _(i):
        ds = pl.ds(pl.multiple_of(i * block, block), block)
        qkv[0, :, ds] = project(x_ref[0, ds], 1, wqkv, cols.at[0], core)

    spread(both[...], 0, cols.at[0], (OB, G1, S1, DB, G2, S2, UB))
    spread(both[...], 1, cols.at[1], range(9))
    for i in range(3):
        b.plane[i].wait()
        b.cores[1 + i].start()
    for c in b.cores:
        c.wait()
    unpack_rest(landed_rest, wqkv, wo, wup, wdn)
    len_copy.wait()
    x_copy.wait()

    @pl.loop(0, count)
    def _(i):
        copy(i).wait()


def start(share, cells):
    length = cells.shape[1]
    count = length // 1024
    return pl.pallas_call(
        start_kernel,
        name="gather_and_project",
        out_shape=(
            shape_of((2, 8, 128), jnp.int32),
            shape_of((2, 384, length), BF),
            shape_of((2, 768, 256), BF),
            shape_of((2, 256, 256), BF),
            shape_of((512, 256), BF),
            shape_of((256, 512), BF),
            shape_of((2, 2560, 128), F32),
            shape_of((2, length, 256), BF),
            shape_of((2, 4, 4, REST, 256), BF),
        ),
        in_specs=[VMEM_SPEC] * 2,
        out_specs=[VMEM_SPEC] * 9,
        scratch_shapes=[
            pltpu.VMEM((FIRST, 256), BF),
            pltpu.VMEM((REST, 256), BF),
            pltpu.VMEM((128, 128), F32),
            pltpu.VMEM((2, 4, 4, FIRST, 256), BF),
            pltpu.VMEM((256, 128), F32),
            pltpu.VMEM((384, length), BF),
            pltpu.VMEM((8, 128), jnp.int32),
            pltpu.SemaphoreType.DMA((2, 10)),
            pltpu.SemaphoreType.DMA((2, 10)),
            pltpu.SemaphoreType.DMA((count + 1,)),
            pltpu.SemaphoreType.DMA((count + 1,)),
            pltpu.SemaphoreType.DMA((2,)),
        ],
        compiler_params=params(1),
    )(share, cells)


def project_kernel(len_ref, x_ref, w_ref, cols_ref, lens, qkv, xs, out, own_len, send, recv):
    core, peer = pair_of()
    cols = cols_ref.at[0]
    own_len[...] = jnp.full(own_len.shape, len_ref[0], jnp.int32)
    greet(peer)
    len_copy = to_peer(own_len, lens.at[1], send.at[0], recv.at[0], peer)
    len_copy.start()
    lens[0] = own_len[...]
    x_copy = to_peer(x_ref.at[0], xs.at[1], send.at[2], recv.at[2], peer)
    x_copy.start()
    xs[0] = x_ref[0]
    out[...] = project(x_ref[0], 1, w_ref, cols, 1 - core)
    qkv_copy = to_peer(out, qkv.at[1], send.at[1], recv.at[1], peer)
    qkv_copy.start()
    qkv[0] = project(x_ref[0], 1, w_ref, cols, core)
    len_copy.wait()
    qkv_copy.wait()
    x_copy.wait()


def project_first(lengths, cells, wqkv, cols):
    length = cells.shape[1]
    return pl.pallas_call(
        project_kernel,
        name="project_first",
        out_shape=(
            shape_of((2, 8, 128), jnp.int32),
            shape_of((2, 384, length), BF),
            shape_of((2, length, 256), BF),
        ),
        in_specs=[SMEM_SPEC] + [VMEM_SPEC] * 3,
        out_specs=[VMEM_SPEC] * 3,
        scratch_shapes=[
            pltpu.VMEM((384, length), BF),
            pltpu.VMEM((8, 128), jnp.int32),
            pltpu.SemaphoreType.DMA((3,)),
            pltpu.SemaphoreType.DMA((3,)),
        ],
        compiler_params=params(2),
    )(lengths, cells, wqkv, cols)


def extended(x, extra):
    return jnp.concatenate([x, extra], axis=0)


def one_head(x, head):
    row = lax.broadcasted_iota(jnp.int32, x.shape, 0)
    return jnp.where((row // HEAD) == head, x, jnp.zeros_like(x))


def head_rows(base, head):
    return pl.ds(pl.multiple_of(base + HEAD * head, HEAD), HEAD)


def over_keys(valid, step):
    whole_ones = (valid + (CHUNK - RESTS[-1] - 1)) // CHUNK
    rest = valid - whole_ones * CHUNK

    @pl.loop(0, whole_ones)
    def _(j):
        step(pl.multiple_of(j * CHUNK, CHUNK), CHUNK)

    for low, size in zip((0,) + RESTS[:-1], RESTS):

        @pl.when((rest > low) & (rest <= size))
        def _(size=size):
            step(pl.multiple_of(whole_ones * CHUNK, CHUNK), size)


def attend_kernel(lens, qkv, ctx, ctx32, logs, kx, scores, total, acc):
    length = qkv.shape[2]
    wide = 1024

    def query_of(cell, i, head, wide):
        q = qkv[cell, 0:128, pl.ds(pl.multiple_of(i * wide, wide), wide)]
        row = lax.broadcasted_iota(jnp.int32, (EXT, wide), 0)
        return extended(one_head(q, head), jnp.where(row == 0, 1.0, 0.0).astype(BF))

    def largest(x):
        x = x.astype(F32)
        square = x * x
        return [
            jnp.max(jnp.sum(square[HEAD * h : HEAD * h + HEAD], axis=0, keepdims=True))
            for h in range(2)
        ]

    @pl.loop(0, 2)
    def _(cell):
        valid = lens[cell, 0, 0]
        q_most = largest(qkv[cell, 0:128])
        k_most = largest(qkv[cell, 128:256])
        plain = jnp.maximum(q_most[0] * k_most[0], q_most[1] * k_most[1]) <= GUARD
        acc[...] = jnp.zeros_like(acc)
        total[...] = jnp.zeros_like(total)

        @pl.loop(0, length // 512)
        def _(i):
            ds = pl.ds(pl.multiple_of(i * 512, 512), 512)
            where = lax.broadcasted_iota(jnp.int32, (EXT, 512), 1) + i * 512
            first = lax.broadcasted_iota(jnp.int32, (EXT, 512), 0) == 0
            extra = jnp.where(first & (where >= valid), NEG, 0.0).astype(BF)
            kx[ds] = jnp.transpose(extended(qkv[cell, 128:256, ds], extra))

        @pl.when(plain)
        def _():
            def step(start, size):
                keys = pl.ds(start, size)

                @pl.loop(0, length // wide)
                def _(i):
                    ds = pl.ds(pl.multiple_of(i * wide, wide), wide)
                    for head in range(2):
                        s = dot(kx[keys], query_of(cell, i, head, wide), 1, 0)
                        e = jnp.exp(s)
                        total[head, :, ds] += jnp.sum(e.reshape(size // 8, 8, wide), axis=0)
                        v = qkv[cell, 256 + HEAD * head : 320 + HEAD * head, keys]
                        acc[HEAD * head : HEAD * head + HEAD, ds] += dot(v, e.astype(BF), 1, 0)

            over_keys(valid, step)
            for head in range(2):
                rows = slice(HEAD * head, HEAD * head + HEAD)
                sums = jnp.sum(total[head], axis=0, keepdims=True)
                out = acc[rows] * (1.0 / sums)
                ctx[cell, rows] = out.astype(BF)
                ctx32[cell, rows] = out
                logs[cell, head : head + 1] = jnp.log(sums)

        @pl.when(jnp.logical_not(plain))
        def _():
            chunks = pl.cdiv(valid, 256)
            wide = 512

            @pl.loop(0, 2 * (length // wide))
            def _(step):
                i, head = step // 2, lax.rem(step, 2)
                ds = pl.ds(pl.multiple_of(i * wide, wide), wide)
                rows = head_rows(0, head)
                query = query_of(cell, i, head, wide)

                def score(j, high):
                    s = dot(kx[pl.ds(pl.multiple_of(j * 256, 256), 256)], query, 1, 0)
                    scores[j] = s
                    return jnp.maximum(high, jnp.max(s.reshape(32, 8, wide), axis=0))

                high = lax.fori_loop(0, chunks, score, jnp.full((8, wide), NEG * 2, F32))
                high = jnp.max(high, axis=0, keepdims=True)

                @pl.loop(0, chunks)
                def _(j):
                    e = jnp.exp(scores[j] - high)
                    total[head, :, ds] += jnp.sum(e.reshape(32, 8, wide), axis=0)
                    v = qkv[cell, head_rows(256, head), pl.ds(pl.multiple_of(j * 256, 256), 256)]
                    acc[rows, ds] += dot(v, e.astype(BF), 1, 0)

                sums = jnp.sum(total[head, :, ds], axis=0, keepdims=True)
                out = acc[rows, ds] * (1.0 / sums)
                ctx[cell, rows, ds] = out.astype(BF)
                ctx32[cell, rows, ds] = out
                logs[cell, pl.ds(head, 1), ds] = jnp.log(sums) + high


def attend(lens, qkv):
    length = qkv.shape[2]
    return pl.pallas_call(
        attend_kernel,
        name="attend",
        out_shape=(
            shape_of((2, 128, length), BF),
            shape_of((2, 128, length), F32),
            shape_of((2, 2, length), F32),
        ),
        in_specs=[SMEM_SPEC, VMEM_SPEC],
        out_specs=[VMEM_SPEC] * 3,
        scratch_shapes=[
            pltpu.VMEM((length, 128 + EXT), BF),
            pltpu.VMEM((length // 256, 256, 512), F32),
            pltpu.VMEM((2, 8, length), F32),
            pltpu.VMEM((128, length), F32),
        ],
        compiler_params=params(),
    )(lens, qkv)


def in_three(x):
    high = x.astype(BF)
    rest = x - high.astype(F32)
    middle = rest.astype(BF)
    return high, middle, (rest - middle.astype(F32)).astype(BF)


def attend_back_kernel(
    has_done, lens, qkv, grad, ctx32, logs, xs, *refs
):
    if has_done:
        done, (out, dwqkv, dvec, placed), refs = refs[0], refs[1:5], refs[5:]
    else:
        (out, dwqkv, dvec), refs = refs[:3], refs[3:]
    right_s, right_d, sum_q, sum_k, sum_v, sums = refs[:6]
    if has_done:
        place = pltpu.make_async_copy(done, placed, refs[6])
        place.start()
    length = qkv.shape[2]
    wide = 512
    row = lax.broadcasted_iota(jnp.int32, (EXT, wide), 0)

    def left(x, head, value, last):
        a, b, c = in_three(value)
        zero = jnp.zeros((EXT, wide), BF)
        extra = jnp.where(row == 0, a, jnp.where(row == 1, b, jnp.where(row == 2, c, zero)))
        if last:
            extra = jnp.where(row == 3, jnp.ones_like(zero), extra)
        return jnp.transpose(extended(one_head(x, head), extra))

    dwqkv[...] = jnp.zeros_like(dwqkv)
    sums[...] = jnp.zeros_like(sums)

    @pl.loop(0, 2)
    def _(cell):
        valid = lens[cell, 0, 0]
        for ref in (sum_q, sum_k, sum_v):
            ref[...] = jnp.zeros_like(ref)
        where = lax.broadcasted_iota(jnp.int32, (EXT, length), 1)
        rows = lax.broadcasted_iota(jnp.int32, (EXT, length), 0)
        extra = jnp.where(
            rows < 3, 1.0, jnp.where((rows == 3) & (where >= valid), NEG, 0.0)
        ).astype(BF)
        right_s[0:128], right_s[128:] = qkv[cell, 128:256], extra
        right_d[0:128], right_d[128:] = qkv[cell, 256:384], extra

        def step(start, size):
            keys = pl.ds(start, size)

            @pl.loop(0, pl.cdiv(valid, wide))
            def _(i):
                ds = pl.ds(pl.multiple_of(i * wide, wide), wide)
                q = qkv[cell, 0:128, ds]
                d = grad[cell, :, ds]
                inner = d.astype(F32) * ctx32[cell, :, ds]
                for head in range(2):
                    at = slice(HEAD * head, HEAD * head + HEAD)
                    delta = jnp.sum(inner[at], axis=0, keepdims=True)
                    log_total = logs[cell, head : head + 1, ds]
                    s = dot(left(q, head, -log_total, True), right_s[:, keys], 1, 0)
                    p = jnp.exp(s)
                    dp = dot(left(d, head, -delta, False), right_d[:, keys], 1, 0)
                    ds_low = (p * dp).astype(BF)
                    sum_v[at, keys] += dot(d[at], p.astype(BF), 1, 0)
                    sum_k[at, keys] += dot(q[at], ds_low, 1, 0)
                    k = qkv[cell, 128 + HEAD * head : 192 + HEAD * head, keys]
                    sum_q[at, ds] += dot(k, ds_low, 1, 1)

        over_keys(valid, step)
        out[cell, 0:128] = (sum_q[...] * 0.125).astype(BF)
        out[cell, 128:256] = sum_k[...].astype(BF)
        out[cell, 256:384] = sum_v[...].astype(BF)
        dwqkv[...] += dot(out[cell], xs[cell], 1, 0)
        sums[0:128] += fold_lanes(out[cell, 0:128].astype(F32))
        sums[128:256] += fold_lanes(out[cell, 256:384].astype(F32))

    lane = lax.broadcasted_iota(jnp.int32, (128, 128), 1)
    q_sum = jnp.sum(sums[0:128], axis=1, keepdims=True)
    v_sum = jnp.sum(sums[128:256], axis=1, keepdims=True)
    dvec[...] = jnp.where(lane == QB, q_sum, jnp.where(lane == VB, v_sum, 0.0))
    if has_done:
        place.wait()


def attend_back(lens, qkv, grad, ctx32, logs, xs, *done):
    length = qkv.shape[2]
    return pl.pallas_call(
        functools.partial(attend_back_kernel, bool(done)),
        name="attend_back",
        out_shape=(
            shape_of((2, 384, length), BF),
            shape_of((384, 256), F32),
            shape_of((128, 128), F32),
        )
        + tuple(shape_of(a.shape, a.dtype) for a in done),
        in_specs=[SMEM_SPEC] + [VMEM_SPEC] * (5 + len(done)),
        out_specs=[VMEM_SPEC] * 3 + [HBM_SPEC] * len(done),
        scratch_shapes=[
            pltpu.VMEM((128 + EXT, length), BF),
            pltpu.VMEM((128 + EXT, length), BF),
            pltpu.VMEM((128, length), F32),
            pltpu.VMEM((128, length), F32),
            pltpu.VMEM((128, length), F32),
            pltpu.VMEM((256, 128), F32),
        ]
        + [pltpu.SemaphoreType.DMA] * len(done),
        compiler_params=params(),
    )(lens, qkv, grad, ctx32, logs, xs, *done)


BLOCK = 1024


def block_of(i):
    return pl.ds(pl.multiple_of(i * BLOCK, BLOCK), BLOCK)


def pair_semaphores(count):
    return [pltpu.SemaphoreType.DMA((count,)), pltpu.SemaphoreType.DMA((count,))]


def between_kernel(
    ctx, x_ref, wqkv, wo, wup, wdn, cols_ref,
    x_out, ctx_out, unit1, hidden, unit2, scales, qkv, lows,
    landed, out, send, recv,
):
    cols, cols_next = cols_ref.at[0], cols_ref.at[1]
    count = x_out.shape[1] // BLOCK
    core, peer = pair_of()

    def arrival(i):
        ds, j = block_of(i), 2 * count + i
        return to_peer(ctx.at[1, :, ds], landed.at[:, ds], send.at[j], recv.at[j], peer)

    def low_copy(i):
        ds, j = block_of(i), count + i
        return to_peer(lows.at[0, ds], lows.at[1, ds], send.at[j], recv.at[j], peer)

    def copy(i):
        ds = block_of(i)
        return to_peer(out.at[:, ds], qkv.at[1, :, ds], send.at[i], recv.at[i], peer)

    greet(peer)

    @pl.loop(0, count)
    def _(i):
        arrival(i).start()

    @pl.loop(0, count)
    def _(i):
        ds = block_of(i)
        x = jnp.transpose(x_ref[0, ds].astype(F32))
        arrival(i).wait()
        context = join(core, ctx[0, :, ds], landed[:, ds])
        ctx_out[:, ds] = context
        one, scale1, hid, two, scale2, x_next = forward_block(
            context, x, wo[0], wup[...], wdn[...], cols
        )
        unit1[:, ds], hidden[:, ds], unit2[:, ds] = one, hid, two
        scales[0:1, ds], scales[1:2, ds] = scale1, scale2
        x_out[:, ds] = x_next
        low = x_next.astype(BF)
        lows[0, ds] = jnp.transpose(low)
        low_copy(i).start()
        out[:, ds] = project(low, 0, wqkv, cols_next, 1 - core, 1)
        copy(i).start()
        qkv[0, :, ds] = project(low, 0, wqkv, cols_next, core, 1)

    @pl.loop(0, count)
    def _(i):
        low_copy(i).wait()
        copy(i).wait()


def between(ctx, cells, wqkv, wo, wup, wdn, cols):
    length = ctx.shape[2]
    shapes = (
        shape_of((256, length), F32),
        shape_of((256, length), BF),
        shape_of((256, length), F32),
        shape_of((512, length), F32),
        shape_of((256, length), F32),
        shape_of((8, length), F32),
        shape_of((2, 384, length), BF),
        shape_of((2, length, 256), BF),
    )
    return pl.pallas_call(
        between_kernel,
        name="between_layers",
        out_shape=shapes,
        in_specs=[VMEM_SPEC] * 7,
        out_specs=[VMEM_SPEC] * len(shapes),
        scratch_shapes=[
            pltpu.VMEM((128, length), BF),
            pltpu.VMEM((384, length), BF),
        ]
        + pair_semaphores(3 * length // BLOCK),
        compiler_params=params(3),
    )(ctx, cells, wqkv, wo, wup, wdn, cols)


def turn_kernel(direct, lens, ctx, x_ref, cot, wo, cols_ref, *refs):
    if direct:
        end, refs = refs[0], refs[1:]
    else:
        (wup, wdn), refs = refs[:2], refs[2:]
    cells_out, d_first, dctx, dwo, dwup, dwdn, dvec = refs[:7]
    landed, sums, out, grad, send, recv = refs[7:13]
    if direct:
        wup, wdn = refs[13:]
    cols = cols_ref.at[1]
    count = x_ref.shape[1] // BLOCK
    core, peer = pair_of()

    def arrival(i):
        ds, j = block_of(i), count + i
        return to_peer(ctx.at[1, :, ds], landed.at[:, ds], send.at[j], recv.at[j], peer)

    def copy(i):
        ds = block_of(i)
        return to_peer(out.at[:, ds], dctx.at[1, :, ds], send.at[i], recv.at[i], peer)

    hail([peer])
    if direct:
        unpack_feed_forward(end, 64, wup, wdn)
    await_hails([peer])

    @pl.loop(0, count)
    def _(i):
        arrival(i).start()

    for ref in (sums, dwo, dwup, dwdn):
        ref[...] = jnp.zeros_like(ref)

    @pl.loop(0, count)
    def _(i):
        ds = block_of(i)
        where = lax.broadcasted_iota(jnp.int32, (1, BLOCK), 1) + i * BLOCK
        valid = jnp.where(where < tile_lanes(lens[0, 0:1], BLOCK), 1.0, 0.0)
        grad[:, ds] = jnp.transpose(cot[0, ds].astype(F32)) * valid

    @pl.loop(0, count)
    def _(i):
        ds = block_of(i)
        arrival(i).wait()
        context = join(core, ctx[0, :, ds], landed[:, ds])
        weights = (wo[1], wup[...], wdn[...])
        unit1, scale1, hidden, unit2, scale2, x_next = forward_block(
            context, x_ref[:, ds], *weights, cols
        )
        cells_out[0, ds] = jnp.transpose(x_next).astype(BF)
        saved = (unit1, scale1, gelu_parts(hidden), unit2, scale2)
        d_first[:, ds], d_context = backward_block(
            grad[:, ds], context, saved, weights, cols, sums, dwo, dwup, dwdn
        )
        low, high = d_context[:128], d_context[128:]
        out[:, ds] = jnp.where(core == 0, high, low)
        copy(i).start()
        dctx[0, :, ds] = jnp.where(core == 0, low, high)

    dvec[...] = place_vectors(sums)

    @pl.loop(0, count)
    def _(i):
        copy(i).wait()


GRAD_SHAPES = ((256, 256), (512, 256), (256, 512), (256, 128))


def turn(direct, lens, ctx, x, cot, wo, cols, feed_forward):
    length = ctx.shape[2]
    shapes = (
        shape_of((1, length, 256), BF),
        shape_of((256, length), F32),
        shape_of((2, 128, length), BF),
    ) + tuple(shape_of(s, F32) for s in GRAD_SHAPES)
    return pl.pallas_call(
        functools.partial(turn_kernel, direct),
        name="turn",
        out_shape=shapes,
        in_specs=[VMEM_SPEC] * (6 + len(feed_forward)),
        out_specs=[VMEM_SPEC] * len(shapes),
        scratch_shapes=[
            pltpu.VMEM((128, length), BF),
            pltpu.VMEM((2560, 128), F32),
            pltpu.VMEM((128, length), BF),
            pltpu.VMEM((256, length), F32),
        ]
        + pair_semaphores(2 * length // BLOCK)
        + ([pltpu.VMEM((512, 256), BF), pltpu.VMEM((256, 512), BF)] if direct else []),
        compiler_params=params(4, 18),
    )(lens, ctx, x, cot, wo, cols, *feed_forward)


OUTER, INNER = 48, 32


def shares(x):
    return x.reshape(32, x.shape[0] // 32, 256)


def vector_shares(vec):
    high = vec.astype(BF).astype(F32)
    return shares(jnp.concatenate([high, vec - high], axis=1))


def outer_shares(dwo, dwup, dwdn, dvec):
    return [
        shares(dwo[...]),
        shares(dwdn[:, 0:256]),
        shares(dwdn[:, 256:512]),
        vector_shares(dvec[...]),
        shares(dwup[...]),
    ]


def reduce_scratch(rows):
    return [
        pltpu.VMEM((2, 4, 4, rows, 256), BF),
        pltpu.VMEM((4, 4, rows, 256), BF),
        pltpu.VMEM((4, 4, rows, 256), BF),
        pltpu.VMEM((3, 4, rows, 256), BF),
        pltpu.VMEM((4, rows, 256), BF),
        pltpu.VMEM((3, rows, 256), BF),
        pltpu.SemaphoreType.DMA((7,)),
        pltpu.SemaphoreType.DMA((7,)),
    ]


REDUCE_REFS = 8


class Reduce:
    def __init__(self, own, from_core, by_plane, from_plane, by_line, from_line, send, recv):
        self.refs = own, from_core, by_plane, from_plane, by_line, from_line
        z, x, y, core = coordinates()
        self.z, self.number, self.core = z, 2 * x + y, core

        def copy(src, dst, i, device):
            return pltpu.make_async_remote_copy(
                src_ref=src,
                dst_ref=dst,
                send_sem=send.at[i],
                recv_sem=recv.at[i],
                device_id=device,
                device_id_type=MESH,
            )

        self.cores = [copy(own.at[1 - core], from_core, 0, sibling())]
        self.plane = [
            copy(by_plane.at[number], from_plane.at[i], 1 + i, device)
            for i, (device, number) in enumerate(plane_mates())
        ]
        self.line = [
            copy(by_line.at[there], from_line.at[i], 4 + i, device)
            for i, (device, there) in enumerate(line_mates())
        ]

    def fill(self, pieces):
        own = self.refs[0]
        rows = own.shape[3]
        terms = jnp.concatenate(pieces, axis=1).astype(BF).reshape(4, 4, 2, rows, 256)
        for core in range(2):
            for plane in range(4):
                own[core, plane] = terms[:, plane, core]

    def first(self):
        for c in self.cores:
            c.start()

    def second(self):
        own, from_core, by_plane = self.refs[:3]
        for c in self.cores:
            c.wait()
        by_plane[...] = (own[self.core].astype(F32) + from_core[...].astype(F32)).astype(BF)
        for c in self.plane:
            c.start()

    def third(self):
        by_plane, from_plane, by_line = self.refs[2:5]
        for c in self.plane:
            c.wait()
        total = by_plane[self.number].astype(F32)
        for i in range(3):
            total = total + from_plane[i].astype(F32)
        by_line[...] = total.astype(BF)
        for c in self.line:
            c.start()

    def result(self):
        by_line, from_line = self.refs[4:6]
        for c in self.line:
            c.wait()
        total = by_line[self.z].astype(F32)
        for i in range(3):
            total = total + from_line[i].astype(F32)
        return total


def reduce_half_scratch(rows):
    return [
        pltpu.VMEM((4, 4, rows, 256), BF),
        pltpu.VMEM((3, 4, rows, 256), BF),
        pltpu.VMEM((4, rows, 256), BF),
        pltpu.VMEM((4, rows, 256), BF),
        pltpu.SemaphoreType.DMA((7,)),
        pltpu.SemaphoreType.DMA((7,)),
    ]


HALF_REFS = 6


class ReduceHalf:
    def __init__(self, own, from_plane, by_line, from_line, send, recv):
        self.refs = own, from_plane, by_line, from_line
        z, x, y, core = coordinates()
        self.number = 2 * x + y

        def copy(src, dst, i, j, device):
            return pltpu.make_async_remote_copy(
                src_ref=src,
                dst_ref=dst,
                send_sem=send.at[i],
                recv_sem=recv.at[j],
                device_id=device,
                device_id_type=MESH,
            )

        self.plane = [
            copy(own.at[number], from_plane.at[i], i, i, device)
            for i, (device, number) in enumerate(plane_mates())
        ]
        self.line, self.mine = [], []
        for block in range(4):
            there, owner = 2 * core + block // 2, block % 2
            device = device_at(there, x, y, owner)
            self.line.append(copy(by_line.at[block], from_line.at[z], 3 + block, 3 + z, device))
            self.mine.append((there == z) & (owner == core))
        self.arrivals = []
        for there in range(4):
            arrival = copy(by_line.at[0], from_line.at[there], 3, 3 + there, sibling())
            self.arrivals.append((arrival, (there == z) & (z // 2 == core)))

    def fill(self, dwqkv, dvec):
        own = self.refs[0]
        rows = own.shape[2]

        def pieces(x):
            return x.reshape(16, 8, 256)

        terms = [pieces(dwqkv[128 * j : 128 * j + 128]) for j in range(3)]
        vec = dvec[...]
        high = vec.astype(BF).astype(F32)
        terms.append(pieces(jnp.concatenate([high, vec - high], axis=1)))
        terms = jnp.concatenate(terms, axis=1).astype(BF).reshape(2, 4, 2, rows, 256)
        for plane in range(4):
            own[plane] = terms[:, plane].reshape(4, rows, 256)

    def first(self):
        for c in self.plane:
            c.start()

    def second(self):
        own, from_plane, by_line, from_line = self.refs
        z = lax.axis_index("wide") // 2
        for c in self.plane:
            c.wait()
        total = own[self.number].astype(F32)
        for i in range(3):
            total = total + from_plane[i].astype(F32)
        by_line[...] = total.astype(BF)
        for block in range(4):

            @pl.when(jnp.logical_not(self.mine[block]))
            def _(block=block):
                self.line[block].start()

            @pl.when(self.mine[block])
            def _(block=block):
                from_line[z] = by_line[block]

    def result(self):
        from_line = self.refs[3]
        for arrival, mine in self.arrivals:
            pl.when(jnp.logical_not(mine))(arrival.wait_recv)
        for copy, mine in zip(self.line, self.mine):
            pl.when(jnp.logical_not(mine))(copy.wait_send)
        total = from_line[0].astype(F32)
        for i in range(1, 4):
            total = total + from_line[i].astype(F32)
        return total


def project_back(half, part, w_ref, layer):
    rows = jnp.concatenate([half_rows(w_ref, layer, 256 * j, half) for j in range(3)], axis=0)
    return dot(rows, part, 0, 0)


def middle_kernel(direct, *refs):
    dqkv, d_first_in, wqkv, ctx, unit1, hidden, unit2, scales, wo, wup, wdn, cols_ref = refs[:12]
    cols = cols_ref.at[0]
    refs = refs[12:]
    if direct:
        outer, inner, refs = refs[:4], refs[4:6], refs[6:]
    d_first, dctx, dwo, dwup, dwdn, dvec = refs[:6]
    refs = refs[6:]
    if direct:
        (sums_outer, sums_inner), refs = refs[:2], refs[2:]
    landed, sums, out, active, slope, send, recv = refs[:7]
    refs = refs[7:]
    count = d_first.shape[1] // BLOCK
    core, peer = pair_of()

    def arrival(i):
        ds, j = block_of(i), count + i
        return to_peer(dqkv.at[1, :, ds], landed.at[:, ds], send.at[j], recv.at[j], peer)

    def copy(i):
        ds = block_of(i)
        return to_peer(out.at[:, ds], dctx.at[1, :, ds], send.at[i], recv.at[i], peer)

    mates = gather_mates() + column_mates() if direct else [peer]
    hail(mates)
    if direct:
        two = ReduceHalf(*refs[:HALF_REFS])
        one = Reduce(*refs[HALF_REFS:])
        one.fill(outer_shares(*outer))
        two.fill(*inner)
    await_hails(mates)
    if direct:
        one.first()
        two.first()

    @pl.loop(0, count)
    def _(i):
        arrival(i).start()

    for ref in (sums, dwo, dwup, dwdn):
        ref[...] = jnp.zeros_like(ref)

    @pl.loop(0, count)
    def _(i):
        ds = block_of(i)
        active[:, ds], slope[:, ds] = gelu_parts(hidden[:, ds])

    if direct:
        one.second()

    @pl.loop(0, count)
    def _(i):
        if direct:

            @pl.when(i == 1)
            def _():
                two.second()
                one.third()

        ds = block_of(i)
        g = d_first_in[:, ds] + project_back(core, dqkv[0, :, ds], wqkv, 1)
        arrival(i).wait()
        g = g + project_back(1 - core, landed[:, ds], wqkv, 1)
        gelu = (active[:, ds], slope[:, ds])
        saved = (unit1[:, ds], scales[0:1, ds], gelu, unit2[:, ds], scales[1:2, ds])
        d_first[:, ds], d_context = backward_block(
            g, ctx[:, ds], saved, (wo[0], wup[...], wdn[...]), cols, sums, dwo, dwup, dwdn
        )
        low, high = d_context[:128], d_context[128:]
        out[:, ds] = jnp.where(core == 0, high, low)
        copy(i).start()
        dctx[0, :, ds] = jnp.where(core == 0, low, high)

    dvec[...] = place_vectors(sums)
    if direct:
        sums_inner[...] = two.result()
        sums_outer[...] = one.result()

    @pl.loop(0, count)
    def _(i):
        copy(i).wait()


def middle(direct, dqkv, d_first, wqkv, ctx, unit1, hidden, unit2, scales, wo, wup, wdn, cols, outer, inner):
    length = d_first.shape[1]
    terms = (*outer, *inner) if direct else ()
    shapes = (shape_of((256, length), F32), shape_of((2, 128, length), BF))
    shapes += tuple(shape_of(s, F32) for s in GRAD_SHAPES)
    if direct:
        shapes += (shape_of((OUTER, 256), F32), shape_of((INNER, 256), F32))
    return pl.pallas_call(
        functools.partial(middle_kernel, direct),
        name="back_between",
        out_shape=shapes,
        in_specs=[VMEM_SPEC] * (12 + len(terms)),
        out_specs=[VMEM_SPEC] * len(shapes),
        scratch_shapes=[
            pltpu.VMEM((384, length), BF),
            pltpu.VMEM((2560, 128), F32),
            pltpu.VMEM((128, length), BF),
            pltpu.VMEM((512, length), BF),
            pltpu.VMEM((512, length), F32),
        ]
        + pair_semaphores(2 * length // BLOCK)
        + (reduce_half_scratch(INNER) + reduce_scratch(OUTER) if direct else []),
        compiler_params=params(5, 18),
    )(dqkv, d_first, wqkv, ctx, unit1, hidden, unit2, scales, wo, wup, wdn, cols, *terms)


def last_kernel(direct, *refs):
    dqkv, d_first, wqkv = refs[:3]
    refs = refs[3:]
    if direct:
        outer, inner, (grad_out, sums_outer, sums_inner) = refs[:4], refs[4:6], refs[6:9]
        refs = refs[9:]
    else:
        grad_out, refs = refs[0], refs[1:]
    landed, grad, send, recv = refs[:4]
    refs = refs[4:]
    count = d_first.shape[1] // BLOCK
    core, peer = pair_of()

    def arrival(i):
        ds = block_of(i)
        return to_peer(dqkv.at[1, :, ds], landed.at[:, ds], send.at[i], recv.at[i], peer)

    mates = gather_mates() + column_mates() if direct else [peer]
    hail(mates)
    if direct:
        two = ReduceHalf(*refs[:HALF_REFS])
        one = Reduce(*refs[HALF_REFS:])
        one.fill(outer_shares(*outer))
        two.fill(*inner)
    await_hails(mates)
    if direct:
        one.first()
        two.first()

    @pl.loop(0, count)
    def _(i):
        arrival(i).start()

    @pl.loop(0, count)
    def _(i):
        ds = block_of(i)
        grad[:, ds] = d_first[:, ds] + project_back(core, dqkv[0, :, ds], wqkv, 0)

    if direct:
        one.second()

    @pl.loop(0, count)
    def _(i):
        if direct:
            pl.when(i == 1)(two.second)
        ds = block_of(i)
        arrival(i).wait()
        g = grad[:, ds] + project_back(1 - core, landed[:, ds], wqkv, 0)
        grad_out[0, ds] = jnp.transpose(g)

    if direct:
        one.third()
        sums_inner[...] = two.result()
        sums_outer[...] = one.result()


def last(direct, dqkv, d_first, wqkv, outer, inner):
    length = d_first.shape[1]
    terms = (*outer, *inner) if direct else ()
    shapes = (shape_of((1, length, 256), F32),)
    if direct:
        shapes += (shape_of((OUTER, 256), F32), shape_of((INNER, 256), F32))
    return pl.pallas_call(
        functools.partial(last_kernel, direct),
        name="back_input",
        out_shape=shapes,
        in_specs=[VMEM_SPEC] * (3 + len(terms)),
        out_specs=[VMEM_SPEC] * len(shapes),
        scratch_shapes=[
            pltpu.VMEM((384, length), BF),
            pltpu.VMEM((256, length), F32),
        ]
        + pair_semaphores(length // BLOCK)
        + (reduce_half_scratch(INNER) + reduce_scratch(OUTER) if direct else []),
        compiler_params=params(6),
    )(dqkv, d_first, wqkv, *terms)


def finish_kernel(factor, outer1, inner1, outer0, inner0, grad, *refs):
    qw, qb, kw, vw, vb, ow, ob, g1, s1, uw, ub, dw, db, g2, s2, placed, place_sem = refs
    place = pltpu.make_async_copy(grad, placed, place_sem)
    place.start()
    layers = (
        (inner0[...] * factor, outer0[...] * factor),
        (inner1[...] * factor, outer1[...] * factor),
    )
    for layer, (inner, outer) in enumerate(layers):
        qw[layer], kw[layer], vw[layer] = inner[0:8], inner[8:16], inner[16:24]
        ow[layer] = outer[0:8]
        dw[layer, :, 0:256], dw[layer, :, 256:512] = outer[8:16], outer[16:24]
        uw[layer] = outer[32:48]
        vec = inner[24:32] + outer[24:32]
        vec = jnp.transpose(vec[:, 0:128] + vec[:, 128:256])
        for i, ref in enumerate((qb, vb, ob, g1, s1, db, g2, s2)):
            ref[layer : layer + 1] = vec[i : i + 1]
        ub[layer : layer + 1, 0:8] = vec[8:9]
        ub[layer : layer + 1, 8:16] = vec[9:10]
    place.wait()


def finish(factor, sums, grad, like):
    found = pl.pallas_call(
        functools.partial(finish_kernel, factor),
        name="finish",
        out_shape=tuple(shape_of(a.shape, F32) for a in (*like, grad)),
        in_specs=[VMEM_SPEC] * 5,
        out_specs=[VMEM_SPEC] * len(like) + [HBM_SPEC],
        scratch_shapes=[pltpu.SemaphoreType.DMA],
        compiler_params=params(),
    )(*sums, grad)
    *found, grad = found
    return grad, [jnp.swapaxes(a, 1, 2) if a.ndim == 3 else a for a in found]


def gather_by_collectives(weights, vectors):
    def whole_of(w):
        return lax.all_gather(w, AXES, axis=1, tiled=True)

    qw, kw, vw, ow, uw, dw = (whole_of(w) for w in weights)
    columns = [lax.all_gather(v, AXES, axis=1, tiled=True).astype(F32) for v in vectors]
    up = columns.pop().reshape(2, 32, 2, 8)
    columns += [up[:, :, 0].reshape(2, 256), up[:, :, 1].reshape(2, 256)]
    lanes = jnp.stack(columns).transpose(2, 0, 1).reshape(256, 20)
    vec = jnp.pad(lanes, ((0, 0), (0, 108)))
    return jnp.concatenate([qw, kw, vw], axis=1), ow, uw, dw, vec


def sum_by_collectives(factor, layers):
    def share(x):
        return lax.psum_scatter(x, AXES, scatter_dimension=0, tiled=True) * factor

    found = []
    core = lax.rem(lax.axis_index("narrow"), 2)

    def widen(x):
        parts = x.reshape(-1, 1, 128, x.shape[1])
        mine = (jnp.arange(2) == core)[None, :, None, None]
        return jnp.where(mine, parts, 0.0).reshape(-1, x.shape[1])

    for dwqkv, dvec_qkv, dwo, dwup, dwdn, dvec in layers:
        dwqkv = widen(dwqkv)
        vec = widen(dvec_qkv) + dvec
        qb, vb, ob, g1, s1, db, g2, s2 = (share(vec[:, i]) for i in range(8))
        up = jnp.stack([vec[:, 8].reshape(32, 8), vec[:, 9].reshape(32, 8)], axis=1)
        qw, kw, vw = (share(dwqkv[256 * i : 256 * i + 256]).T for i in range(3))
        ow, uw, dw = share(dwo).T, share(dwup).T, share(dwdn).T
        ub = share(up.reshape(512))
        found.append((qw, qb, kw, vw, vb, ow, ob, g1, s1, uw, ub, dw, db, g2, s2))
    return [jnp.stack(pair) for pair in zip(*found)]


def on_device(devices, direct, cells_in, lengths, cotangent, *weights):
    qw, qb, kw, vw, vb, ow, ob, g1, s1, uw, ub, dw, db, g2, s2 = weights
    matrices, vectors = (qw, kw, vw, ow, uw, dw), (qb, vb, ob, g1, s1, db, g2, s2, ub)
    turned = [jnp.swapaxes(w, 1, 2) for w in matrices]
    if direct:
        share = own_share(lengths, turned, vectors)
        lens, qkv0, wqkv, wo, wup0, wdn0, cols, xs0, landed = start(share, cells_in)
        feed_forward = (landed,)
    else:
        wqkv, wo, wup, wdn, vec = gather_by_collectives(turned, vectors)
        wup0, wdn0, feed_forward = wup[0], wdn[0], (wup[1], wdn[1])
        cols = columns(vec)
        lens, qkv0, xs0 = project_first(lengths, cells_in, wqkv, cols)
    ctx_pair, ctx32_0, logs0 = attend(lens, qkv0)
    x1, ctx0, unit1, hidden, unit2, scales, qkv1, xs1 = between(
        ctx_pair, cells_in, wqkv, wo, wup0, wdn0, cols
    )
    ctx_pair, ctx32_1, logs1 = attend(lens, qkv1)
    cells_out, d_first, dctx, *outer1 = turn(
        direct, lens, ctx_pair, x1, cotangent, wo, cols, feed_forward
    )
    dqkv, *inner1, cells_out = attend_back(lens, qkv1, dctx, ctx32_1, logs1, xs1, cells_out)
    d_first, dctx, *found = middle(
        direct, dqkv, d_first, wqkv, ctx0, unit1, hidden, unit2, scales, wo, wup0, wdn0, cols, outer1, inner1
    )
    outer0, sums1 = found[:4], found[4:]
    dqkv, *inner0 = attend_back(lens, qkv0, dctx, ctx32_0, logs0, xs0)
    grad_in, *sums0 = last(direct, dqkv, d_first, wqkv, outer0, inner0)
    factor = 1.0 / math.sqrt(devices * cells_in.shape[0] * cells_in.shape[1])
    if direct:
        like = [shape_of(a.shape[:1] + a.shape[:0:-1], F32) for a in weights]
        grad_in, grads = finish(factor, (*sums1, *sums0), grad_in, like)
    else:
        grads = sum_by_collectives(factor, ((*inner0, *outer0), (*inner1, *outer1)))
    return (cells_out, grad_in, *grads)


def solution(mesh):
    devices = mesh.size
    direct = (mesh.shape["wide"], mesh.shape["narrow"]) == (8, 4)
    cell, vector, matrix = P(AXES, None, None), P(None, AXES), P(None, None, AXES)
    placed = (
        matrix, vector, matrix, matrix, vector, matrix, vector, vector, vector,
        matrix, vector, matrix, vector, vector, vector,
    )
    return jax.shard_map(
        functools.partial(on_device, devices, direct),
        mesh=mesh,
        in_specs=(cell, P(AXES), cell) + placed,
        out_specs=(cell, cell) + placed,
        check_vma=False,
    )
```

```python
import functools
import math

import jax
import jax.numpy as jnp
from jax import lax
from jax.experimental import pallas as pl
from jax.experimental.pallas import tpu as pltpu
from jax.sharding import PartitionSpec as P

HEAD = 64
NEG = -1000000000.0
EPS = 1e-06
AXES = ("wide", "narrow")
MESH = pl.DeviceIdType.MESH
BF = jnp.bfloat16
F32 = jnp.float32
EXT = 16
GUARD = 3600.0
KEY_SIZES = (512, 640, 768, 1024, 1280, 1536)
ROWS = 64
VMEM_SPEC = pl.BlockSpec(memory_space=pltpu.VMEM)
SMEM_SPEC = pl.BlockSpec(memory_space=pltpu.SMEM)
HBM_SPEC = pl.BlockSpec(memory_space=pltpu.HBM)
QB, VB, OB, G1, S1, DB, G2, S2, UB = range(9)


def dot(a, b, ca, cb):
    return lax.dot_general(a, b, (((ca,), (cb,)), ((), ())), preferred_element_type=F32)


def params(collective_id=None, limit=16):
    if collective_id is None:
        return pltpu.CompilerParams(vmem_limit_bytes=limit << 20)
    return pltpu.CompilerParams(
        vmem_limit_bytes=limit << 20, collective_id=collective_id, has_side_effects=True
    )


def shape_of(shape, dtype):
    return jax.ShapeDtypeStruct(shape, dtype)


def pair_of():
    narrow = lax.axis_index("narrow")
    core = lax.rem(narrow, 2)
    return core, (lax.axis_index("wide"), narrow + 1 - 2 * core)


def greet(peer):
    hail([peer])
    await_hails([peer])


def to_peer(src, dst, send, recv, peer):
    return pltpu.make_async_remote_copy(
        src_ref=src, dst_ref=dst, send_sem=send, recv_sem=recv, device_id=peer, device_id_type=MESH
    )


def half_rows(ref, layer, base, half):
    return ref[layer, pl.ds(pl.multiple_of(base + half * 128, 128), 128)]


def tile_lanes(column, count):
    return jnp.concatenate([column] * (count // 128), axis=1)


def spread(both, layer, cols_ref, names):
    def every_lane(i):
        return jnp.broadcast_to(both[:, 2 * i + layer : 2 * i + layer + 1], (256, 128))

    for i in names:
        if i < UB:
            cols_ref[pl.ds(i * 256, 256)] = every_lane(i)
        else:
            halves = [every_lane(j).reshape(32, 8, 128) for j in (UB, UB + 1)]
            cols_ref[pl.ds(i * 256, 512)] = jnp.concatenate(halves, axis=1).reshape(512, 128)


def columns_kernel(vec, cols):
    for layer in range(2):
        spread(vec[...], layer, cols.at[layer], range(9))


def columns(vec):
    return pl.pallas_call(
        columns_kernel,
        name="columns",
        out_shape=shape_of((2, 2560, 128), F32),
        in_specs=[VMEM_SPEC],
        out_specs=VMEM_SPEC,
        compiler_params=params(),
    )(vec)


def column(cols_ref, i, count):
    rows = 512 if i == UB else 256
    return tile_lanes(cols_ref[pl.ds(i * 256, rows)], count)


def fold_lanes(x):
    total = x[:, :128]
    for start in range(128, x.shape[1], 128):
        total = total + x[:, start : start + 128]
    return total


def norm(resid):
    offset = resid - jnp.mean(resid, axis=0, keepdims=True)
    scale = lax.rsqrt(jnp.mean(offset * offset, axis=0, keepdims=True) + EPS)
    return offset * scale, scale


def norm_back(grad, gain, unit, scale):
    q = grad * gain
    return (
        q - jnp.mean(q, axis=0, keepdims=True) - unit * jnp.mean(q * unit, axis=0, keepdims=True)
    ) * scale


GELU_C = 0.7978845608028654
GELU_A = 0.044715


def project(xb, contract, w_ref, cols_ref, half, layer=0):
    parts = []
    for i in range(3):
        y = dot(half_rows(w_ref, layer, i * 256, half), xb, 1, contract)
        if i != 1:
            bias = cols_ref[
                pl.ds(pl.multiple_of((QB if i == 0 else VB) * 256 + half * 128, 128), 128)
            ]
            y = y + tile_lanes(bias, y.shape[1])
        y = y.astype(BF)
        parts.append(y * jnp.asarray(0.125, BF) if i == 0 else y)
    return jnp.concatenate(parts, axis=0)


def join(core, own, peer):
    return jnp.concatenate(
        [jnp.where(core == 0, own, peer), jnp.where(core == 0, peer, own)], axis=0
    )


def forward_block(context, x, wo, wup, wdn, cols_ref):
    count = x.shape[1]
    unit1, scale1 = norm(x + dot(wo, context, 1, 0) + column(cols_ref, OB, count))
    middle = unit1 * column(cols_ref, G1, count) + column(cols_ref, S1, count)
    hidden = dot(wup, middle.astype(BF), 1, 0) + column(cols_ref, UB, count)
    t = jnp.tanh(hidden * (GELU_C + (GELU_C * GELU_A) * (hidden * hidden)))
    active = (0.5 * hidden * (1.0 + t)).astype(BF)
    unit2, scale2 = norm(middle + dot(wdn, active, 1, 0) + column(cols_ref, DB, count))
    x_next = unit2 * column(cols_ref, G2, count) + column(cols_ref, S2, count)
    return unit1, scale1, hidden, unit2, scale2, x_next


def gelu_parts(hidden):
    square = hidden * hidden
    t = jnp.tanh(hidden * (GELU_C + (GELU_C * GELU_A) * square))
    half, more = 0.5 * hidden, 1.0 + t
    slope = 0.5 * more + half * (1.0 - t * t) * (GELU_C + (3.0 * GELU_C * GELU_A) * square)
    return (half * more).astype(BF), slope


def backward_block(grad, context, saved, weights, cols_ref, sums, dwo, dwup, dwdn):
    unit1, scale1, (active, slope), unit2, scale2 = saved
    wo, wup, wdn = weights
    count = grad.shape[1]

    def add(i, x):
        rows = x.shape[0]
        sums[pl.ds(i * 256, rows)] += fold_lanes(x)

    add(S2, grad)
    add(G2, grad * unit2)
    d_second = norm_back(grad, column(cols_ref, G2, count), unit2, scale2)
    branch = d_second.astype(BF)
    add(DB, branch.astype(F32))
    d_hidden = (dot(wdn, branch, 0, 0) * slope).astype(BF)
    dwdn[...] += dot(branch, active, 1, 1)
    add(UB, d_hidden.astype(F32))
    middle = unit1 * column(cols_ref, G1, count) + column(cols_ref, S1, count)
    dwup[...] += dot(d_hidden, middle.astype(BF), 1, 1)
    d_middle = d_second + dot(wup, d_hidden, 0, 0)
    add(S1, d_middle)
    add(G1, d_middle * unit1)
    d_first = norm_back(d_middle, column(cols_ref, G1, count), unit1, scale1)
    attn = d_first.astype(BF)
    add(OB, attn.astype(F32))
    dwo[...] += dot(attn, context, 1, 1)
    return d_first, dot(wo, attn, 0, 0).astype(BF)


def place_vectors(sums):
    lane = lax.broadcasted_iota(jnp.int32, (256, 128), 1)
    out = jnp.zeros((256, 128), F32)
    for i in range(8):
        total = jnp.sum(sums[pl.ds(i * 256, 256)], axis=1, keepdims=True)
        out = jnp.where(lane == i, total, out)
    up = jnp.sum(sums[pl.ds(2048, 512)], axis=1, keepdims=True)
    up = jnp.broadcast_to(up, (512, 128)).reshape(32, 16, 128)
    out = jnp.where(lane == 8, up[:, :8].reshape(256, 128), out)
    return jnp.where(lane == 9, up[:, 8:].reshape(256, 128), out)


def coordinates():
    wide, narrow = lax.axis_index("wide"), lax.axis_index("narrow")
    return wide // 2, lax.rem(wide, 2), narrow // 2, lax.rem(narrow, 2)


def device_at(z, x, y, core):
    return (2 * z + x, 2 * y + core)


def plane_mates():
    z, x, y, core = coordinates()
    return [
        (device_at(z, a, b, core), 2 * a + b) for a, b in ((x, 1 - y), (1 - x, y), (1 - x, 1 - y))
    ]


def line_mates():
    z, x, y, core = coordinates()
    there = [lax.rem(z + j, 4) for j in (1, 2, 3)]
    return [(device_at(a, x, y, core), a) for a in there]


def sibling():
    z, x, y, core = coordinates()
    return device_at(z, x, y, 1 - core)


def column_mates():
    z, x, y, core = coordinates()
    return [device_at(there, x, y, 1 - core) for _, there in line_mates()]


def hail(mates):
    for mate in mates:
        pl.semaphore_signal(
            pltpu.get_barrier_semaphore(), inc=1, device_id=mate, device_id_type=MESH
        )


def await_hails(mates):
    pl.semaphore_wait(pltpu.get_barrier_semaphore(), len(mates))


def gather_mates():
    return [sibling()] + [d for d, _ in plane_mates()] + [d for d, _ in line_mates()]


FIRST, REST = 48, 96


SHARE = 80


def share_kernel(length, qw, kw, vw, ow, uw, dw, *refs):
    vectors, share = refs[:-1], refs[-1]
    for layer in range(2):
        for i, w in enumerate((qw, kw, vw, ow)):
            share[layer, 8 * i : 8 * i + 8] = w[layer]
        share[layer, 32:48] = uw[layer]
        share[layer, 48:56] = dw[layer, :, 0:256]
        share[layer, 56:64] = dw[layer, :, 256:512]
        share[layer, 64:80] = jnp.zeros((16, 256), BF)
        at = 0
        for v in vectors:
            share[layer, 64:65, at : at + v.shape[1]] = v[layer : layer + 1]
            at += v.shape[1]
        number = length[...].reshape(1, 1)
        share[layer, 64:65, at : at + 1] = (number // 256).astype(F32).astype(BF)
        share[layer, 64:65, at + 1 : at + 2] = (number % 256).astype(F32).astype(BF)


def own_share(lengths, weights, vectors):
    return pl.pallas_call(
        share_kernel,
        name="own_share",
        out_shape=shape_of((2, SHARE, 256), BF),
        in_specs=[VMEM_SPEC] * 16,
        out_specs=VMEM_SPEC,
        compiler_params=params(limit=60),
    )(lengths, *weights, *vectors)


def pack_own(share, first, rest, flat):
    flat[...] = jnp.zeros_like(flat)
    for layer in range(2):
        row = share[layer, 64:80].astype(F32)[0:1]
        for i in range(10):
            at = 2 * i + layer
            flat[at : at + 1, 0:8] = row[:, 8 * i : 8 * i + 8]
    columns = jnp.transpose(flat[...])[0:8]
    block = jnp.concatenate([columns, jnp.zeros_like(columns)], axis=1)
    first[0:32] = share[0, 0:32]
    first[32:48] = jnp.concatenate([block, jnp.zeros_like(block)], axis=0).astype(BF)
    rest[0:32] = share[0, 32:64]
    rest[32:96] = share[1, 0:64]


def ordered(landed, at, rows):
    pieces = [
        landed[core, plane, z, at : at + rows]
        for z in range(4)
        for plane in range(4)
        for core in range(2)
    ]
    return jnp.stack(pieces)


def two_matrices(landed, at):
    pair = ordered(landed, at, 16).astype(F32)
    return (
        pair[:, :8].reshape(256, 256).astype(BF),
        pair[:, 8:].reshape(256, 256).astype(BF),
    )


def unpack_first(landed, wqkv, wo, both):
    wqkv[0, 0:256], wqkv[0, 256:512] = two_matrices(landed, 0)
    wqkv[0, 512:768], wo[0] = two_matrices(landed, 16)
    both[...] = ordered(landed, 32, 16).astype(F32)[:, :8, :128].reshape(256, 128)


def unpack_feed_forward(landed, at, up, down):
    up[...] = ordered(landed, at, 16).reshape(512, 256)
    down[:, 0:256], down[:, 256:512] = two_matrices(landed, at + 16)


def unpack_rest(landed, wqkv, wo, up, down):
    unpack_feed_forward(landed, 0, up, down)
    wqkv[1, 0:256], wqkv[1, 256:512] = two_matrices(landed, 32)
    wqkv[1, 512:768], wo[1] = two_matrices(landed, 48)


class Gather:
    def __init__(self, own, landed, send, recv, part):
        z, x, y, core = coordinates()
        plane = 2 * x + y

        def copy(src, dst, i, device):
            return pltpu.make_async_remote_copy(
                src_ref=src,
                dst_ref=dst,
                send_sem=send.at[part, i],
                recv_sem=recv.at[part, i],
                device_id=device,
                device_id_type=MESH,
            )

        def column(i):
            return landed.at[core, i]

        self.keep = lambda: landed.at[core, plane, z].__setitem__(Ellipsis, own[...])
        self.line = [
            copy(own, landed.at[core, plane, z], i, device)
            for i, (device, _) in enumerate(line_mates())
        ]
        self.plane = [
            copy(column(plane), column(plane), 3 + i, device)
            for i, (device, _) in enumerate(plane_mates())
        ]
        columns = [plane] + [number for _, number in plane_mates()]
        self.cores = [
            copy(column(number), column(number), 6 + i, sibling())
            for i, number in enumerate(columns)
        ]


def start_kernel(
    share, x_ref,
    lens, qkv, wqkv, wo, wup, wdn, cols, xs, landed_rest,
    first, rest, flat, landed_first, both, out, own_len, send, recv, pair_send, pair_recv, x_sems,
):
    core, peer = pair_of()
    mates = gather_mates()
    hail(mates)
    pack_own(share, first, rest, flat)
    number = share[0, 64:80].astype(F32)[0:1]
    number = number[:, 80:81] * 256.0 + number[:, 81:82]
    own_len[...] = jnp.broadcast_to(number, own_len.shape).astype(jnp.int32)
    a = Gather(first, landed_first, send, recv, 0)
    b = Gather(rest, landed_rest, send, recv, 1)
    await_hails(mates)
    for c in a.line + b.line:
        c.start()
    len_copy = to_peer(own_len, lens.at[1], pair_send.at[0], pair_recv.at[0], peer)
    len_copy.start()
    x_copy = to_peer(x_ref.at[0], xs.at[1], x_sems.at[0], x_sems.at[1], peer)
    x_copy.start()
    a.keep()
    b.keep()
    lens[0] = own_len[...]
    xs[0] = x_ref[0]
    for part in (a, b):
        for c in part.line:
            c.wait()
        for c in part.plane + part.cores[:1]:
            c.start()
    for i in range(3):
        a.plane[i].wait()
        a.cores[1 + i].start()
    for c in a.cores:
        c.wait()
    unpack_first(landed_first, wqkv, wo, both)
    spread(both[...], 0, cols.at[0], (QB, VB))
    block = 1024
    count = x_ref.shape[1] // block

    def copy(i):
        ds = pl.ds(pl.multiple_of(i * block, block), block)
        return to_peer(
            out.at[:, ds], qkv.at[1, :, ds], pair_send.at[1 + i], pair_recv.at[1 + i], peer
        )

    @pl.loop(0, count)
    def _(i):
        ds = pl.ds(pl.multiple_of(i * block, block), block)
        out[:, ds] = project(x_ref[0, ds], 1, wqkv, cols.at[0], 1 - core)
        copy(i).start()

    @pl.loop(0, count)
    def _(i):
        ds = pl.ds(pl.multiple_of(i * block, block), block)
        qkv[0, :, ds] = project(x_ref[0, ds], 1, wqkv, cols.at[0], core)

    spread(both[...], 0, cols.at[0], (OB, G1, S1, DB, G2, S2, UB))
    spread(both[...], 1, cols.at[1], range(9))
    for i in range(3):
        b.plane[i].wait()
        b.cores[1 + i].start()
    for c in b.cores:
        c.wait()
    unpack_rest(landed_rest, wqkv, wo, wup, wdn)
    len_copy.wait()
    x_copy.wait()

    @pl.loop(0, count)
    def _(i):
        copy(i).wait()


def start(share, cells):
    length = cells.shape[1]
    count = length // 1024
    return pl.pallas_call(
        start_kernel,
        name="gather_and_project",
        out_shape=(
            shape_of((2, 8, 128), jnp.int32),
            shape_of((2, 384, length), BF),
            shape_of((2, 768, 256), BF),
            shape_of((2, 256, 256), BF),
            shape_of((512, 256), BF),
            shape_of((256, 512), BF),
            shape_of((2, 2560, 128), F32),
            shape_of((2, length, 256), BF),
            shape_of((2, 4, 4, REST, 256), BF),
        ),
        in_specs=[VMEM_SPEC] * 2,
        out_specs=[VMEM_SPEC] * 9,
        scratch_shapes=[
            pltpu.VMEM((FIRST, 256), BF),
            pltpu.VMEM((REST, 256), BF),
            pltpu.VMEM((128, 128), F32),
            pltpu.VMEM((2, 4, 4, FIRST, 256), BF),
            pltpu.VMEM((256, 128), F32),
            pltpu.VMEM((384, length), BF),
            pltpu.VMEM((8, 128), jnp.int32),
            pltpu.SemaphoreType.DMA((2, 10)),
            pltpu.SemaphoreType.DMA((2, 10)),
            pltpu.SemaphoreType.DMA((count + 1,)),
            pltpu.SemaphoreType.DMA((count + 1,)),
            pltpu.SemaphoreType.DMA((2,)),
        ],
        compiler_params=params(1),
    )(share, cells)


def project_kernel(len_ref, x_ref, w_ref, cols_ref, lens, qkv, xs, out, own_len, send, recv):
    core, peer = pair_of()
    cols = cols_ref.at[0]
    own_len[...] = jnp.full(own_len.shape, len_ref[0], jnp.int32)
    greet(peer)
    len_copy = to_peer(own_len, lens.at[1], send.at[0], recv.at[0], peer)
    len_copy.start()
    lens[0] = own_len[...]
    x_copy = to_peer(x_ref.at[0], xs.at[1], send.at[2], recv.at[2], peer)
    x_copy.start()
    xs[0] = x_ref[0]
    out[...] = project(x_ref[0], 1, w_ref, cols, 1 - core)
    qkv_copy = to_peer(out, qkv.at[1], send.at[1], recv.at[1], peer)
    qkv_copy.start()
    qkv[0] = project(x_ref[0], 1, w_ref, cols, core)
    len_copy.wait()
    qkv_copy.wait()
    x_copy.wait()


def project_first(lengths, cells, wqkv, cols):
    length = cells.shape[1]
    return pl.pallas_call(
        project_kernel,
        name="project_first",
        out_shape=(
            shape_of((2, 8, 128), jnp.int32),
            shape_of((2, 384, length), BF),
            shape_of((2, length, 256), BF),
        ),
        in_specs=[SMEM_SPEC] + [VMEM_SPEC] * 3,
        out_specs=[VMEM_SPEC] * 3,
        scratch_shapes=[
            pltpu.VMEM((384, length), BF),
            pltpu.VMEM((8, 128), jnp.int32),
            pltpu.SemaphoreType.DMA((3,)),
            pltpu.SemaphoreType.DMA((3,)),
        ],
        compiler_params=params(2),
    )(lengths, cells, wqkv, cols)


def key_sizes(length):
    return [size for size in KEY_SIZES if size < length] + [length]


def extended(x, extra):
    return jnp.concatenate([x, extra], axis=0)


def one_head(x, head):
    row = lax.broadcasted_iota(jnp.int32, x.shape, 0)
    return jnp.where((row // HEAD) == head, x, jnp.zeros_like(x))


def attend_kernel(lens, qkv, ctx, ctx32, logs, kx, scores, total, acc):
    length = qkv.shape[2]

    def query_of(cell, i, head, wide):
        q = qkv[cell, 0:128, pl.ds(pl.multiple_of(i * wide, wide), wide)]
        row = lax.broadcasted_iota(jnp.int32, (EXT, wide), 0)
        return extended(one_head(q, head), jnp.where(row == 0, 1.0, 0.0).astype(BF))

    def finish(cell, i, head, wide, high, sums, out):
        ds = pl.ds(pl.multiple_of(i * wide, wide), wide)
        sums = jnp.sum(sums, axis=0, keepdims=True)
        out = out * (1.0 / sums)
        rows = slice(HEAD * head, HEAD * head + HEAD)
        ctx[cell, rows, ds] = out.astype(BF)
        ctx32[cell, rows, ds] = out
        logs[cell, head : head + 1, ds] = jnp.log(sums) + high

    def largest(x):
        x = x.astype(F32)
        square = x * x
        return [
            jnp.max(jnp.sum(square[HEAD * h : HEAD * h + HEAD], axis=0, keepdims=True))
            for h in range(2)
        ]

    @pl.loop(0, 2)
    def _(cell):
        valid = lens[cell, 0, 0]
        q_most = largest(qkv[cell, 0:128])
        k_most = largest(qkv[cell, 128:256])
        plain = jnp.maximum(q_most[0] * k_most[0], q_most[1] * k_most[1]) <= GUARD

        @pl.loop(0, jnp.minimum(pl.cdiv(valid, 256) + 1, length // 256))
        def _(i):
            ds = pl.ds(pl.multiple_of(i * 256, 256), 256)
            where = lax.broadcasted_iota(jnp.int32, (EXT, 256), 1) + i * 256
            first = lax.broadcasted_iota(jnp.int32, (EXT, 256), 0) == 0
            extra = jnp.where(first & (where >= valid), NEG, 0.0).astype(BF)
            kx[ds] = jnp.transpose(extended(qkv[cell, 128:256, ds], extra))

        sizes = key_sizes(length)
        for low, size in zip([0] + sizes[:-1], sizes):
            wide = next(w for w in (2048, 1024, 512) if w * size <= 1024 * 1024 or w == 512)
            wide = min(wide, length)

            @pl.when(plain & (valid > low) & (valid <= size))
            def _(size=size, wide=wide):
                @pl.loop(0, length // wide)
                def _(i):
                    for head in range(2):
                        s = dot(kx[0:size], query_of(cell, i, head, wide), 1, 0)
                        e = jnp.exp(s)
                        sums = jnp.sum(e.reshape(size // 8, 8, wide), axis=0)
                        v = qkv[cell, 256 + HEAD * head : 320 + HEAD * head, 0:size]
                        finish(cell, i, head, wide, 0.0, sums, dot(v, e.astype(BF), 1, 0))

        @pl.when(jnp.logical_not(plain))
        def _():
            chunks = pl.cdiv(valid, 256)
            wide = 512

            @pl.loop(0, length // wide)
            def _(i):
                for head in range(2):
                    query = query_of(cell, i, head, wide)

                    def score(j, high):
                        s = dot(kx[pl.ds(pl.multiple_of(j * 256, 256), 256)], query, 1, 0)
                        scores[j] = s
                        return jnp.maximum(high, jnp.max(s.reshape(32, 8, wide), axis=0))

                    high = lax.fori_loop(0, chunks, score, jnp.full((8, wide), NEG * 2, F32))
                    high = jnp.max(high, axis=0, keepdims=True)
                    acc[...] = jnp.zeros_like(acc)
                    total[...] = jnp.zeros_like(total)

                    @pl.loop(0, chunks)
                    def _(j):
                        e = jnp.exp(scores[j] - high)
                        total[...] += jnp.sum(e.reshape(32, 8, wide), axis=0)
                        v = qkv[
                            cell,
                            256 + HEAD * head : 320 + HEAD * head,
                            pl.ds(pl.multiple_of(j * 256, 256), 256),
                        ]
                        acc[...] += dot(v, e.astype(BF), 1, 0)

                    finish(cell, i, head, wide, high, total[...], acc[...])


def attend(lens, qkv):
    length = qkv.shape[2]
    return pl.pallas_call(
        attend_kernel,
        name="attend",
        out_shape=(
            shape_of((2, 128, length), BF),
            shape_of((2, 128, length), F32),
            shape_of((2, 2, length), F32),
        ),
        in_specs=[SMEM_SPEC, VMEM_SPEC],
        out_specs=[VMEM_SPEC] * 3,
        scratch_shapes=[
            pltpu.VMEM((length, 128 + EXT), BF),
            pltpu.VMEM((length // 256, 256, 512), F32),
            pltpu.VMEM((8, 512), F32),
            pltpu.VMEM((HEAD, 512), F32),
        ],
        compiler_params=params(),
    )(lens, qkv)


def in_three(x):
    high = x.astype(BF)
    rest = x - high.astype(F32)
    middle = rest.astype(BF)
    return high, middle, (rest - middle.astype(F32)).astype(BF)


def attend_back_kernel(
    has_done, lens, qkv, grad, ctx32, logs, xs, *refs
):
    if has_done:
        done, (out, dwqkv, dvec, placed), refs = refs[0], refs[1:5], refs[5:]
    else:
        (out, dwqkv, dvec), refs = refs[:3], refs[3:]
    right_s, right_d, sum_k, sum_v, sums = refs[:5]
    if has_done:
        place = pltpu.make_async_copy(done, placed, refs[5])
        place.start()
    length = qkv.shape[2]
    wide = 512
    row = lax.broadcasted_iota(jnp.int32, (EXT, wide), 0)

    def left(x, head, value, last):
        a, b, c = in_three(value)
        zero = jnp.zeros((EXT, wide), BF)
        extra = jnp.where(row == 0, a, jnp.where(row == 1, b, jnp.where(row == 2, c, zero)))
        if last:
            extra = jnp.where(row == 3, jnp.ones_like(zero), extra)
        return jnp.transpose(extended(one_head(x, head), extra))

    dwqkv[...] = jnp.zeros_like(dwqkv)
    sums[...] = jnp.zeros_like(sums)

    @pl.loop(0, 2)
    def _(cell):
        valid = lens[cell, 0, 0]
        out[cell] = jnp.zeros_like(out[cell])
        sizes = key_sizes(length)
        for low, size in zip([0] + sizes[:-1], sizes):

            @pl.when((valid > low) & (valid <= size))
            def _(size=size):
                where = lax.broadcasted_iota(jnp.int32, (EXT, size), 1)
                rows = lax.broadcasted_iota(jnp.int32, (EXT, size), 0)
                extra = jnp.where(
                    rows < 3, 1.0, jnp.where((rows == 3) & (where >= valid), NEG, 0.0)
                ).astype(BF)
                right_s[0:128, 0:size] = qkv[cell, 128:256, 0:size]
                right_s[128:, 0:size] = extra
                right_d[0:128, 0:size] = qkv[cell, 256:384, 0:size]
                right_d[128:, 0:size] = extra
                sum_k[:, 0:size] = jnp.zeros((128, size), F32)
                sum_v[:, 0:size] = jnp.zeros((128, size), F32)

                @pl.loop(0, pl.cdiv(valid, wide))
                def _(i):
                    ds = pl.ds(pl.multiple_of(i * wide, wide), wide)
                    q = qkv[cell, 0:128, ds]
                    d = grad[cell, :, ds]
                    inner = d.astype(F32) * ctx32[cell, :, ds]
                    for head in range(2):
                        at = slice(HEAD * head, HEAD * head + HEAD)
                        delta = jnp.sum(inner[at], axis=0, keepdims=True)
                        s = dot(
                            left(q, head, -logs[cell, head : head + 1, ds], True),
                            right_s[:, 0:size],
                            1,
                            0,
                        )
                        p = jnp.exp(s)
                        dp = dot(left(d, head, -delta, False), right_d[:, 0:size], 1, 0)
                        ds_low = (p * dp).astype(BF)
                        sum_v[at, 0:size] += dot(d[at], p.astype(BF), 1, 0)
                        sum_k[at, 0:size] += dot(q[at], ds_low, 1, 0)
                        dq = dot(qkv[cell, 128 + HEAD * head : 192 + HEAD * head, 0:size], ds_low, 1, 1)
                        out[cell, at, ds] = (dq * 0.125).astype(BF)

                out[cell, 128:256, 0:size] = sum_k[:, 0:size].astype(BF)
                out[cell, 256:384, 0:size] = sum_v[:, 0:size].astype(BF)
                part = out[cell, :, 0:size]
                dwqkv[...] += dot(part, xs[cell, 0:size], 1, 0)
                sums[0:128] += fold_lanes(part[0:128].astype(F32))
                sums[128:256] += fold_lanes(part[256:384].astype(F32))

    lane = lax.broadcasted_iota(jnp.int32, (128, 128), 1)
    q_sum = jnp.sum(sums[0:128], axis=1, keepdims=True)
    v_sum = jnp.sum(sums[128:256], axis=1, keepdims=True)
    dvec[...] = jnp.where(lane == QB, q_sum, jnp.where(lane == VB, v_sum, 0.0))
    if has_done:
        place.wait()


def attend_back(lens, qkv, grad, ctx32, logs, xs, *done):
    length = qkv.shape[2]
    return pl.pallas_call(
        functools.partial(attend_back_kernel, bool(done)),
        name="attend_back",
        out_shape=(
            shape_of((2, 384, length), BF),
            shape_of((384, 256), F32),
            shape_of((128, 128), F32),
        )
        + tuple(shape_of(a.shape, a.dtype) for a in done),
        in_specs=[SMEM_SPEC] + [VMEM_SPEC] * (5 + len(done)),
        out_specs=[VMEM_SPEC] * 3 + [HBM_SPEC] * len(done),
        scratch_shapes=[
            pltpu.VMEM((128 + EXT, length), BF),
            pltpu.VMEM((128 + EXT, length), BF),
            pltpu.VMEM((128, length), F32),
            pltpu.VMEM((128, length), F32),
            pltpu.VMEM((256, 128), F32),
        ]
        + [pltpu.SemaphoreType.DMA] * len(done),
        compiler_params=params(),
    )(lens, qkv, grad, ctx32, logs, xs, *done)


BLOCK = 1024


def block_of(i):
    return pl.ds(pl.multiple_of(i * BLOCK, BLOCK), BLOCK)


def pair_semaphores(count):
    return [pltpu.SemaphoreType.DMA((count,)), pltpu.SemaphoreType.DMA((count,))]


def between_kernel(
    ctx, x_ref, wqkv, wo, wup, wdn, cols_ref,
    x_out, ctx_out, unit1, hidden, unit2, scales, qkv, lows,
    landed, out, send, recv,
):
    cols, cols_next = cols_ref.at[0], cols_ref.at[1]
    count = x_out.shape[1] // BLOCK
    core, peer = pair_of()

    def arrival(i):
        ds, j = block_of(i), 2 * count + i
        return to_peer(ctx.at[1, :, ds], landed.at[:, ds], send.at[j], recv.at[j], peer)

    def low_copy(i):
        ds, j = block_of(i), count + i
        return to_peer(lows.at[0, ds], lows.at[1, ds], send.at[j], recv.at[j], peer)

    def copy(i):
        ds = block_of(i)
        return to_peer(out.at[:, ds], qkv.at[1, :, ds], send.at[i], recv.at[i], peer)

    greet(peer)

    @pl.loop(0, count)
    def _(i):
        arrival(i).start()

    @pl.loop(0, count)
    def _(i):
        ds = block_of(i)
        x = jnp.transpose(x_ref[0, ds].astype(F32))
        arrival(i).wait()
        context = join(core, ctx[0, :, ds], landed[:, ds])
        ctx_out[:, ds] = context
        one, scale1, hid, two, scale2, x_next = forward_block(
            context, x, wo[0], wup[...], wdn[...], cols
        )
        unit1[:, ds], hidden[:, ds], unit2[:, ds] = one, hid, two
        scales[0:1, ds], scales[1:2, ds] = scale1, scale2
        x_out[:, ds] = x_next
        low = x_next.astype(BF)
        lows[0, ds] = jnp.transpose(low)
        low_copy(i).start()
        out[:, ds] = project(low, 0, wqkv, cols_next, 1 - core, 1)
        copy(i).start()
        qkv[0, :, ds] = project(low, 0, wqkv, cols_next, core, 1)

    @pl.loop(0, count)
    def _(i):
        low_copy(i).wait()
        copy(i).wait()


def between(ctx, cells, wqkv, wo, wup, wdn, cols):
    length = ctx.shape[2]
    shapes = (
        shape_of((256, length), F32),
        shape_of((256, length), BF),
        shape_of((256, length), F32),
        shape_of((512, length), F32),
        shape_of((256, length), F32),
        shape_of((8, length), F32),
        shape_of((2, 384, length), BF),
        shape_of((2, length, 256), BF),
    )
    return pl.pallas_call(
        between_kernel,
        name="between_layers",
        out_shape=shapes,
        in_specs=[VMEM_SPEC] * 7,
        out_specs=[VMEM_SPEC] * len(shapes),
        scratch_shapes=[
            pltpu.VMEM((128, length), BF),
            pltpu.VMEM((384, length), BF),
        ]
        + pair_semaphores(3 * length // BLOCK),
        compiler_params=params(3),
    )(ctx, cells, wqkv, wo, wup, wdn, cols)


def turn_kernel(direct, lens, ctx, x_ref, cot, wo, cols_ref, *refs):
    if direct:
        end, refs = refs[0], refs[1:]
    else:
        (wup, wdn), refs = refs[:2], refs[2:]
    cells_out, d_first, dctx, dwo, dwup, dwdn, dvec = refs[:7]
    landed, sums, out, grad, send, recv = refs[7:13]
    if direct:
        wup, wdn = refs[13:]
    cols = cols_ref.at[1]
    count = x_ref.shape[1] // BLOCK
    core, peer = pair_of()

    def arrival(i):
        ds, j = block_of(i), count + i
        return to_peer(ctx.at[1, :, ds], landed.at[:, ds], send.at[j], recv.at[j], peer)

    def copy(i):
        ds = block_of(i)
        return to_peer(out.at[:, ds], dctx.at[1, :, ds], send.at[i], recv.at[i], peer)

    hail([peer])
    if direct:
        unpack_feed_forward(end, 64, wup, wdn)
    await_hails([peer])

    @pl.loop(0, count)
    def _(i):
        arrival(i).start()

    for ref in (sums, dwo, dwup, dwdn):
        ref[...] = jnp.zeros_like(ref)

    @pl.loop(0, count)
    def _(i):
        ds = block_of(i)
        where = lax.broadcasted_iota(jnp.int32, (1, BLOCK), 1) + i * BLOCK
        valid = jnp.where(where < tile_lanes(lens[0, 0:1], BLOCK), 1.0, 0.0)
        grad[:, ds] = jnp.transpose(cot[0, ds].astype(F32)) * valid

    @pl.loop(0, count)
    def _(i):
        ds = block_of(i)
        arrival(i).wait()
        context = join(core, ctx[0, :, ds], landed[:, ds])
        weights = (wo[1], wup[...], wdn[...])
        unit1, scale1, hidden, unit2, scale2, x_next = forward_block(
            context, x_ref[:, ds], *weights, cols
        )
        cells_out[0, ds] = jnp.transpose(x_next).astype(BF)
        saved = (unit1, scale1, gelu_parts(hidden), unit2, scale2)
        d_first[:, ds], d_context = backward_block(
            grad[:, ds], context, saved, weights, cols, sums, dwo, dwup, dwdn
        )
        low, high = d_context[:128], d_context[128:]
        out[:, ds] = jnp.where(core == 0, high, low)
        copy(i).start()
        dctx[0, :, ds] = jnp.where(core == 0, low, high)

    dvec[...] = place_vectors(sums)

    @pl.loop(0, count)
    def _(i):
        copy(i).wait()


GRAD_SHAPES = ((256, 256), (512, 256), (256, 512), (256, 128))


def turn(direct, lens, ctx, x, cot, wo, cols, feed_forward):
    length = ctx.shape[2]
    shapes = (
        shape_of((1, length, 256), BF),
        shape_of((256, length), F32),
        shape_of((2, 128, length), BF),
    ) + tuple(shape_of(s, F32) for s in GRAD_SHAPES)
    return pl.pallas_call(
        functools.partial(turn_kernel, direct),
        name="turn",
        out_shape=shapes,
        in_specs=[VMEM_SPEC] * (6 + len(feed_forward)),
        out_specs=[VMEM_SPEC] * len(shapes),
        scratch_shapes=[
            pltpu.VMEM((128, length), BF),
            pltpu.VMEM((2560, 128), F32),
            pltpu.VMEM((128, length), BF),
            pltpu.VMEM((256, length), F32),
        ]
        + pair_semaphores(2 * length // BLOCK)
        + ([pltpu.VMEM((512, 256), BF), pltpu.VMEM((256, 512), BF)] if direct else []),
        compiler_params=params(4, 18),
    )(lens, ctx, x, cot, wo, cols, *feed_forward)


OUTER, INNER = 48, 32


def shares(x):
    return x.reshape(32, x.shape[0] // 32, 256)


def vector_shares(vec):
    high = vec.astype(BF).astype(F32)
    return shares(jnp.concatenate([high, vec - high], axis=1))


def outer_shares(dwo, dwup, dwdn, dvec):
    return [
        shares(dwo[...]),
        shares(dwdn[:, 0:256]),
        shares(dwdn[:, 256:512]),
        vector_shares(dvec[...]),
        shares(dwup[...]),
    ]


def reduce_scratch(rows):
    return [
        pltpu.VMEM((2, 4, 4, rows, 256), BF),
        pltpu.VMEM((4, 4, rows, 256), BF),
        pltpu.VMEM((4, 4, rows, 256), BF),
        pltpu.VMEM((3, 4, rows, 256), BF),
        pltpu.VMEM((4, rows, 256), BF),
        pltpu.VMEM((3, rows, 256), BF),
        pltpu.SemaphoreType.DMA((7,)),
        pltpu.SemaphoreType.DMA((7,)),
    ]


REDUCE_REFS = 8


class Reduce:
    def __init__(self, own, from_core, by_plane, from_plane, by_line, from_line, send, recv):
        self.refs = own, from_core, by_plane, from_plane, by_line, from_line
        z, x, y, core = coordinates()
        self.z, self.number, self.core = z, 2 * x + y, core

        def copy(src, dst, i, device):
            return pltpu.make_async_remote_copy(
                src_ref=src,
                dst_ref=dst,
                send_sem=send.at[i],
                recv_sem=recv.at[i],
                device_id=device,
                device_id_type=MESH,
            )

        self.cores = [copy(own.at[1 - core], from_core, 0, sibling())]
        self.plane = [
            copy(by_plane.at[number], from_plane.at[i], 1 + i, device)
            for i, (device, number) in enumerate(plane_mates())
        ]
        self.line = [
            copy(by_line.at[there], from_line.at[i], 4 + i, device)
            for i, (device, there) in enumerate(line_mates())
        ]

    def fill(self, pieces):
        own = self.refs[0]
        rows = own.shape[3]
        terms = jnp.concatenate(pieces, axis=1).astype(BF).reshape(4, 4, 2, rows, 256)
        for core in range(2):
            for plane in range(4):
                own[core, plane] = terms[:, plane, core]

    def first(self):
        for c in self.cores:
            c.start()

    def second(self):
        own, from_core, by_plane = self.refs[:3]
        for c in self.cores:
            c.wait()
        by_plane[...] = (own[self.core].astype(F32) + from_core[...].astype(F32)).astype(BF)
        for c in self.plane:
            c.start()

    def third(self):
        by_plane, from_plane, by_line = self.refs[2:5]
        for c in self.plane:
            c.wait()
        total = by_plane[self.number].astype(F32)
        for i in range(3):
            total = total + from_plane[i].astype(F32)
        by_line[...] = total.astype(BF)
        for c in self.line:
            c.start()

    def result(self):
        by_line, from_line = self.refs[4:6]
        for c in self.line:
            c.wait()
        total = by_line[self.z].astype(F32)
        for i in range(3):
            total = total + from_line[i].astype(F32)
        return total


def reduce_half_scratch(rows):
    return [
        pltpu.VMEM((4, 4, rows, 256), BF),
        pltpu.VMEM((3, 4, rows, 256), BF),
        pltpu.VMEM((4, rows, 256), BF),
        pltpu.VMEM((4, rows, 256), BF),
        pltpu.SemaphoreType.DMA((7,)),
        pltpu.SemaphoreType.DMA((7,)),
    ]


HALF_REFS = 6


class ReduceHalf:
    def __init__(self, own, from_plane, by_line, from_line, send, recv):
        self.refs = own, from_plane, by_line, from_line
        z, x, y, core = coordinates()
        self.number = 2 * x + y

        def copy(src, dst, i, j, device):
            return pltpu.make_async_remote_copy(
                src_ref=src,
                dst_ref=dst,
                send_sem=send.at[i],
                recv_sem=recv.at[j],
                device_id=device,
                device_id_type=MESH,
            )

        self.plane = [
            copy(own.at[number], from_plane.at[i], i, i, device)
            for i, (device, number) in enumerate(plane_mates())
        ]
        self.line, self.mine = [], []
        for block in range(4):
            there, owner = 2 * core + block // 2, block % 2
            device = device_at(there, x, y, owner)
            self.line.append(copy(by_line.at[block], from_line.at[z], 3 + block, 3 + z, device))
            self.mine.append((there == z) & (owner == core))
        self.arrivals = []
        for there in range(4):
            arrival = copy(by_line.at[0], from_line.at[there], 3, 3 + there, sibling())
            self.arrivals.append((arrival, (there == z) & (z // 2 == core)))

    def fill(self, dwqkv, dvec):
        own = self.refs[0]
        rows = own.shape[2]

        def pieces(x):
            return x.reshape(16, 8, 256)

        terms = [pieces(dwqkv[128 * j : 128 * j + 128]) for j in range(3)]
        vec = dvec[...]
        high = vec.astype(BF).astype(F32)
        terms.append(pieces(jnp.concatenate([high, vec - high], axis=1)))
        terms = jnp.concatenate(terms, axis=1).astype(BF).reshape(2, 4, 2, rows, 256)
        for plane in range(4):
            own[plane] = terms[:, plane].reshape(4, rows, 256)

    def first(self):
        for c in self.plane:
            c.start()

    def second(self):
        own, from_plane, by_line, from_line = self.refs
        z = lax.axis_index("wide") // 2
        for c in self.plane:
            c.wait()
        total = own[self.number].astype(F32)
        for i in range(3):
            total = total + from_plane[i].astype(F32)
        by_line[...] = total.astype(BF)
        for block in range(4):

            @pl.when(jnp.logical_not(self.mine[block]))
            def _(block=block):
                self.line[block].start()

            @pl.when(self.mine[block])
            def _(block=block):
                from_line[z] = by_line[block]

    def result(self):
        from_line = self.refs[3]
        for arrival, mine in self.arrivals:
            pl.when(jnp.logical_not(mine))(arrival.wait_recv)
        for copy, mine in zip(self.line, self.mine):
            pl.when(jnp.logical_not(mine))(copy.wait_send)
        total = from_line[0].astype(F32)
        for i in range(1, 4):
            total = total + from_line[i].astype(F32)
        return total


def project_back(half, part, w_ref, layer):
    rows = jnp.concatenate([half_rows(w_ref, layer, 256 * j, half) for j in range(3)], axis=0)
    return dot(rows, part, 0, 0)


def middle_kernel(direct, *refs):
    dqkv, d_first_in, wqkv, ctx, unit1, hidden, unit2, scales, wo, wup, wdn, cols_ref = refs[:12]
    cols = cols_ref.at[0]
    refs = refs[12:]
    if direct:
        outer, inner, refs = refs[:4], refs[4:6], refs[6:]
    d_first, dctx, dwo, dwup, dwdn, dvec = refs[:6]
    refs = refs[6:]
    if direct:
        (sums_outer, sums_inner), refs = refs[:2], refs[2:]
    landed, sums, out, active, slope, send, recv = refs[:7]
    refs = refs[7:]
    count = d_first.shape[1] // BLOCK
    core, peer = pair_of()

    def arrival(i):
        ds, j = block_of(i), count + i
        return to_peer(dqkv.at[1, :, ds], landed.at[:, ds], send.at[j], recv.at[j], peer)

    def copy(i):
        ds = block_of(i)
        return to_peer(out.at[:, ds], dctx.at[1, :, ds], send.at[i], recv.at[i], peer)

    mates = gather_mates() + column_mates() if direct else [peer]
    hail(mates)
    if direct:
        two = ReduceHalf(*refs[:HALF_REFS])
        one = Reduce(*refs[HALF_REFS:])
        one.fill(outer_shares(*outer))
        two.fill(*inner)
    await_hails(mates)
    if direct:
        one.first()
        two.first()

    @pl.loop(0, count)
    def _(i):
        arrival(i).start()

    for ref in (sums, dwo, dwup, dwdn):
        ref[...] = jnp.zeros_like(ref)

    @pl.loop(0, count)
    def _(i):
        ds = block_of(i)
        active[:, ds], slope[:, ds] = gelu_parts(hidden[:, ds])

    if direct:
        one.second()

    @pl.loop(0, count)
    def _(i):
        if direct:

            @pl.when(i == 1)
            def _():
                two.second()
                one.third()

        ds = block_of(i)
        g = d_first_in[:, ds] + project_back(core, dqkv[0, :, ds], wqkv, 1)
        arrival(i).wait()
        g = g + project_back(1 - core, landed[:, ds], wqkv, 1)
        gelu = (active[:, ds], slope[:, ds])
        saved = (unit1[:, ds], scales[0:1, ds], gelu, unit2[:, ds], scales[1:2, ds])
        d_first[:, ds], d_context = backward_block(
            g, ctx[:, ds], saved, (wo[0], wup[...], wdn[...]), cols, sums, dwo, dwup, dwdn
        )
        low, high = d_context[:128], d_context[128:]
        out[:, ds] = jnp.where(core == 0, high, low)
        copy(i).start()
        dctx[0, :, ds] = jnp.where(core == 0, low, high)

    dvec[...] = place_vectors(sums)
    if direct:
        sums_inner[...] = two.result()
        sums_outer[...] = one.result()

    @pl.loop(0, count)
    def _(i):
        copy(i).wait()


def middle(direct, dqkv, d_first, wqkv, ctx, unit1, hidden, unit2, scales, wo, wup, wdn, cols, outer, inner):
    length = d_first.shape[1]
    terms = (*outer, *inner) if direct else ()
    shapes = (shape_of((256, length), F32), shape_of((2, 128, length), BF))
    shapes += tuple(shape_of(s, F32) for s in GRAD_SHAPES)
    if direct:
        shapes += (shape_of((OUTER, 256), F32), shape_of((INNER, 256), F32))
    return pl.pallas_call(
        functools.partial(middle_kernel, direct),
        name="back_between",
        out_shape=shapes,
        in_specs=[VMEM_SPEC] * (12 + len(terms)),
        out_specs=[VMEM_SPEC] * len(shapes),
        scratch_shapes=[
            pltpu.VMEM((384, length), BF),
            pltpu.VMEM((2560, 128), F32),
            pltpu.VMEM((128, length), BF),
            pltpu.VMEM((512, length), BF),
            pltpu.VMEM((512, length), F32),
        ]
        + pair_semaphores(2 * length // BLOCK)
        + (reduce_half_scratch(INNER) + reduce_scratch(OUTER) if direct else []),
        compiler_params=params(5, 18),
    )(dqkv, d_first, wqkv, ctx, unit1, hidden, unit2, scales, wo, wup, wdn, cols, *terms)


def last_kernel(direct, *refs):
    dqkv, d_first, wqkv = refs[:3]
    refs = refs[3:]
    if direct:
        outer, inner, (grad_out, sums_outer, sums_inner) = refs[:4], refs[4:6], refs[6:9]
        refs = refs[9:]
    else:
        grad_out, refs = refs[0], refs[1:]
    landed, grad, send, recv = refs[:4]
    refs = refs[4:]
    count = d_first.shape[1] // BLOCK
    core, peer = pair_of()

    def arrival(i):
        ds = block_of(i)
        return to_peer(dqkv.at[1, :, ds], landed.at[:, ds], send.at[i], recv.at[i], peer)

    mates = gather_mates() + column_mates() if direct else [peer]
    hail(mates)
    if direct:
        two = ReduceHalf(*refs[:HALF_REFS])
        one = Reduce(*refs[HALF_REFS:])
        one.fill(outer_shares(*outer))
        two.fill(*inner)
    await_hails(mates)
    if direct:
        one.first()
        two.first()

    @pl.loop(0, count)
    def _(i):
        arrival(i).start()

    @pl.loop(0, count)
    def _(i):
        ds = block_of(i)
        grad[:, ds] = d_first[:, ds] + project_back(core, dqkv[0, :, ds], wqkv, 0)

    if direct:
        one.second()

    @pl.loop(0, count)
    def _(i):
        if direct:
            pl.when(i == 1)(two.second)
        ds = block_of(i)
        arrival(i).wait()
        g = grad[:, ds] + project_back(1 - core, landed[:, ds], wqkv, 0)
        grad_out[0, ds] = jnp.transpose(g)

    if direct:
        one.third()
        sums_inner[...] = two.result()
        sums_outer[...] = one.result()


def last(direct, dqkv, d_first, wqkv, outer, inner):
    length = d_first.shape[1]
    terms = (*outer, *inner) if direct else ()
    shapes = (shape_of((1, length, 256), F32),)
    if direct:
        shapes += (shape_of((OUTER, 256), F32), shape_of((INNER, 256), F32))
    return pl.pallas_call(
        functools.partial(last_kernel, direct),
        name="back_input",
        out_shape=shapes,
        in_specs=[VMEM_SPEC] * (3 + len(terms)),
        out_specs=[VMEM_SPEC] * len(shapes),
        scratch_shapes=[
            pltpu.VMEM((384, length), BF),
            pltpu.VMEM((256, length), F32),
        ]
        + pair_semaphores(length // BLOCK)
        + (reduce_half_scratch(INNER) + reduce_scratch(OUTER) if direct else []),
        compiler_params=params(6),
    )(dqkv, d_first, wqkv, *terms)


def finish_kernel(factor, outer1, inner1, outer0, inner0, grad, *refs):
    qw, qb, kw, vw, vb, ow, ob, g1, s1, uw, ub, dw, db, g2, s2, placed, place_sem = refs
    place = pltpu.make_async_copy(grad, placed, place_sem)
    place.start()
    layers = (
        (inner0[...] * factor, outer0[...] * factor),
        (inner1[...] * factor, outer1[...] * factor),
    )
    for layer, (inner, outer) in enumerate(layers):
        qw[layer], kw[layer], vw[layer] = inner[0:8], inner[8:16], inner[16:24]
        ow[layer] = outer[0:8]
        dw[layer, :, 0:256], dw[layer, :, 256:512] = outer[8:16], outer[16:24]
        uw[layer] = outer[32:48]
        vec = inner[24:32] + outer[24:32]
        vec = jnp.transpose(vec[:, 0:128] + vec[:, 128:256])
        for i, ref in enumerate((qb, vb, ob, g1, s1, db, g2, s2)):
            ref[layer : layer + 1] = vec[i : i + 1]
        ub[layer : layer + 1, 0:8] = vec[8:9]
        ub[layer : layer + 1, 8:16] = vec[9:10]
    place.wait()


def finish(factor, sums, grad, like):
    found = pl.pallas_call(
        functools.partial(finish_kernel, factor),
        name="finish",
        out_shape=tuple(shape_of(a.shape, F32) for a in (*like, grad)),
        in_specs=[VMEM_SPEC] * 5,
        out_specs=[VMEM_SPEC] * len(like) + [HBM_SPEC],
        scratch_shapes=[pltpu.SemaphoreType.DMA],
        compiler_params=params(),
    )(*sums, grad)
    *found, grad = found
    return grad, [jnp.swapaxes(a, 1, 2) if a.ndim == 3 else a for a in found]


def gather_by_collectives(weights, vectors):
    def whole_of(w):
        return lax.all_gather(w, AXES, axis=1, tiled=True)

    qw, kw, vw, ow, uw, dw = (whole_of(w) for w in weights)
    columns = [lax.all_gather(v, AXES, axis=1, tiled=True).astype(F32) for v in vectors]
    up = columns.pop().reshape(2, 32, 2, 8)
    columns += [up[:, :, 0].reshape(2, 256), up[:, :, 1].reshape(2, 256)]
    lanes = jnp.stack(columns).transpose(2, 0, 1).reshape(256, 20)
    vec = jnp.pad(lanes, ((0, 0), (0, 108)))
    return jnp.concatenate([qw, kw, vw], axis=1), ow, uw, dw, vec


def sum_by_collectives(factor, layers):
    def share(x):
        return lax.psum_scatter(x, AXES, scatter_dimension=0, tiled=True) * factor

    found = []
    core = lax.rem(lax.axis_index("narrow"), 2)

    def widen(x):
        parts = x.reshape(-1, 1, 128, x.shape[1])
        mine = (jnp.arange(2) == core)[None, :, None, None]
        return jnp.where(mine, parts, 0.0).reshape(-1, x.shape[1])

    for dwqkv, dvec_qkv, dwo, dwup, dwdn, dvec in layers:
        dwqkv = widen(dwqkv)
        vec = widen(dvec_qkv) + dvec
        qb, vb, ob, g1, s1, db, g2, s2 = (share(vec[:, i]) for i in range(8))
        up = jnp.stack([vec[:, 8].reshape(32, 8), vec[:, 9].reshape(32, 8)], axis=1)
        qw, kw, vw = (share(dwqkv[256 * i : 256 * i + 256]).T for i in range(3))
        ow, uw, dw = share(dwo).T, share(dwup).T, share(dwdn).T
        ub = share(up.reshape(512))
        found.append((qw, qb, kw, vw, vb, ow, ob, g1, s1, uw, ub, dw, db, g2, s2))
    return [jnp.stack(pair) for pair in zip(*found)]


def on_device(devices, direct, cells_in, lengths, cotangent, *weights):
    qw, qb, kw, vw, vb, ow, ob, g1, s1, uw, ub, dw, db, g2, s2 = weights
    matrices, vectors = (qw, kw, vw, ow, uw, dw), (qb, vb, ob, g1, s1, db, g2, s2, ub)
    turned = [jnp.swapaxes(w, 1, 2) for w in matrices]
    if direct:
        share = own_share(lengths, turned, vectors)
        lens, qkv0, wqkv, wo, wup0, wdn0, cols, xs0, landed = start(share, cells_in)
        feed_forward = (landed,)
    else:
        wqkv, wo, wup, wdn, vec = gather_by_collectives(turned, vectors)
        wup0, wdn0, feed_forward = wup[0], wdn[0], (wup[1], wdn[1])
        cols = columns(vec)
        lens, qkv0, xs0 = project_first(lengths, cells_in, wqkv, cols)
    ctx_pair, ctx32_0, logs0 = attend(lens, qkv0)
    x1, ctx0, unit1, hidden, unit2, scales, qkv1, xs1 = between(
        ctx_pair, cells_in, wqkv, wo, wup0, wdn0, cols
    )
    ctx_pair, ctx32_1, logs1 = attend(lens, qkv1)
    cells_out, d_first, dctx, *outer1 = turn(
        direct, lens, ctx_pair, x1, cotangent, wo, cols, feed_forward
    )
    dqkv, *inner1, cells_out = attend_back(lens, qkv1, dctx, ctx32_1, logs1, xs1, cells_out)
    d_first, dctx, *found = middle(
        direct, dqkv, d_first, wqkv, ctx0, unit1, hidden, unit2, scales, wo, wup0, wdn0, cols, outer1, inner1
    )
    outer0, sums1 = found[:4], found[4:]
    dqkv, *inner0 = attend_back(lens, qkv0, dctx, ctx32_0, logs0, xs0)
    grad_in, *sums0 = last(direct, dqkv, d_first, wqkv, outer0, inner0)
    factor = 1.0 / math.sqrt(devices * cells_in.shape[0] * cells_in.shape[1])
    if direct:
        like = [shape_of(a.shape[:1] + a.shape[:0:-1], F32) for a in weights]
        grad_in, grads = finish(factor, (*sums1, *sums0), grad_in, like)
    else:
        grads = sum_by_collectives(factor, ((*inner0, *outer0), (*inner1, *outer1)))
    return (cells_out, grad_in, *grads)


def solution(mesh):
    devices = mesh.size
    direct = (mesh.shape["wide"], mesh.shape["narrow"]) == (8, 4)
    cell, vector, matrix = P(AXES, None, None), P(None, AXES), P(None, None, AXES)
    placed = (
        matrix, vector, matrix, matrix, vector, matrix, vector, vector, vector,
        matrix, vector, matrix, vector, vector, vector,
    )
    return jax.shard_map(
        functools.partial(on_device, devices, direct),
        mesh=mesh,
        in_specs=(cell, P(AXES), cell) + placed,
        out_specs=(cell, cell) + placed,
        check_vma=False,
    )
```

```python
import functools
import math

import jax
import jax.numpy as jnp
from jax import lax
from jax.experimental import pallas as pl
from jax.experimental.pallas import tpu as pltpu
from jax.sharding import PartitionSpec as P

HEAD = 64
NEG = -1000000000.0
EPS = 1e-06
AXES = ("wide", "narrow")
MESH = pl.DeviceIdType.MESH
BF = jnp.bfloat16
F32 = jnp.float32
EXT = 16
GUARD = 3600.0
KEY_SIZES = (640, 768, 1024, 1280, 1536)
ROWS = 64
VMEM_SPEC = pl.BlockSpec(memory_space=pltpu.VMEM)
SMEM_SPEC = pl.BlockSpec(memory_space=pltpu.SMEM)
HBM_SPEC = pl.BlockSpec(memory_space=pltpu.HBM)
QB, VB, OB, G1, S1, DB, G2, S2, UB = range(9)


def dot(a, b, ca, cb):
    return lax.dot_general(a, b, (((ca,), (cb,)), ((), ())), preferred_element_type=F32)


def params(collective_id=None, limit=16):
    if collective_id is None:
        return pltpu.CompilerParams(vmem_limit_bytes=limit << 20)
    return pltpu.CompilerParams(
        vmem_limit_bytes=limit << 20, collective_id=collective_id, has_side_effects=True
    )


def shape_of(shape, dtype):
    return jax.ShapeDtypeStruct(shape, dtype)


def pair_of():
    narrow = lax.axis_index("narrow")
    core = lax.rem(narrow, 2)
    return core, (lax.axis_index("wide"), narrow + 1 - 2 * core)


def greet(peer):
    hail([peer])
    await_hails([peer])


def to_peer(src, dst, send, recv, peer):
    return pltpu.make_async_remote_copy(
        src_ref=src, dst_ref=dst, send_sem=send, recv_sem=recv, device_id=peer, device_id_type=MESH
    )


def half_rows(ref, layer, base, half):
    return ref[layer, pl.ds(pl.multiple_of(base + half * 128, 128), 128)]


def tile_lanes(column, count):
    return jnp.concatenate([column] * (count // 128), axis=1)


def spread(both, layer, cols_ref, names):
    def every_lane(i):
        return jnp.broadcast_to(both[:, 2 * i + layer : 2 * i + layer + 1], (256, 128))

    for i in names:
        if i < UB:
            cols_ref[pl.ds(i * 256, 256)] = every_lane(i)
        else:
            halves = [every_lane(j).reshape(32, 8, 128) for j in (UB, UB + 1)]
            cols_ref[pl.ds(i * 256, 512)] = jnp.concatenate(halves, axis=1).reshape(512, 128)


def columns_kernel(vec, cols):
    for layer in range(2):
        spread(vec[...], layer, cols.at[layer], range(9))


def columns(vec):
    return pl.pallas_call(
        columns_kernel,
        name="columns",
        out_shape=shape_of((2, 2560, 128), F32),
        in_specs=[VMEM_SPEC],
        out_specs=VMEM_SPEC,
        compiler_params=params(),
    )(vec)


def column(cols_ref, i, count):
    rows = 512 if i == UB else 256
    return tile_lanes(cols_ref[pl.ds(i * 256, rows)], count)


def fold_lanes(x):
    total = x[:, :128]
    for start in range(128, x.shape[1], 128):
        total = total + x[:, start : start + 128]
    return total


def norm(resid):
    offset = resid - jnp.mean(resid, axis=0, keepdims=True)
    scale = lax.rsqrt(jnp.mean(offset * offset, axis=0, keepdims=True) + EPS)
    return offset * scale, scale


def norm_back(grad, gain, unit, scale):
    q = grad * gain
    return (
        q - jnp.mean(q, axis=0, keepdims=True) - unit * jnp.mean(q * unit, axis=0, keepdims=True)
    ) * scale


GELU_C = 0.7978845608028654
GELU_A = 0.044715


def project(xb, contract, w_ref, cols_ref, half, layer=0):
    parts = []
    for i in range(3):
        y = dot(half_rows(w_ref, layer, i * 256, half), xb, 1, contract)
        if i != 1:
            bias = cols_ref[
                pl.ds(pl.multiple_of((QB if i == 0 else VB) * 256 + half * 128, 128), 128)
            ]
            y = y + tile_lanes(bias, y.shape[1])
        y = y.astype(BF)
        parts.append(y * jnp.asarray(0.125, BF) if i == 0 else y)
    return jnp.concatenate(parts, axis=0)


def join(core, own, peer):
    return jnp.concatenate(
        [jnp.where(core == 0, own, peer), jnp.where(core == 0, peer, own)], axis=0
    )


def forward_block(context, x, wo, wup, wdn, cols_ref):
    count = x.shape[1]
    unit1, scale1 = norm(x + dot(wo, context, 1, 0) + column(cols_ref, OB, count))
    middle = unit1 * column(cols_ref, G1, count) + column(cols_ref, S1, count)
    hidden = dot(wup, middle.astype(BF), 1, 0) + column(cols_ref, UB, count)
    t = jnp.tanh(hidden * (GELU_C + (GELU_C * GELU_A) * (hidden * hidden)))
    active = (0.5 * hidden * (1.0 + t)).astype(BF)
    unit2, scale2 = norm(middle + dot(wdn, active, 1, 0) + column(cols_ref, DB, count))
    x_next = unit2 * column(cols_ref, G2, count) + column(cols_ref, S2, count)
    return unit1, scale1, hidden, unit2, scale2, x_next


def gelu_parts(hidden):
    square = hidden * hidden
    t = jnp.tanh(hidden * (GELU_C + (GELU_C * GELU_A) * square))
    half, more = 0.5 * hidden, 1.0 + t
    slope = 0.5 * more + half * (1.0 - t * t) * (GELU_C + (3.0 * GELU_C * GELU_A) * square)
    return (half * more).astype(BF), slope


def backward_block(grad, context, saved, weights, cols_ref, sums, dwo, dwup, dwdn):
    unit1, scale1, (active, slope), unit2, scale2 = saved
    wo, wup, wdn = weights
    count = grad.shape[1]

    def add(i, x):
        rows = x.shape[0]
        sums[pl.ds(i * 256, rows)] += fold_lanes(x)

    add(S2, grad)
    add(G2, grad * unit2)
    d_second = norm_back(grad, column(cols_ref, G2, count), unit2, scale2)
    branch = d_second.astype(BF)
    add(DB, branch.astype(F32))
    d_hidden = (dot(wdn, branch, 0, 0) * slope).astype(BF)
    dwdn[...] += dot(branch, active, 1, 1)
    add(UB, d_hidden.astype(F32))
    middle = unit1 * column(cols_ref, G1, count) + column(cols_ref, S1, count)
    dwup[...] += dot(d_hidden, middle.astype(BF), 1, 1)
    d_middle = d_second + dot(wup, d_hidden, 0, 0)
    add(S1, d_middle)
    add(G1, d_middle * unit1)
    d_first = norm_back(d_middle, column(cols_ref, G1, count), unit1, scale1)
    attn = d_first.astype(BF)
    add(OB, attn.astype(F32))
    dwo[...] += dot(attn, context, 1, 1)
    return d_first, dot(wo, attn, 0, 0).astype(BF)


def place_vectors(sums):
    lane = lax.broadcasted_iota(jnp.int32, (256, 128), 1)
    out = jnp.zeros((256, 128), F32)
    for i in range(8):
        total = jnp.sum(sums[pl.ds(i * 256, 256)], axis=1, keepdims=True)
        out = jnp.where(lane == i, total, out)
    up = jnp.sum(sums[pl.ds(2048, 512)], axis=1, keepdims=True)
    up = jnp.broadcast_to(up, (512, 128)).reshape(32, 16, 128)
    out = jnp.where(lane == 8, up[:, :8].reshape(256, 128), out)
    return jnp.where(lane == 9, up[:, 8:].reshape(256, 128), out)


def coordinates():
    wide, narrow = lax.axis_index("wide"), lax.axis_index("narrow")
    return wide // 2, lax.rem(wide, 2), narrow // 2, lax.rem(narrow, 2)


def device_at(z, x, y, core):
    return (2 * z + x, 2 * y + core)


def plane_mates():
    z, x, y, core = coordinates()
    return [
        (device_at(z, a, b, core), 2 * a + b) for a, b in ((x, 1 - y), (1 - x, y), (1 - x, 1 - y))
    ]


def line_mates():
    z, x, y, core = coordinates()
    there = [lax.rem(z + j, 4) for j in (1, 2, 3)]
    return [(device_at(a, x, y, core), a) for a in there]


def sibling():
    z, x, y, core = coordinates()
    return device_at(z, x, y, 1 - core)


def column_mates():
    z, x, y, core = coordinates()
    return [device_at(there, x, y, 1 - core) for _, there in line_mates()]


def hail(mates):
    for mate in mates:
        pl.semaphore_signal(
            pltpu.get_barrier_semaphore(), inc=1, device_id=mate, device_id_type=MESH
        )


def await_hails(mates):
    pl.semaphore_wait(pltpu.get_barrier_semaphore(), len(mates))


def gather_mates():
    return [sibling()] + [d for d, _ in plane_mates()] + [d for d, _ in line_mates()]


FIRST, REST = 48, 96


SHARE = 80


def share_kernel(length, qw, kw, vw, ow, uw, dw, *refs):
    vectors, share = refs[:-1], refs[-1]
    for layer in range(2):
        for i, w in enumerate((qw, kw, vw, ow)):
            share[layer, 8 * i : 8 * i + 8] = w[layer]
        share[layer, 32:48] = uw[layer]
        share[layer, 48:56] = dw[layer, :, 0:256]
        share[layer, 56:64] = dw[layer, :, 256:512]
        share[layer, 64:80] = jnp.zeros((16, 256), BF)
        at = 0
        for v in vectors:
            share[layer, 64:65, at : at + v.shape[1]] = v[layer : layer + 1]
            at += v.shape[1]
        number = length[...].reshape(1, 1)
        share[layer, 64:65, at : at + 1] = (number // 256).astype(F32).astype(BF)
        share[layer, 64:65, at + 1 : at + 2] = (number % 256).astype(F32).astype(BF)


def own_share(lengths, weights, vectors):
    return pl.pallas_call(
        share_kernel,
        name="own_share",
        out_shape=shape_of((2, SHARE, 256), BF),
        in_specs=[VMEM_SPEC] * 16,
        out_specs=VMEM_SPEC,
        compiler_params=params(limit=60),
    )(lengths, *weights, *vectors)


def pack_own(share, first, rest, flat):
    flat[...] = jnp.zeros_like(flat)
    for layer in range(2):
        row = share[layer, 64:80].astype(F32)[0:1]
        for i in range(10):
            at = 2 * i + layer
            flat[at : at + 1, 0:8] = row[:, 8 * i : 8 * i + 8]
    columns = jnp.transpose(flat[...])[0:8]
    block = jnp.concatenate([columns, jnp.zeros_like(columns)], axis=1)
    first[0:32] = share[0, 0:32]
    first[32:48] = jnp.concatenate([block, jnp.zeros_like(block)], axis=0).astype(BF)
    rest[0:32] = share[0, 32:64]
    rest[32:96] = share[1, 0:64]


def ordered(landed, at, rows):
    pieces = [
        landed[core, plane, z, at : at + rows]
        for z in range(4)
        for plane in range(4)
        for core in range(2)
    ]
    return jnp.stack(pieces)


def two_matrices(landed, at):
    pair = ordered(landed, at, 16).astype(F32)
    return (
        pair[:, :8].reshape(256, 256).astype(BF),
        pair[:, 8:].reshape(256, 256).astype(BF),
    )


def unpack_first(landed, wqkv, wo, both):
    wqkv[0, 0:256], wqkv[0, 256:512] = two_matrices(landed, 0)
    wqkv[0, 512:768], wo[0] = two_matrices(landed, 16)
    both[...] = ordered(landed, 32, 16).astype(F32)[:, :8, :128].reshape(256, 128)


def unpack_feed_forward(landed, at, up, down):
    up[...] = ordered(landed, at, 16).reshape(512, 256)
    down[:, 0:256], down[:, 256:512] = two_matrices(landed, at + 16)


def unpack_rest(landed, wqkv, wo, up, down):
    unpack_feed_forward(landed, 0, up, down)
    wqkv[1, 0:256], wqkv[1, 256:512] = two_matrices(landed, 32)
    wqkv[1, 512:768], wo[1] = two_matrices(landed, 48)


class Gather:
    def __init__(self, own, landed, send, recv, part):
        z, x, y, core = coordinates()
        plane = 2 * x + y

        def copy(src, dst, i, device):
            return pltpu.make_async_remote_copy(
                src_ref=src,
                dst_ref=dst,
                send_sem=send.at[part, i],
                recv_sem=recv.at[part, i],
                device_id=device,
                device_id_type=MESH,
            )

        def column(i):
            return landed.at[core, i]

        self.keep = lambda: landed.at[core, plane, z].__setitem__(Ellipsis, own[...])
        self.line = [
            copy(own, landed.at[core, plane, z], i, device)
            for i, (device, _) in enumerate(line_mates())
        ]
        self.plane = [
            copy(column(plane), column(plane), 3 + i, device)
            for i, (device, _) in enumerate(plane_mates())
        ]
        columns = [plane] + [number for _, number in plane_mates()]
        self.cores = [
            copy(column(number), column(number), 6 + i, sibling())
            for i, number in enumerate(columns)
        ]


def start_kernel(
    share, x_ref,
    lens, qkv, wqkv, wo, wup, wdn, cols, xs, landed_rest,
    first, rest, flat, landed_first, both, out, own_len, send, recv, pair_send, pair_recv, x_sems,
):
    core, peer = pair_of()
    mates = gather_mates()
    hail(mates)
    pack_own(share, first, rest, flat)
    number = share[0, 64:80].astype(F32)[0:1]
    number = number[:, 80:81] * 256.0 + number[:, 81:82]
    own_len[...] = jnp.broadcast_to(number, own_len.shape).astype(jnp.int32)
    a = Gather(first, landed_first, send, recv, 0)
    b = Gather(rest, landed_rest, send, recv, 1)
    await_hails(mates)
    for c in a.line + b.line:
        c.start()
    len_copy = to_peer(own_len, lens.at[1], pair_send.at[0], pair_recv.at[0], peer)
    len_copy.start()
    x_copy = to_peer(x_ref.at[0], xs.at[1], x_sems.at[0], x_sems.at[1], peer)
    x_copy.start()
    a.keep()
    b.keep()
    lens[0] = own_len[...]
    xs[0] = x_ref[0]
    for part in (a, b):
        for c in part.line:
            c.wait()
        for c in part.plane + part.cores[:1]:
            c.start()
    for i in range(3):
        a.plane[i].wait()
        a.cores[1 + i].start()
    for c in a.cores:
        c.wait()
    unpack_first(landed_first, wqkv, wo, both)
    spread(both[...], 0, cols.at[0], (QB, VB))
    block = 1024
    count = x_ref.shape[1] // block

    def copy(i):
        ds = pl.ds(pl.multiple_of(i * block, block), block)
        return to_peer(
            out.at[:, ds], qkv.at[1, :, ds], pair_send.at[1 + i], pair_recv.at[1 + i], peer
        )

    @pl.loop(0, count)
    def _(i):
        ds = pl.ds(pl.multiple_of(i * block, block), block)
        out[:, ds] = project(x_ref[0, ds], 1, wqkv, cols.at[0], 1 - core)
        copy(i).start()

    @pl.loop(0, count)
    def _(i):
        ds = pl.ds(pl.multiple_of(i * block, block), block)
        qkv[0, :, ds] = project(x_ref[0, ds], 1, wqkv, cols.at[0], core)

    spread(both[...], 0, cols.at[0], (OB, G1, S1, DB, G2, S2, UB))
    spread(both[...], 1, cols.at[1], range(9))
    for i in range(3):
        b.plane[i].wait()
        b.cores[1 + i].start()
    for c in b.cores:
        c.wait()
    unpack_rest(landed_rest, wqkv, wo, wup, wdn)
    len_copy.wait()
    x_copy.wait()

    @pl.loop(0, count)
    def _(i):
        copy(i).wait()


def start(share, cells):
    length = cells.shape[1]
    count = length // 1024
    return pl.pallas_call(
        start_kernel,
        name="gather_and_project",
        out_shape=(
            shape_of((2, 8, 128), jnp.int32),
            shape_of((2, 384, length), BF),
            shape_of((2, 768, 256), BF),
            shape_of((2, 256, 256), BF),
            shape_of((512, 256), BF),
            shape_of((256, 512), BF),
            shape_of((2, 2560, 128), F32),
            shape_of((2, length, 256), BF),
            shape_of((2, 4, 4, REST, 256), BF),
        ),
        in_specs=[VMEM_SPEC] * 2,
        out_specs=[VMEM_SPEC] * 9,
        scratch_shapes=[
            pltpu.VMEM((FIRST, 256), BF),
            pltpu.VMEM((REST, 256), BF),
            pltpu.VMEM((128, 128), F32),
            pltpu.VMEM((2, 4, 4, FIRST, 256), BF),
            pltpu.VMEM((256, 128), F32),
            pltpu.VMEM((384, length), BF),
            pltpu.VMEM((8, 128), jnp.int32),
            pltpu.SemaphoreType.DMA((2, 10)),
            pltpu.SemaphoreType.DMA((2, 10)),
            pltpu.SemaphoreType.DMA((count + 1,)),
            pltpu.SemaphoreType.DMA((count + 1,)),
            pltpu.SemaphoreType.DMA((2,)),
        ],
        compiler_params=params(1),
    )(share, cells)


def project_kernel(len_ref, x_ref, w_ref, cols_ref, lens, qkv, xs, out, own_len, send, recv):
    core, peer = pair_of()
    cols = cols_ref.at[0]
    own_len[...] = jnp.full(own_len.shape, len_ref[0], jnp.int32)
    greet(peer)
    len_copy = to_peer(own_len, lens.at[1], send.at[0], recv.at[0], peer)
    len_copy.start()
    lens[0] = own_len[...]
    x_copy = to_peer(x_ref.at[0], xs.at[1], send.at[2], recv.at[2], peer)
    x_copy.start()
    xs[0] = x_ref[0]
    out[...] = project(x_ref[0], 1, w_ref, cols, 1 - core)
    qkv_copy = to_peer(out, qkv.at[1], send.at[1], recv.at[1], peer)
    qkv_copy.start()
    qkv[0] = project(x_ref[0], 1, w_ref, cols, core)
    len_copy.wait()
    qkv_copy.wait()
    x_copy.wait()


def project_first(lengths, cells, wqkv, cols):
    length = cells.shape[1]
    return pl.pallas_call(
        project_kernel,
        name="project_first",
        out_shape=(
            shape_of((2, 8, 128), jnp.int32),
            shape_of((2, 384, length), BF),
            shape_of((2, length, 256), BF),
        ),
        in_specs=[SMEM_SPEC] + [VMEM_SPEC] * 3,
        out_specs=[VMEM_SPEC] * 3,
        scratch_shapes=[
            pltpu.VMEM((384, length), BF),
            pltpu.VMEM((8, 128), jnp.int32),
            pltpu.SemaphoreType.DMA((3,)),
            pltpu.SemaphoreType.DMA((3,)),
        ],
        compiler_params=params(2),
    )(lengths, cells, wqkv, cols)


def key_sizes(length):
    return [size for size in KEY_SIZES if size < length] + [length]


def extended(x, extra):
    return jnp.concatenate([x, extra], axis=0)


def one_head(x, head):
    row = lax.broadcasted_iota(jnp.int32, x.shape, 0)
    return jnp.where((row // HEAD) == head, x, jnp.zeros_like(x))


def attend_kernel(lens, qkv, ctx, ctx32, logs, kx, scores, total, acc):
    length = qkv.shape[2]

    def query_of(cell, i, head, wide):
        q = qkv[cell, 0:128, pl.ds(pl.multiple_of(i * wide, wide), wide)]
        row = lax.broadcasted_iota(jnp.int32, (EXT, wide), 0)
        return extended(one_head(q, head), jnp.where(row == 0, 1.0, 0.0).astype(BF))

    def finish(cell, i, head, wide, high, sums, out):
        ds = pl.ds(pl.multiple_of(i * wide, wide), wide)
        sums = jnp.sum(sums, axis=0, keepdims=True)
        out = out * (1.0 / sums)
        rows = slice(HEAD * head, HEAD * head + HEAD)
        ctx[cell, rows, ds] = out.astype(BF)
        ctx32[cell, rows, ds] = out
        logs[cell, head : head + 1, ds] = jnp.log(sums) + high

    def largest(x):
        x = x.astype(F32)
        square = x * x
        return [
            jnp.max(jnp.sum(square[HEAD * h : HEAD * h + HEAD], axis=0, keepdims=True))
            for h in range(2)
        ]

    @pl.loop(0, 2)
    def _(cell):
        valid = lens[cell, 0, 0]
        q_most = largest(qkv[cell, 0:128])
        k_most = largest(qkv[cell, 128:256])
        plain = jnp.maximum(q_most[0] * k_most[0], q_most[1] * k_most[1]) <= GUARD

        @pl.loop(0, jnp.minimum(pl.cdiv(valid, 256) + 1, length // 256))
        def _(i):
            ds = pl.ds(pl.multiple_of(i * 256, 256), 256)
            where = lax.broadcasted_iota(jnp.int32, (EXT, 256), 1) + i * 256
            first = lax.broadcasted_iota(jnp.int32, (EXT, 256), 0) == 0
            extra = jnp.where(first & (where >= valid), NEG, 0.0).astype(BF)
            kx[ds] = jnp.transpose(extended(qkv[cell, 128:256, ds], extra))

        sizes = key_sizes(length)
        for low, size in zip([0] + sizes[:-1], sizes):
            wide = next(w for w in (2048, 1024, 512) if w * size <= 1024 * 1024 or w == 512)
            wide = min(wide, length)

            @pl.when(plain & (valid > low) & (valid <= size))
            def _(size=size, wide=wide):
                @pl.loop(0, length // wide)
                def _(i):
                    for head in range(2):
                        s = dot(kx[0:size], query_of(cell, i, head, wide), 1, 0)
                        e = jnp.exp(s)
                        sums = jnp.sum(e.reshape(size // 8, 8, wide), axis=0)
                        v = qkv[cell, 256 + HEAD * head : 320 + HEAD * head, 0:size]
                        finish(cell, i, head, wide, 0.0, sums, dot(v, e.astype(BF), 1, 0))

        @pl.when(jnp.logical_not(plain))
        def _():
            chunks = pl.cdiv(valid, 256)
            wide = 512

            @pl.loop(0, length // wide)
            def _(i):
                for head in range(2):
                    query = query_of(cell, i, head, wide)

                    def score(j, high):
                        s = dot(kx[pl.ds(pl.multiple_of(j * 256, 256), 256)], query, 1, 0)
                        scores[j] = s
                        return jnp.maximum(high, jnp.max(s.reshape(32, 8, wide), axis=0))

                    high = lax.fori_loop(0, chunks, score, jnp.full((8, wide), NEG * 2, F32))
                    high = jnp.max(high, axis=0, keepdims=True)
                    acc[...] = jnp.zeros_like(acc)
                    total[...] = jnp.zeros_like(total)

                    @pl.loop(0, chunks)
                    def _(j):
                        e = jnp.exp(scores[j] - high)
                        total[...] += jnp.sum(e.reshape(32, 8, wide), axis=0)
                        v = qkv[
                            cell,
                            256 + HEAD * head : 320 + HEAD * head,
                            pl.ds(pl.multiple_of(j * 256, 256), 256),
                        ]
                        acc[...] += dot(v, e.astype(BF), 1, 0)

                    finish(cell, i, head, wide, high, total[...], acc[...])


def attend(lens, qkv):
    length = qkv.shape[2]
    return pl.pallas_call(
        attend_kernel,
        name="attend",
        out_shape=(
            shape_of((2, 128, length), BF),
            shape_of((2, 128, length), F32),
            shape_of((2, 2, length), F32),
        ),
        in_specs=[SMEM_SPEC, VMEM_SPEC],
        out_specs=[VMEM_SPEC] * 3,
        scratch_shapes=[
            pltpu.VMEM((length, 128 + EXT), BF),
            pltpu.VMEM((length // 256, 256, 512), F32),
            pltpu.VMEM((8, 512), F32),
            pltpu.VMEM((HEAD, 512), F32),
        ],
        compiler_params=params(),
    )(lens, qkv)


def in_three(x):
    high = x.astype(BF)
    rest = x - high.astype(F32)
    middle = rest.astype(BF)
    return high, middle, (rest - middle.astype(F32)).astype(BF)


def attend_back_kernel(
    has_done, lens, qkv, grad, ctx32, logs, xs, *refs
):
    if has_done:
        done, (out, dwqkv, dvec, placed), refs = refs[0], refs[1:5], refs[5:]
    else:
        (out, dwqkv, dvec), refs = refs[:3], refs[3:]
    right_s, right_d, sum_k, sum_v, sums = refs[:5]
    if has_done:
        place = pltpu.make_async_copy(done, placed, refs[5])
        place.start()
    length = qkv.shape[2]
    wide = 512
    row = lax.broadcasted_iota(jnp.int32, (EXT, wide), 0)

    def left(x, head, value, last):
        a, b, c = in_three(value)
        zero = jnp.zeros((EXT, wide), BF)
        extra = jnp.where(row == 0, a, jnp.where(row == 1, b, jnp.where(row == 2, c, zero)))
        if last:
            extra = jnp.where(row == 3, jnp.ones_like(zero), extra)
        return jnp.transpose(extended(one_head(x, head), extra))

    dwqkv[...] = jnp.zeros_like(dwqkv)
    sums[...] = jnp.zeros_like(sums)

    @pl.loop(0, 2)
    def _(cell):
        valid = lens[cell, 0, 0]
        out[cell] = jnp.zeros_like(out[cell])
        sizes = key_sizes(length)
        for low, size in zip([0] + sizes[:-1], sizes):

            @pl.when((valid > low) & (valid <= size))
            def _(size=size):
                where = lax.broadcasted_iota(jnp.int32, (EXT, size), 1)
                rows = lax.broadcasted_iota(jnp.int32, (EXT, size), 0)
                extra = jnp.where(
                    rows < 3, 1.0, jnp.where((rows == 3) & (where >= valid), NEG, 0.0)
                ).astype(BF)
                right_s[0:128, 0:size] = qkv[cell, 128:256, 0:size]
                right_s[128:, 0:size] = extra
                right_d[0:128, 0:size] = qkv[cell, 256:384, 0:size]
                right_d[128:, 0:size] = extra
                sum_k[:, 0:size] = jnp.zeros((128, size), F32)
                sum_v[:, 0:size] = jnp.zeros((128, size), F32)

                @pl.loop(0, pl.cdiv(valid, wide))
                def _(i):
                    ds = pl.ds(pl.multiple_of(i * wide, wide), wide)
                    q = qkv[cell, 0:128, ds]
                    d = grad[cell, :, ds]
                    inner = d.astype(F32) * ctx32[cell, :, ds]
                    for head in range(2):
                        at = slice(HEAD * head, HEAD * head + HEAD)
                        delta = jnp.sum(inner[at], axis=0, keepdims=True)
                        s = dot(
                            left(q, head, -logs[cell, head : head + 1, ds], True),
                            right_s[:, 0:size],
                            1,
                            0,
                        )
                        p = jnp.exp(s)
                        dp = dot(left(d, head, -delta, False), right_d[:, 0:size], 1, 0)
                        ds_low = (p * dp).astype(BF)
                        sum_v[at, 0:size] += dot(d[at], p.astype(BF), 1, 0)
                        sum_k[at, 0:size] += dot(q[at], ds_low, 1, 0)
                        dq = dot(qkv[cell, 128 + HEAD * head : 192 + HEAD * head, 0:size], ds_low, 1, 1)
                        out[cell, at, ds] = (dq * 0.125).astype(BF)

                out[cell, 128:256, 0:size] = sum_k[:, 0:size].astype(BF)
                out[cell, 256:384, 0:size] = sum_v[:, 0:size].astype(BF)
                part = out[cell, :, 0:size]
                dwqkv[...] += dot(part, xs[cell, 0:size], 1, 0)
                sums[0:128] += fold_lanes(part[0:128].astype(F32))
                sums[128:256] += fold_lanes(part[256:384].astype(F32))

    lane = lax.broadcasted_iota(jnp.int32, (128, 128), 1)
    q_sum = jnp.sum(sums[0:128], axis=1, keepdims=True)
    v_sum = jnp.sum(sums[128:256], axis=1, keepdims=True)
    dvec[...] = jnp.where(lane == QB, q_sum, jnp.where(lane == VB, v_sum, 0.0))
    if has_done:
        place.wait()


def attend_back(lens, qkv, grad, ctx32, logs, xs, *done):
    length = qkv.shape[2]
    return pl.pallas_call(
        functools.partial(attend_back_kernel, bool(done)),
        name="attend_back",
        out_shape=(
            shape_of((2, 384, length), BF),
            shape_of((384, 256), F32),
            shape_of((128, 128), F32),
        )
        + tuple(shape_of(a.shape, a.dtype) for a in done),
        in_specs=[SMEM_SPEC] + [VMEM_SPEC] * (5 + len(done)),
        out_specs=[VMEM_SPEC] * 3 + [HBM_SPEC] * len(done),
        scratch_shapes=[
            pltpu.VMEM((128 + EXT, length), BF),
            pltpu.VMEM((128 + EXT, length), BF),
            pltpu.VMEM((128, length), F32),
            pltpu.VMEM((128, length), F32),
            pltpu.VMEM((256, 128), F32),
        ]
        + [pltpu.SemaphoreType.DMA] * len(done),
        compiler_params=params(),
    )(lens, qkv, grad, ctx32, logs, xs, *done)


BLOCK = 1024


def block_of(i):
    return pl.ds(pl.multiple_of(i * BLOCK, BLOCK), BLOCK)


def pair_semaphores(count):
    return [pltpu.SemaphoreType.DMA((count,)), pltpu.SemaphoreType.DMA((count,))]


def between_kernel(
    ctx, x_ref, wqkv, wo, wup, wdn, cols_ref,
    x_out, ctx_out, unit1, hidden, unit2, scales, qkv, lows,
    landed, out, send, recv,
):
    cols, cols_next = cols_ref.at[0], cols_ref.at[1]
    count = x_out.shape[1] // BLOCK
    core, peer = pair_of()

    def arrival(i):
        ds, j = block_of(i), 2 * count + i
        return to_peer(ctx.at[1, :, ds], landed.at[:, ds], send.at[j], recv.at[j], peer)

    def low_copy(i):
        ds, j = block_of(i), count + i
        return to_peer(lows.at[0, ds], lows.at[1, ds], send.at[j], recv.at[j], peer)

    def copy(i):
        ds = block_of(i)
        return to_peer(out.at[:, ds], qkv.at[1, :, ds], send.at[i], recv.at[i], peer)

    greet(peer)

    @pl.loop(0, count)
    def _(i):
        arrival(i).start()

    @pl.loop(0, count)
    def _(i):
        ds = block_of(i)
        x = jnp.transpose(x_ref[0, ds].astype(F32))
        arrival(i).wait()
        context = join(core, ctx[0, :, ds], landed[:, ds])
        ctx_out[:, ds] = context
        one, scale1, hid, two, scale2, x_next = forward_block(
            context, x, wo[0], wup[...], wdn[...], cols
        )
        unit1[:, ds], hidden[:, ds], unit2[:, ds] = one, hid, two
        scales[0:1, ds], scales[1:2, ds] = scale1, scale2
        x_out[:, ds] = x_next
        low = x_next.astype(BF)
        lows[0, ds] = jnp.transpose(low)
        low_copy(i).start()
        out[:, ds] = project(low, 0, wqkv, cols_next, 1 - core, 1)
        copy(i).start()
        qkv[0, :, ds] = project(low, 0, wqkv, cols_next, core, 1)

    @pl.loop(0, count)
    def _(i):
        low_copy(i).wait()
        copy(i).wait()


def between(ctx, cells, wqkv, wo, wup, wdn, cols):
    length = ctx.shape[2]
    shapes = (
        shape_of((256, length), F32),
        shape_of((256, length), BF),
        shape_of((256, length), F32),
        shape_of((512, length), F32),
        shape_of((256, length), F32),
        shape_of((8, length), F32),
        shape_of((2, 384, length), BF),
        shape_of((2, length, 256), BF),
    )
    return pl.pallas_call(
        between_kernel,
        name="between_layers",
        out_shape=shapes,
        in_specs=[VMEM_SPEC] * 7,
        out_specs=[VMEM_SPEC] * len(shapes),
        scratch_shapes=[
            pltpu.VMEM((128, length), BF),
            pltpu.VMEM((384, length), BF),
        ]
        + pair_semaphores(3 * length // BLOCK),
        compiler_params=params(3),
    )(ctx, cells, wqkv, wo, wup, wdn, cols)


def turn_kernel(direct, lens, ctx, x_ref, cot, wo, cols_ref, *refs):
    if direct:
        end, refs = refs[0], refs[1:]
    else:
        (wup, wdn), refs = refs[:2], refs[2:]
    cells_out, d_first, dctx, dwo, dwup, dwdn, dvec = refs[:7]
    landed, sums, out, grad, send, recv = refs[7:13]
    if direct:
        wup, wdn = refs[13:]
    cols = cols_ref.at[1]
    count = x_ref.shape[1] // BLOCK
    core, peer = pair_of()

    def arrival(i):
        ds, j = block_of(i), count + i
        return to_peer(ctx.at[1, :, ds], landed.at[:, ds], send.at[j], recv.at[j], peer)

    def copy(i):
        ds = block_of(i)
        return to_peer(out.at[:, ds], dctx.at[1, :, ds], send.at[i], recv.at[i], peer)

    hail([peer])
    if direct:
        unpack_feed_forward(end, 64, wup, wdn)
    await_hails([peer])

    @pl.loop(0, count)
    def _(i):
        arrival(i).start()

    for ref in (sums, dwo, dwup, dwdn):
        ref[...] = jnp.zeros_like(ref)

    @pl.loop(0, count)
    def _(i):
        ds = block_of(i)
        where = lax.broadcasted_iota(jnp.int32, (1, BLOCK), 1) + i * BLOCK
        valid = jnp.where(where < tile_lanes(lens[0, 0:1], BLOCK), 1.0, 0.0)
        grad[:, ds] = jnp.transpose(cot[0, ds].astype(F32)) * valid

    @pl.loop(0, count)
    def _(i):
        ds = block_of(i)
        arrival(i).wait()
        context = join(core, ctx[0, :, ds], landed[:, ds])
        weights = (wo[1], wup[...], wdn[...])
        unit1, scale1, hidden, unit2, scale2, x_next = forward_block(
            context, x_ref[:, ds], *weights, cols
        )
        cells_out[0, ds] = jnp.transpose(x_next).astype(BF)
        saved = (unit1, scale1, gelu_parts(hidden), unit2, scale2)
        d_first[:, ds], d_context = backward_block(
            grad[:, ds], context, saved, weights, cols, sums, dwo, dwup, dwdn
        )
        low, high = d_context[:128], d_context[128:]
        out[:, ds] = jnp.where(core == 0, high, low)
        copy(i).start()
        dctx[0, :, ds] = jnp.where(core == 0, low, high)

    dvec[...] = place_vectors(sums)

    @pl.loop(0, count)
    def _(i):
        copy(i).wait()


GRAD_SHAPES = ((256, 256), (512, 256), (256, 512), (256, 128))


def turn(direct, lens, ctx, x, cot, wo, cols, feed_forward):
    length = ctx.shape[2]
    shapes = (
        shape_of((1, length, 256), BF),
        shape_of((256, length), F32),
        shape_of((2, 128, length), BF),
    ) + tuple(shape_of(s, F32) for s in GRAD_SHAPES)
    return pl.pallas_call(
        functools.partial(turn_kernel, direct),
        name="turn",
        out_shape=shapes,
        in_specs=[VMEM_SPEC] * (6 + len(feed_forward)),
        out_specs=[VMEM_SPEC] * len(shapes),
        scratch_shapes=[
            pltpu.VMEM((128, length), BF),
            pltpu.VMEM((2560, 128), F32),
            pltpu.VMEM((128, length), BF),
            pltpu.VMEM((256, length), F32),
        ]
        + pair_semaphores(2 * length // BLOCK)
        + ([pltpu.VMEM((512, 256), BF), pltpu.VMEM((256, 512), BF)] if direct else []),
        compiler_params=params(4, 18),
    )(lens, ctx, x, cot, wo, cols, *feed_forward)


OUTER, INNER = 48, 32


def shares(x):
    return x.reshape(32, x.shape[0] // 32, 256)


def vector_shares(vec):
    high = vec.astype(BF).astype(F32)
    return shares(jnp.concatenate([high, vec - high], axis=1))


def outer_shares(dwo, dwup, dwdn, dvec):
    return [
        shares(dwo[...]),
        shares(dwdn[:, 0:256]),
        shares(dwdn[:, 256:512]),
        vector_shares(dvec[...]),
        shares(dwup[...]),
    ]


def reduce_scratch(rows):
    return [
        pltpu.VMEM((2, 4, 4, rows, 256), BF),
        pltpu.VMEM((4, 4, rows, 256), BF),
        pltpu.VMEM((4, 4, rows, 256), BF),
        pltpu.VMEM((3, 4, rows, 256), BF),
        pltpu.VMEM((4, rows, 256), BF),
        pltpu.VMEM((3, rows, 256), BF),
        pltpu.SemaphoreType.DMA((7,)),
        pltpu.SemaphoreType.DMA((7,)),
    ]


REDUCE_REFS = 8


class Reduce:
    def __init__(self, own, from_core, by_plane, from_plane, by_line, from_line, send, recv):
        self.refs = own, from_core, by_plane, from_plane, by_line, from_line
        z, x, y, core = coordinates()
        self.z, self.number, self.core = z, 2 * x + y, core

        def copy(src, dst, i, device):
            return pltpu.make_async_remote_copy(
                src_ref=src,
                dst_ref=dst,
                send_sem=send.at[i],
                recv_sem=recv.at[i],
                device_id=device,
                device_id_type=MESH,
            )

        self.cores = [copy(own.at[1 - core], from_core, 0, sibling())]
        self.plane = [
            copy(by_plane.at[number], from_plane.at[i], 1 + i, device)
            for i, (device, number) in enumerate(plane_mates())
        ]
        self.line = [
            copy(by_line.at[there], from_line.at[i], 4 + i, device)
            for i, (device, there) in enumerate(line_mates())
        ]

    def fill(self, pieces):
        own = self.refs[0]
        rows = own.shape[3]
        terms = jnp.concatenate(pieces, axis=1).astype(BF).reshape(4, 4, 2, rows, 256)
        for core in range(2):
            for plane in range(4):
                own[core, plane] = terms[:, plane, core]

    def first(self):
        for c in self.cores:
            c.start()

    def second(self):
        own, from_core, by_plane = self.refs[:3]
        for c in self.cores:
            c.wait()
        by_plane[...] = (own[self.core].astype(F32) + from_core[...].astype(F32)).astype(BF)
        for c in self.plane:
            c.start()

    def third(self):
        by_plane, from_plane, by_line = self.refs[2:5]
        for c in self.plane:
            c.wait()
        total = by_plane[self.number].astype(F32)
        for i in range(3):
            total = total + from_plane[i].astype(F32)
        by_line[...] = total.astype(BF)
        for c in self.line:
            c.start()

    def result(self):
        by_line, from_line = self.refs[4:6]
        for c in self.line:
            c.wait()
        total = by_line[self.z].astype(F32)
        for i in range(3):
            total = total + from_line[i].astype(F32)
        return total


def reduce_half_scratch(rows):
    return [
        pltpu.VMEM((4, 4, rows, 256), BF),
        pltpu.VMEM((3, 4, rows, 256), BF),
        pltpu.VMEM((4, rows, 256), BF),
        pltpu.VMEM((4, rows, 256), BF),
        pltpu.SemaphoreType.DMA((7,)),
        pltpu.SemaphoreType.DMA((7,)),
    ]


HALF_REFS = 6


class ReduceHalf:
    def __init__(self, own, from_plane, by_line, from_line, send, recv):
        self.refs = own, from_plane, by_line, from_line
        z, x, y, core = coordinates()
        self.number = 2 * x + y

        def copy(src, dst, i, j, device):
            return pltpu.make_async_remote_copy(
                src_ref=src,
                dst_ref=dst,
                send_sem=send.at[i],
                recv_sem=recv.at[j],
                device_id=device,
                device_id_type=MESH,
            )

        self.plane = [
            copy(own.at[number], from_plane.at[i], i, i, device)
            for i, (device, number) in enumerate(plane_mates())
        ]
        self.line, self.mine = [], []
        for block in range(4):
            there, owner = 2 * core + block // 2, block % 2
            device = device_at(there, x, y, owner)
            self.line.append(copy(by_line.at[block], from_line.at[z], 3 + block, 3 + z, device))
            self.mine.append((there == z) & (owner == core))
        self.arrivals = []
        for there in range(4):
            arrival = copy(by_line.at[0], from_line.at[there], 3, 3 + there, sibling())
            self.arrivals.append((arrival, (there == z) & (z // 2 == core)))

    def fill(self, dwqkv, dvec):
        own = self.refs[0]
        rows = own.shape[2]

        def pieces(x):
            return x.reshape(16, 8, 256)

        terms = [pieces(dwqkv[128 * j : 128 * j + 128]) for j in range(3)]
        vec = dvec[...]
        high = vec.astype(BF).astype(F32)
        terms.append(pieces(jnp.concatenate([high, vec - high], axis=1)))
        terms = jnp.concatenate(terms, axis=1).astype(BF).reshape(2, 4, 2, rows, 256)
        for plane in range(4):
            own[plane] = terms[:, plane].reshape(4, rows, 256)

    def first(self):
        for c in self.plane:
            c.start()

    def second(self):
        own, from_plane, by_line, from_line = self.refs
        z = lax.axis_index("wide") // 2
        for c in self.plane:
            c.wait()
        total = own[self.number].astype(F32)
        for i in range(3):
            total = total + from_plane[i].astype(F32)
        by_line[...] = total.astype(BF)
        for block in range(4):

            @pl.when(jnp.logical_not(self.mine[block]))
            def _(block=block):
                self.line[block].start()

            @pl.when(self.mine[block])
            def _(block=block):
                from_line[z] = by_line[block]

    def result(self):
        from_line = self.refs[3]
        for arrival, mine in self.arrivals:
            pl.when(jnp.logical_not(mine))(arrival.wait_recv)
        for copy, mine in zip(self.line, self.mine):
            pl.when(jnp.logical_not(mine))(copy.wait_send)
        total = from_line[0].astype(F32)
        for i in range(1, 4):
            total = total + from_line[i].astype(F32)
        return total


def project_back(half, part, w_ref, layer):
    rows = jnp.concatenate([half_rows(w_ref, layer, 256 * j, half) for j in range(3)], axis=0)
    return dot(rows, part, 0, 0)


def middle_kernel(direct, *refs):
    dqkv, d_first_in, wqkv, ctx, unit1, hidden, unit2, scales, wo, wup, wdn, cols_ref = refs[:12]
    cols = cols_ref.at[0]
    refs = refs[12:]
    if direct:
        outer, inner, refs = refs[:4], refs[4:6], refs[6:]
    d_first, dctx, dwo, dwup, dwdn, dvec = refs[:6]
    refs = refs[6:]
    if direct:
        (sums_outer, sums_inner), refs = refs[:2], refs[2:]
    landed, sums, out, active, slope, send, recv = refs[:7]
    refs = refs[7:]
    count = d_first.shape[1] // BLOCK
    core, peer = pair_of()

    def arrival(i):
        ds, j = block_of(i), count + i
        return to_peer(dqkv.at[1, :, ds], landed.at[:, ds], send.at[j], recv.at[j], peer)

    def copy(i):
        ds = block_of(i)
        return to_peer(out.at[:, ds], dctx.at[1, :, ds], send.at[i], recv.at[i], peer)

    mates = gather_mates() + column_mates() if direct else [peer]
    hail(mates)
    if direct:
        two = ReduceHalf(*refs[:HALF_REFS])
        one = Reduce(*refs[HALF_REFS:])
        one.fill(outer_shares(*outer))
        two.fill(*inner)
    await_hails(mates)
    if direct:
        one.first()
        two.first()

    @pl.loop(0, count)
    def _(i):
        arrival(i).start()

    for ref in (sums, dwo, dwup, dwdn):
        ref[...] = jnp.zeros_like(ref)

    @pl.loop(0, count)
    def _(i):
        ds = block_of(i)
        active[:, ds], slope[:, ds] = gelu_parts(hidden[:, ds])

    if direct:
        one.second()

    @pl.loop(0, count)
    def _(i):
        if direct:

            @pl.when(i == 1)
            def _():
                two.second()
                one.third()

        ds = block_of(i)
        g = d_first_in[:, ds] + project_back(core, dqkv[0, :, ds], wqkv, 1)
        arrival(i).wait()
        g = g + project_back(1 - core, landed[:, ds], wqkv, 1)
        gelu = (active[:, ds], slope[:, ds])
        saved = (unit1[:, ds], scales[0:1, ds], gelu, unit2[:, ds], scales[1:2, ds])
        d_first[:, ds], d_context = backward_block(
            g, ctx[:, ds], saved, (wo[0], wup[...], wdn[...]), cols, sums, dwo, dwup, dwdn
        )
        low, high = d_context[:128], d_context[128:]
        out[:, ds] = jnp.where(core == 0, high, low)
        copy(i).start()
        dctx[0, :, ds] = jnp.where(core == 0, low, high)

    dvec[...] = place_vectors(sums)
    if direct:
        sums_inner[...] = two.result()
        sums_outer[...] = one.result()

    @pl.loop(0, count)
    def _(i):
        copy(i).wait()


def middle(direct, dqkv, d_first, wqkv, ctx, unit1, hidden, unit2, scales, wo, wup, wdn, cols, outer, inner):
    length = d_first.shape[1]
    terms = (*outer, *inner) if direct else ()
    shapes = (shape_of((256, length), F32), shape_of((2, 128, length), BF))
    shapes += tuple(shape_of(s, F32) for s in GRAD_SHAPES)
    if direct:
        shapes += (shape_of((OUTER, 256), F32), shape_of((INNER, 256), F32))
    return pl.pallas_call(
        functools.partial(middle_kernel, direct),
        name="back_between",
        out_shape=shapes,
        in_specs=[VMEM_SPEC] * (12 + len(terms)),
        out_specs=[VMEM_SPEC] * len(shapes),
        scratch_shapes=[
            pltpu.VMEM((384, length), BF),
            pltpu.VMEM((2560, 128), F32),
            pltpu.VMEM((128, length), BF),
            pltpu.VMEM((512, length), BF),
            pltpu.VMEM((512, length), F32),
        ]
        + pair_semaphores(2 * length // BLOCK)
        + (reduce_half_scratch(INNER) + reduce_scratch(OUTER) if direct else []),
        compiler_params=params(5, 18),
    )(dqkv, d_first, wqkv, ctx, unit1, hidden, unit2, scales, wo, wup, wdn, cols, *terms)


def last_kernel(direct, *refs):
    dqkv, d_first, wqkv = refs[:3]
    refs = refs[3:]
    if direct:
        outer, inner, (grad_out, sums_outer, sums_inner) = refs[:4], refs[4:6], refs[6:9]
        refs = refs[9:]
    else:
        grad_out, refs = refs[0], refs[1:]
    landed, grad, send, recv = refs[:4]
    refs = refs[4:]
    count = d_first.shape[1] // BLOCK
    core, peer = pair_of()

    def arrival(i):
        ds = block_of(i)
        return to_peer(dqkv.at[1, :, ds], landed.at[:, ds], send.at[i], recv.at[i], peer)

    mates = gather_mates() + column_mates() if direct else [peer]
    hail(mates)
    if direct:
        two = ReduceHalf(*refs[:HALF_REFS])
        one = Reduce(*refs[HALF_REFS:])
        one.fill(outer_shares(*outer))
        two.fill(*inner)
    await_hails(mates)
    if direct:
        one.first()
        two.first()

    @pl.loop(0, count)
    def _(i):
        arrival(i).start()

    @pl.loop(0, count)
    def _(i):
        ds = block_of(i)
        grad[:, ds] = d_first[:, ds] + project_back(core, dqkv[0, :, ds], wqkv, 0)

    if direct:
        one.second()

    @pl.loop(0, count)
    def _(i):
        if direct:
            pl.when(i == 1)(two.second)
        ds = block_of(i)
        arrival(i).wait()
        g = grad[:, ds] + project_back(1 - core, landed[:, ds], wqkv, 0)
        grad_out[0, ds] = jnp.transpose(g)

    if direct:
        one.third()
        sums_inner[...] = two.result()
        sums_outer[...] = one.result()


def last(direct, dqkv, d_first, wqkv, outer, inner):
    length = d_first.shape[1]
    terms = (*outer, *inner) if direct else ()
    shapes = (shape_of((1, length, 256), F32),)
    if direct:
        shapes += (shape_of((OUTER, 256), F32), shape_of((INNER, 256), F32))
    return pl.pallas_call(
        functools.partial(last_kernel, direct),
        name="back_input",
        out_shape=shapes,
        in_specs=[VMEM_SPEC] * (3 + len(terms)),
        out_specs=[VMEM_SPEC] * len(shapes),
        scratch_shapes=[
            pltpu.VMEM((384, length), BF),
            pltpu.VMEM((256, length), F32),
        ]
        + pair_semaphores(length // BLOCK)
        + (reduce_half_scratch(INNER) + reduce_scratch(OUTER) if direct else []),
        compiler_params=params(6),
    )(dqkv, d_first, wqkv, *terms)


def finish_kernel(factor, outer1, inner1, outer0, inner0, grad, *refs):
    qw, qb, kw, vw, vb, ow, ob, g1, s1, uw, ub, dw, db, g2, s2, placed, place_sem = refs
    place = pltpu.make_async_copy(grad, placed, place_sem)
    place.start()
    layers = (
        (inner0[...] * factor, outer0[...] * factor),
        (inner1[...] * factor, outer1[...] * factor),
    )
    for layer, (inner, outer) in enumerate(layers):
        qw[layer], kw[layer], vw[layer] = inner[0:8], inner[8:16], inner[16:24]
        ow[layer] = outer[0:8]
        dw[layer, :, 0:256], dw[layer, :, 256:512] = outer[8:16], outer[16:24]
        uw[layer] = outer[32:48]
        vec = inner[24:32] + outer[24:32]
        vec = jnp.transpose(vec[:, 0:128] + vec[:, 128:256])
        for i, ref in enumerate((qb, vb, ob, g1, s1, db, g2, s2)):
            ref[layer : layer + 1] = vec[i : i + 1]
        ub[layer : layer + 1, 0:8] = vec[8:9]
        ub[layer : layer + 1, 8:16] = vec[9:10]
    place.wait()


def finish(factor, sums, grad, like):
    found = pl.pallas_call(
        functools.partial(finish_kernel, factor),
        name="finish",
        out_shape=tuple(shape_of(a.shape, F32) for a in (*like, grad)),
        in_specs=[VMEM_SPEC] * 5,
        out_specs=[VMEM_SPEC] * len(like) + [HBM_SPEC],
        scratch_shapes=[pltpu.SemaphoreType.DMA],
        compiler_params=params(),
    )(*sums, grad)
    *found, grad = found
    return grad, [jnp.swapaxes(a, 1, 2) if a.ndim == 3 else a for a in found]


def gather_by_collectives(weights, vectors):
    def whole_of(w):
        return lax.all_gather(w, AXES, axis=1, tiled=True)

    qw, kw, vw, ow, uw, dw = (whole_of(w) for w in weights)
    columns = [lax.all_gather(v, AXES, axis=1, tiled=True).astype(F32) for v in vectors]
    up = columns.pop().reshape(2, 32, 2, 8)
    columns += [up[:, :, 0].reshape(2, 256), up[:, :, 1].reshape(2, 256)]
    lanes = jnp.stack(columns).transpose(2, 0, 1).reshape(256, 20)
    vec = jnp.pad(lanes, ((0, 0), (0, 108)))
    return jnp.concatenate([qw, kw, vw], axis=1), ow, uw, dw, vec


def sum_by_collectives(factor, layers):
    def share(x):
        return lax.psum_scatter(x, AXES, scatter_dimension=0, tiled=True) * factor

    found = []
    core = lax.rem(lax.axis_index("narrow"), 2)

    def widen(x):
        parts = x.reshape(-1, 1, 128, x.shape[1])
        mine = (jnp.arange(2) == core)[None, :, None, None]
        return jnp.where(mine, parts, 0.0).reshape(-1, x.shape[1])

    for dwqkv, dvec_qkv, dwo, dwup, dwdn, dvec in layers:
        dwqkv = widen(dwqkv)
        vec = widen(dvec_qkv) + dvec
        qb, vb, ob, g1, s1, db, g2, s2 = (share(vec[:, i]) for i in range(8))
        up = jnp.stack([vec[:, 8].reshape(32, 8), vec[:, 9].reshape(32, 8)], axis=1)
        qw, kw, vw = (share(dwqkv[256 * i : 256 * i + 256]).T for i in range(3))
        ow, uw, dw = share(dwo).T, share(dwup).T, share(dwdn).T
        ub = share(up.reshape(512))
        found.append((qw, qb, kw, vw, vb, ow, ob, g1, s1, uw, ub, dw, db, g2, s2))
    return [jnp.stack(pair) for pair in zip(*found)]


def on_device(devices, direct, cells_in, lengths, cotangent, *weights):
    qw, qb, kw, vw, vb, ow, ob, g1, s1, uw, ub, dw, db, g2, s2 = weights
    matrices, vectors = (qw, kw, vw, ow, uw, dw), (qb, vb, ob, g1, s1, db, g2, s2, ub)
    turned = [jnp.swapaxes(w, 1, 2) for w in matrices]
    if direct:
        share = own_share(lengths, turned, vectors)
        lens, qkv0, wqkv, wo, wup0, wdn0, cols, xs0, landed = start(share, cells_in)
        feed_forward = (landed,)
    else:
        wqkv, wo, wup, wdn, vec = gather_by_collectives(turned, vectors)
        wup0, wdn0, feed_forward = wup[0], wdn[0], (wup[1], wdn[1])
        cols = columns(vec)
        lens, qkv0, xs0 = project_first(lengths, cells_in, wqkv, cols)
    ctx_pair, ctx32_0, logs0 = attend(lens, qkv0)
    x1, ctx0, unit1, hidden, unit2, scales, qkv1, xs1 = between(
        ctx_pair, cells_in, wqkv, wo, wup0, wdn0, cols
    )
    ctx_pair, ctx32_1, logs1 = attend(lens, qkv1)
    cells_out, d_first, dctx, *outer1 = turn(
        direct, lens, ctx_pair, x1, cotangent, wo, cols, feed_forward
    )
    dqkv, *inner1, cells_out = attend_back(lens, qkv1, dctx, ctx32_1, logs1, xs1, cells_out)
    d_first, dctx, *found = middle(
        direct, dqkv, d_first, wqkv, ctx0, unit1, hidden, unit2, scales, wo, wup0, wdn0, cols, outer1, inner1
    )
    outer0, sums1 = found[:4], found[4:]
    dqkv, *inner0 = attend_back(lens, qkv0, dctx, ctx32_0, logs0, xs0)
    grad_in, *sums0 = last(direct, dqkv, d_first, wqkv, outer0, inner0)
    factor = 1.0 / math.sqrt(devices * cells_in.shape[0] * cells_in.shape[1])
    if direct:
        like = [shape_of(a.shape[:1] + a.shape[:0:-1], F32) for a in weights]
        grad_in, grads = finish(factor, (*sums1, *sums0), grad_in, like)
    else:
        grads = sum_by_collectives(factor, ((*inner0, *outer0), (*inner1, *outer1)))
    return (cells_out, grad_in, *grads)


def solution(mesh):
    devices = mesh.size
    direct = (mesh.shape["wide"], mesh.shape["narrow"]) == (8, 4)
    cell, vector, matrix = P(AXES, None, None), P(None, AXES), P(None, None, AXES)
    placed = (
        matrix, vector, matrix, matrix, vector, matrix, vector, vector, vector,
        matrix, vector, matrix, vector, vector, vector,
    )
    return jax.shard_map(
        functools.partial(on_device, devices, direct),
        mesh=mesh,
        in_specs=(cell, P(AXES), cell) + placed,
        out_specs=(cell, cell) + placed,
        check_vma=False,
    )
```
